256 devices in a mesh: section: 8 (over x, y_hi), member: 32 (over z, y_lo, core).
Axes of the slice: x: 4, y: 4 (y_hi: 2, y_lo: 2; y = y_hi * 2 + y_lo), z: 8, core: 2. Of those that a mesh axis runs over, the one named last changes fastest.
Arguments:
- populations: float32 [512, 19, 4096], P(('section', 'member'))
- fluid_mask: int32 [512, 4096], P(('section', 'member')), may hold values 0 or 1
- section_level: int32 [8], replicated, may hold values from 0 to 2, as said below
- neighbours: int32 [512, 18], P(('section', 'member')), may hold values from -1 to 511, as said below
- interface: int32 [512, 6, 4], P(('section', 'member')), may hold values from -1 to 511, as said below
Outputs:
- final_populations: float32 [512, 19, 4096], P(('section', 'member'))
The draws below stay inside these ranges and needn't reach their ends.
Inputs may be any that keep to these rules, and one draw needn't show every extreme that they name: `section_level`: levels never fall along the section axis and each of 0, 1, 2 is held by some section. `neighbours`: A neighbour lies in the same section as the block, on the same member index or one beside it. `interface`: entries stand only on faces whose neighbour is -1; the named blocks lie in a section whose level differs from the block's by one, on the same member index or one beside it. Where that level is below the block's, exactly one quadrant of the face is named, else all four.
All inputs are finite; a program needn't handle non-finite values. No bound on the sum of `fluid_mask` on one device may be relied on, other than what follows from the above.
Results may differ from the reference program's by a relative error of at most 0.0003.
Values sent between devices are 32-bit elements; how exact they have to be, the bound alone decides.
A program may use at most 64 MiB of HBM per device.

```python
import jax
import jax.numpy as jnp
from jax import lax

EDGE = 16
CELLS = 4096
BLK_DEV = 2
BLOCKS = 512
PACK = 7936
N_SECTION = 8
N_MEMBER = 32


VELOCITY_TABLE = ((0, 0, 0), (1, 0, 0), (-1, 0, 0), (0, 1, 0), (0, -1, 0), (0, 0, 1), (0, 0, -1), (1, 1, 0), (-1, -1, 0), (1, -1, 0), (-1, 1, 0), (1, 0, 1), (-1, 0, -1), (1, 0, -1), (-1, 0, 1), (0, 1, 1), (0, -1, -1), (0, 1, -1), (0, -1, 1))


WEIGHT_TABLE = (1.0 / 3.0,) + (1.0 / 18.0,) * 6 + (1.0 / 36.0,) * 12


def geometry(key):
    sections = jnp.arange(N_SECTION)
    cut_one = jax.random.randint(jax.random.fold_in(key, 11), (), 1, N_SECTION - 1)
    cut_two = jax.random.randint(jax.random.fold_in(key, 12), (), cut_one + 1, N_SECTION)
    levels = (sections >= cut_one).astype(jnp.int32) + (sections >= cut_two).astype(jnp.int32)
    blocks = jnp.arange(BLOCKS)
    block_section = blocks // (N_MEMBER * BLK_DEV)
    block_member = blocks // BLK_DEV % N_MEMBER
    step = jax.random.randint(jax.random.fold_in(key, 13), (BLOCKS, 18), -1, 2)
    member_next = jnp.clip(block_member[:, None] + step, 0, N_MEMBER - 1)
    within = jax.random.randint(jax.random.fold_in(key, 14), (BLOCKS, 18), 0, BLK_DEV)
    present = jax.random.randint(jax.random.fold_in(key, 15), (BLOCKS, 18), 0, 8) < 6
    block_ids = jnp.where(present, (block_section[:, None] * N_MEMBER + member_next) * BLK_DEV + within, -1)
    special = cut_two * N_MEMBER * BLK_DEV - 1
    block_ids = block_ids.at[0, 0].set(-1).at[BLOCKS - 1, 0].set(BLOCKS - 1).at[special, 0].set(-1).astype(jnp.int32)
    own_level = levels[block_section]
    scores = jax.random.randint(jax.random.fold_in(key, 16), (BLOCKS, 6, N_SECTION), 0, 1000) * N_SECTION + sections
    valid = jnp.abs(levels[None, None, :] - own_level[:, None, None]) == 1
    chosen = jnp.argmax(jnp.where(valid, scores, -1), axis=2)
    coarser = levels[chosen] < own_level[:, None]
    quadrant = jax.random.randint(jax.random.fold_in(key, 17), (BLOCKS, 6), 0, 4)
    step_four = jax.random.randint(jax.random.fold_in(key, 18), (BLOCKS, 6, 4), -1, 2)
    member_four = jnp.clip(block_member[:, None, None] + step_four, 0, N_MEMBER - 1)
    within_four = jax.random.randint(jax.random.fold_in(key, 19), (BLOCKS, 6, 4), 0, BLK_DEV)
    source = (chosen[:, :, None] * N_MEMBER + member_four) * BLK_DEV + within_four
    used = (block_ids[:, :6] == -1) & (jax.random.randint(jax.random.fold_in(key, 20), (BLOCKS, 6), 0, 4) < 3)
    keep = jnp.where(coarser[:, :, None], jnp.arange(4)[None, None, :] == quadrant[:, :, None], True)
    links = jnp.where(used[:, :, None] & keep, source, -1)
    links = links.at[special, 0].set(jnp.full((4,), BLOCKS - 1, links.dtype)).astype(jnp.int32)
    return (levels, block_ids, links)


def draw_section_level(key, part):
    return geometry(key)[0]


def draw_neighbours(key, part):
    return geometry(key)[1]


def draw_interface(key, part):
    return geometry(key)[2]


def draw_populations(key, part):
    lattice = jnp.array(VELOCITY_TABLE, jnp.float32)
    weight_vector = jnp.array(WEIGHT_TABLE, jnp.float32)
    flow = jax.random.uniform(jax.random.fold_in(key, 1), (BLOCKS, 3, CELLS), jnp.float32, -0.05, 0.05)
    along = lattice[None, :, 0, None] * flow[:, None, 0, :] + lattice[None, :, 1, None] * flow[:, None, 1, :] + lattice[None, :, 2, None] * flow[:, None, 2, :]
    noise = 0.25 * jnp.clip(jax.random.normal(jax.random.fold_in(key, 2), (BLOCKS, 19, CELLS), jnp.float32), -2.5, 2.5)
    values = weight_vector[None, :, None] * (1.0 + 3.0 * along + noise)
    return values.astype(jnp.float32)


def place_ends(drawn, own_key, low, top_value):
    place = [jax.random.randint(jax.random.fold_in(own_key, axis), (), 0, length) for axis, length in enumerate(drawn.shape)]
    main_axis = drawn.shape.index(max(drawn.shape))
    beside = place[:main_axis] + [(place[main_axis] + 1) % drawn.shape[main_axis]] + place[main_axis + 1:]
    return drawn.at[tuple(place)].set(low).at[tuple(beside)].set(top_value)


def setup_inputs(seed: int = 0) -> dict:
    key_list = jax.random.split(jax.random.key(seed), 6)
    populations = draw_populations(jax.random.fold_in(key_list[5], 71), 0)
    fluid_mask = place_ends((jax.random.randint(key_list[1], (BLOCKS, CELLS), 0, 8) < 7).astype(jnp.int32), jax.random.fold_in(key_list[1], 1), 0, 1)
    section_level = draw_section_level(jax.random.fold_in(key_list[5], 71), 0)
    neighbours = draw_neighbours(jax.random.fold_in(key_list[5], 71), 0)
    interface = draw_interface(jax.random.fold_in(key_list[5], 71), 0)
    return dict(populations=populations, fluid_mask=fluid_mask, section_level=section_level, neighbours=neighbours, interface=interface)


VELOCITIES = ((0, 0, 0), (1, 0, 0), (-1, 0, 0), (0, 1, 0), (0, -1, 0), (0, 0, 1), (0, 0, -1),
              (1, 1, 0), (-1, -1, 0), (1, -1, 0), (-1, 1, 0), (1, 0, 1), (-1, 0, -1), (1, 0, -1),
              (-1, 0, 1), (0, 1, 1), (0, -1, -1), (0, 1, -1), (0, -1, 1))
WEIGHTS = (1.0 / 3.0,) + (1.0 / 18.0,) * 6 + (1.0 / 36.0,) * 12
OPPOSITE = (0, 2, 1, 4, 3, 6, 5, 8, 7, 10, 9, 12, 11, 14, 13, 16, 15, 18, 17)
HIGH = lax.Precision.HIGHEST


def export_lists():
    result = []
    for j in range(6):
        side = VELOCITIES[1 + j]
        result.append([q for q in range(19) if sum(a * b for a, b in zip(VELOCITIES[q], side)) == 1])
    return result


def relax_rate(level):
    return jnp.where(level == 0, 1.0 / 0.55, jnp.where(level == 1, 1.0 / 0.6, 1.0 / 0.7)).astype(jnp.float32)


def collide(current, fluid, rate):
    lattice = jnp.array(VELOCITIES, jnp.float32)
    weight_vector = jnp.array(WEIGHTS, jnp.float32)
    density = jnp.sum(current, axis=1)
    momentum = jnp.einsum('nqc,qd->ndc', current, lattice, precision=HIGH)
    velocity = momentum / density[:, None, :]
    along = jnp.einsum('qd,ndc->nqc', lattice, velocity, precision=HIGH)
    speed_square = jnp.sum(velocity * velocity, axis=1)
    equilibrium = weight_vector[None, :, None] * density[:, None, :] * (
        1.0 + 3.0 * along + 4.5 * along * along - 1.5 * speed_square[:, None, :])
    relaxed = current - rate * (current - equilibrium)
    bounced = jnp.stack([current[:, o] for o in OPPOSITE], axis=1)
    return jnp.where(fluid[:, None, :] == 1, relaxed, bounced)


def export(current):
    count = current.shape[0]
    blocks_view = current.reshape(count, 19, EDGE, EDGE, EDGE)
    lists = export_lists()
    pieces = []
    for j in range(6):
        layer_index = EDGE - 1 if j % 2 == 0 else 0
        chosen = jnp.stack([blocks_view[:, q] for q in lists[j]], axis=1)
        plane_data = jnp.take(chosen, layer_index, axis=2 + j // 2)
        pieces.append(plane_data.reshape(count, 5 * EDGE * EDGE))
    for j in range(12):
        direction = VELOCITIES[7 + j]
        index_list = [slice(None)]
        for a in range(3):
            if direction[a] > 0:
                index_list.append(EDGE - 1)
            elif direction[a] < 0:
                index_list.append(0)
            else:
                index_list.append(slice(None))
        pieces.append(blocks_view[:, 7 + j][tuple(index_list)])
    flat = jnp.concatenate(pieces, axis=1)
    return jnp.pad(flat, ((0, 0), (0, PACK - flat.shape[1])))


def quadrant_tables():
    half = EDGE // 2
    places = jnp.arange(EDGE)
    tables = []
    for k in range(4):
        first = (places[None, :] == half * (k // 2) + places[:, None] // 2).astype(jnp.float32)
        second = (places[None, :] == half * (k % 2) + places[:, None] // 2).astype(jnp.float32)
        tables.append(jnp.einsum('ai,bj->ijab', first, second, precision=HIGH).reshape(EDGE * EDGE, EDGE * EDGE))
    prolong = jnp.stack(tables, axis=0)
    restrict = 0.25 * jnp.transpose(prolong, (0, 2, 1))
    return prolong, restrict


def boundary_data(neighbour_rows, neighbour_ok, link_rows, link_ok, coarse_source):
    count = neighbour_rows.shape[0]
    area = EDGE * EDGE
    face_size = 5 * area
    lists = export_lists()
    face_list = []
    link_list = []
    edge_list = []
    for j in range(6):
        start = (j ^ 1) * face_size
        face_list.append(neighbour_rows[:, j, start:start + face_size].reshape(count, 5, area))
        link_list.append(link_rows[:, j, :, start:start + face_size].reshape(count, 4, 5, area))
    for j in range(12):
        start = 30 * area + (j ^ 1) * EDGE
        edge_list.append(neighbour_rows[:, 6 + j, start:start + EDGE])
    face_planes = jnp.stack(face_list, axis=1)
    link_planes = jnp.stack(link_list, axis=1)
    edge_planes = jnp.stack(edge_list, axis=1)
    prolong, restrict = quadrant_tables()
    upward = jnp.einsum('njkpi,kio->njkpo', link_planes, prolong, precision=HIGH)
    downward = jnp.einsum('njkpi,kio->njkpo', link_planes, restrict, precision=HIGH)
    mapped = jnp.where(link_ok[:, :, :, None, None],
                       jnp.where(coarse_source[:, :, :, None, None], upward, downward), 0.0)
    link_sum = jnp.sum(mapped, axis=2)
    has_link = jnp.any(link_ok, axis=2)
    rest_faces = jnp.array([[WEIGHTS[q] for q in lists[j ^ 1]] for j in range(6)], jnp.float32)
    faces_out = jnp.where(neighbour_ok[:, :6, None, None], face_planes,
                          jnp.where(has_link[:, :, None, None], link_sum, rest_faces[None, :, :, None]))
    edges_out = jnp.where(neighbour_ok[:, 6:, None], edge_planes, jnp.float32(1.0 / 36.0))
    return faces_out, edges_out


def stream(current, face_planes, edge_lines):
    count = current.shape[0]
    blocks_view = current.reshape(count, 19, EDGE, EDGE, EDGE)
    lists = export_lists()
    outputs = []
    for q in range(19):
        direction = VELOCITIES[q]
        padded = jnp.pad(blocks_view[:, q], ((0, 0), (1, 1), (1, 1), (1, 1)))
        moving = [a for a in range(3) if direction[a] != 0]
        for a in moving:
            toward = -direction[a]
            slot = 2 * a + (0 if toward > 0 else 1)
            position = lists[slot ^ 1].index(q)
            index_list = [slice(None)] + [slice(1, EDGE + 1)] * 3
            index_list[1 + a] = EDGE + 1 if toward > 0 else 0
            padded = padded.at[tuple(index_list)].set(face_planes[:, slot, position].reshape(count, EDGE, EDGE))
        if len(moving) == 2:
            slot = VELOCITIES.index(tuple(-v for v in direction)) - 7
            index_list = [slice(None)] + [slice(1, EDGE + 1)] * 3
            for a in moving:
                index_list[1 + a] = EDGE + 1 if direction[a] < 0 else 0
            padded = padded.at[tuple(index_list)].set(edge_lines[:, slot])
        shifted = padded[:, 1 - direction[0]:1 - direction[0] + EDGE,
                         1 - direction[1]:1 - direction[1] + EDGE,
                         1 - direction[2]:1 - direction[2] + EDGE]
        outputs.append(shifted.reshape(count, CELLS))
    return jnp.stack(outputs, axis=1)


def reference(populations, fluid_mask, section_level, neighbours, interface):
    groups = BLOCKS // BLK_DEV
    group_level = section_level[jnp.arange(groups) // N_MEMBER]
    fluid_groups = fluid_mask.reshape(groups, BLK_DEV, CELLS)
    neighbour_groups = neighbours.reshape(groups, BLK_DEV, 18)
    link_groups = interface.reshape(groups, BLK_DEV, 6, 4)
    current = populations.reshape(groups, BLK_DEV, 19, CELLS)
    for k in range(2):
        if k == 0:
            advances = group_level >= 1
        else:
            advances = group_level == 2

        def post_collision(inputs):
            block_pops, block_fluid, level_here, moves = inputs
            starred = collide(block_pops, block_fluid, relax_rate(level_here))
            return jnp.where(moves, starred, block_pops)

        starred = lax.map(post_collision, (current, fluid_groups, group_level, advances))
        exports = lax.map(export, starred).reshape(BLOCKS, PACK)

        def advance_group(inputs):
            block_star, block_old, block_ids, link_ids, level_here, moves = inputs
            neighbour_rows = exports[jnp.maximum(block_ids, 0)]
            link_rows = exports[jnp.maximum(link_ids, 0)]
            source_level = section_level[jnp.maximum(link_ids, 0) // (N_MEMBER * BLK_DEV)]
            face_planes, edge_lines = boundary_data(neighbour_rows, block_ids >= 0, link_rows, link_ids >= 0,
                                                    source_level < level_here)
            moved = stream(block_star, face_planes, edge_lines)
            return jnp.where(moves, moved, block_old)

        current = lax.map(advance_group, (starred, current, neighbour_groups, link_groups, group_level, advances))
    return current.reshape(BLOCKS, 19, CELLS)
```

```python
import jax
import jax.numpy as jnp
from jax import lax
from jax.experimental import pallas as pl
from jax.experimental.pallas import tpu as pltpu
from jax.sharding import PartitionSpec as P

MESH = pl.DeviceIdType.MESH
F32 = jnp.float32
NSEC = 8
NMEM = 32

VELOCITIES = (
    (0, 0, 0),
    (1, 0, 0),
    (-1, 0, 0),
    (0, 1, 0),
    (0, -1, 0),
    (0, 0, 1),
    (0, 0, -1),
    (1, 1, 0),
    (-1, -1, 0),
    (1, -1, 0),
    (-1, 1, 0),
    (1, 0, 1),
    (-1, 0, -1),
    (1, 0, -1),
    (-1, 0, 1),
    (0, 1, 1),
    (0, -1, -1),
    (0, 1, -1),
    (0, -1, 1),
)
OPPOSITE = (0, 2, 1, 4, 3, 6, 5, 8, 7, 10, 9, 12, 11, 14, 13, 16, 15, 18, 17)
SIDE_LISTS = tuple(
    tuple(tuple(q for q in range(19) if VELOCITIES[q][axis] == sign) for sign in (1, -1))
    for axis in range(3)
)


def side_of(q, axis):
    side = 0 if VELOCITIES[q][axis] > 0 else 1
    return side, SIDE_LISTS[axis][side].index(q)


def iotas(shape=(8, 128)):
    return lax.broadcasted_iota(jnp.int32, shape, 0), lax.broadcasted_iota(jnp.int32, shape, 1)


def lanes_from(x, index):
    return jnp.take_along_axis(x, index, axis=1)


def rows_from(x, index):
    return jnp.take_along_axis(x, index, axis=0)


def pick(cond, a, b):
    return lax.select(cond, a, b)


def tile_slices(axis, tile):
    first, second = 8 * (tile // 2), 128 * (tile % 2)
    return slice(first, first + 8), slice(second, second + 128)


def collide(cur, mask_ref, star, b, rate, advances):
    for tile in range(4):
        rows, lanes = tile_slices(0, tile)
        f = [cur[b, q, rows, lanes] for q in range(19)]
        density = f[0]
        for q in range(1, 19):
            density = density + f[q]
        velocity = []
        for axis in range(3):
            plus, minus = SIDE_LISTS[axis]
            momentum = f[plus[0]] - f[minus[0]]
            for i in range(1, 5):
                momentum = momentum + f[plus[i]]
            for i in range(1, 5):
                momentum = momentum - f[minus[i]]
            velocity.append(momentum / density)
        base = 1.0 - 1.5 * (
            velocity[0] * velocity[0] + velocity[1] * velocity[1] + velocity[2] * velocity[2]
        )
        fluid = mask_ref[b, rows, lanes] == 1
        keep = 1.0 - rate
        scaled = rate * density

        def put(q, relaxed):
            star[b, q, rows, lanes] = pick(
                advances, jnp.where(fluid, relaxed, f[OPPOSITE[q]]), f[q]
            )

        put(0, keep * f[0] + scaled * (1.0 / 3.0) * base)
        axis_weight = scaled * (1.0 / 18.0)
        edge_weight = scaled * (1.0 / 36.0)
        for q in range(1, 19, 2):
            c = VELOCITIES[q]
            along = None
            for axis in range(3):
                if c[axis]:
                    term = velocity[axis] if c[axis] > 0 else -velocity[axis]
                    along = term if along is None else along + term
            weight = axis_weight if q < 7 else edge_weight
            even = weight * (base + 4.5 * along * along)
            odd = weight * (3.0 * along)
            put(q, keep * f[q] + (even + odd))
            put(q + 1, keep * f[q + 1] + (even - odd))


def export(star, faces, b):
    row, lane = iotas()
    group, within = lane // 16, lane % 16
    for side in range(2):
        for p, q in enumerate(SIDE_LISTS[0][side]):
            layer = 15 if side == 0 else 0
            for half in range(2):
                faces[2 + b, 0, side * 2 + half, p : p + 1, :] = star[
                    b, q, layer : layer + 1, 128 * half : 128 * half + 128
                ]
    zero = jnp.zeros((8, 128), F32)
    for a in range(2):
        for side in range(2):
            total = zero
            for p, q in enumerate(SIDE_LISTS[1][side]):
                half = 1 - side
                x = star[b, q, 8 * a : 8 * a + 8, 128 * half : 128 * half + 128]
                shift = (16 * p + 16 if side == 0 else 16 * p) % 128
                x = pltpu.roll(x, shift, 1) if shift else x
                total = jnp.where(group == p, x, total)
            faces[2 + b, 1, a * 2 + side] = total
        for half in range(2):
            total = zero
            for side in range(2):
                for p, q in enumerate(SIDE_LISTS[2][side]):
                    x = star[b, q, 8 * a : 8 * a + 8, 128 * half : 128 * half + 128]
                    shift = 113 + p if side == 0 else 8 + p
                    x = pltpu.roll(x, shift, 1)
                    total = jnp.where(within == side * 8 + p, x, total)
            faces[2 + b, 2, a * 2 + half] = total


def restrict(faces, down, b):
    row, lane = iotas()
    group, within, low = lane // 16, lane % 16, lane % 8
    second = (lane // 8) % 2
    fine = group * 16 + 2 * low
    coarse = (2 * (group % 4)) * 16
    pair_rows = 2 * (row % 4)
    parts = []
    for side in range(2):
        halves = []
        for half in range(2):
            t = faces[2 + b, 0, side * 2 + half]
            t = t + pltpu.roll(t, 127, 1)
            t = t + pltpu.roll(t, 112, 1)
            halves.append(lanes_from(t, coarse + 2 * low))
        parts.append(jnp.where(group < 4, halves[0], halves[1]))
    down[3 * b] = 0.25 * jnp.where(second == 0, parts[0], parts[1])
    parts = []
    for side in range(2):
        rows = []
        for a in range(2):
            t = faces[2 + b, 1, a * 2 + side]
            t = t + pltpu.roll(t, 127, 1)
            t = t + pltpu.roll(t, 7, 0)
            rows.append(rows_from(lanes_from(t, fine), pair_rows))
        parts.append(jnp.where(row < 4, rows[0], rows[1]))
    down[3 * b + 1] = 0.25 * jnp.where(second == 0, parts[0], parts[1])
    rows = []
    for a in range(2):
        halves = []
        for half in range(2):
            t = faces[2 + b, 2, a * 2 + half]
            t = t + pltpu.roll(t, 112, 1)
            halves.append(lanes_from(t, coarse + within))
        t = jnp.where(group < 4, halves[0], halves[1])
        t = t + pltpu.roll(t, 7, 0)
        rows.append(rows_from(t, pair_rows))
    down[3 * b + 2] = 0.25 * jnp.where(row < 4, rows[0], rows[1])


def slot_of(block, member):
    safe = jnp.maximum(block, 0)
    offset = lax.rem(lax.div(safe, 2), NMEM) - member + 1
    return jnp.clip(offset * 2 + lax.rem(safe, 2), 0, 5)


def select_quadrants(faces, wanted, out, other, member):
    row, lane = iotas()
    second = (lane // 8) % 2
    for b in range(2):
        for axis in range(3):
            parts = []
            for side in range(2):
                code = jnp.maximum(wanted[other, b * 6 + 2 * axis + 1 - side], 0)
                quadrant = lax.rem(code, 4)
                first, last = lax.div(quadrant, 2), lax.rem(quadrant, 2)
                slot = slot_of(lax.div(code, 4), member)
                if axis == 0:
                    tile = side * 2 + first
                elif axis == 1:
                    tile = first * 2 + side
                else:
                    tile = quadrant
                t = faces[slot, axis, tile]
                if axis < 2:
                    t = pick(last == side, t, pltpu.roll(t, 8 if side else 120, 1))
                parts.append(t)
            out[other, b * 3 + axis] = jnp.where(second == 0, parts[0], parts[1])


def build_halo(faces, up, down, halo, b, nbr, link, wanted, level, own, member):
    row, lane = iotas()
    group, within, low = lane // 16, lane % 16, lane % 8
    second = (lane // 8) % 2
    spread_rows = [4 * a + row // 2 for a in range(2)]

    def link_state(j):
        code = wanted[b * 6 + j]
        section = lax.div(lax.div(jnp.maximum(code, 0), 4), 2 * NMEM)
        any_link = code >= 0
        coarse = level[section] < own
        return section, any_link, coarse

    def means(axis, j, k):
        block = link[(b * 6 + j) * 4 + k]
        safe = jnp.maximum(block, 0)
        section = lax.div(safe, 2 * NMEM)
        offset = jnp.clip(lax.rem(lax.div(safe, 2), NMEM) - member + 1, 0, 2)
        t = down[section, offset, lax.rem(safe, 2) * 3 + axis]
        return pick(block >= 0, t, jnp.zeros_like(t))

    for axis in range(3):
        states, near, quads, ups = [], [], [], []
        for side in range(2):
            j = 2 * axis + 1 - side
            section, any_link, coarse = link_state(j)
            states.append((nbr[b * 18 + j] >= 0, any_link, coarse))
            near.append(slot_of(nbr[b * 18 + j], member))
            ups.append(up[section, b * 3 + axis])
            if down is not None:
                quads.append([means(axis, j, k) for k in range(4)])
        if axis == 0:
            rest = jnp.where(row == 0, F32(1.0 / 18.0), F32(1.0 / 36.0))
        elif axis == 1:
            rest = jnp.where(group == 0, F32(1.0 / 18.0), F32(1.0 / 36.0))
        else:
            rest = jnp.where(low == 0, F32(1.0 / 18.0), F32(1.0 / 36.0))

        def choose(side, tile, from_up, from_down):
            is_near, any_link, coarse = states[side]
            linked = from_up if from_down is None else pick(coarse, from_up, from_down)
            far = pick(any_link, linked, rest)
            return pick(is_near, faces[near[side], axis, tile], far)

        if axis < 2:
            for side in range(2):
                if axis == 1:
                    wide = lanes_from(ups[side], group * 16 + side * 8 + within // 2)
                for a in range(2):
                    if axis == 0:
                        tile = side * 2 + a
                        from_up = lanes_from(
                            ups[side], (4 * a + group // 2) * 16 + side * 8 + within // 2
                        )
                    else:
                        tile = a * 2 + side
                        from_up = rows_from(wide, spread_rows[a])
                    from_down = None
                    if down is not None:
                        low_part, high_part = quads[side][2 * a], quads[side][2 * a + 1]
                        if side:
                            low_part = pltpu.roll(low_part, 120, 1)
                        else:
                            high_part = pltpu.roll(high_part, 8, 1)
                        from_down = jnp.where(second == 0, low_part, high_part)
                    rows, lanes = tile_slices(axis, tile)
                    halo[axis, rows, lanes] = choose(side, tile, from_up, from_down)
        else:
            both = jnp.where(second == 0, ups[0], ups[1])
            for half in range(2):
                wide = lanes_from(both, (4 * half + group // 2) * 16 + within)
                for a in range(2):
                    tile = a * 2 + half
                    from_up = rows_from(wide, spread_rows[a])
                    parts = [
                        choose(side, tile, from_up, quads[side][tile] if down is not None else None)
                        for side in range(2)
                    ]
                    rows, lanes = tile_slices(axis, tile)
                    halo[axis, rows, lanes] = jnp.where(second == 0, parts[0], parts[1])

    for q in range(7, 19):
        c = VELOCITIES[q]
        one, two = [axis for axis in range(3) if c[axis]]
        side, p = side_of(q, two)
        block = nbr[b * 18 + OPPOSITE[q] - 1]
        slot = slot_of(block, member)
        far_end = c[one] > 0
        if two == 1:
            tiles = [(1 if far_end else 0) * 2 + side]
            where = (row == (7 if far_end else 0)) & (group == p)
        elif one == 0:
            tiles = [(1 if far_end else 0) * 2 + half for half in range(2)]
            where = (row == (7 if far_end else 0)) & (within == side * 8 + p)
        else:
            tiles = [a * 2 + (1 if far_end else 0) for a in range(2)]
            where = lane == (7 if far_end else 0) * 16 + side * 8 + p
        for tile in tiles:
            rows, lanes = tile_slices(two, tile)
            line = faces[slot, two, tile]
            line = pick(block >= 0, line, jnp.full_like(line, 1.0 / 36.0))
            halo[two, rows, lanes] = jnp.where(where, line, halo[two, rows, lanes])


def stream(star, halo, out, b, advances):
    row, lane = iotas((16, 128))
    within = lane % 16
    first, last = lane < 16, lane >= 112

    def roll(x, shift, axis):
        shift %= x.shape[axis]
        return pltpu.roll(x, shift, axis) if shift else x

    def ring(left, right, sign):
        a, c = roll(left, 16 * sign, 1), roll(right, 16 * sign, 1)
        if sign > 0:
            return jnp.where(first, c, a), jnp.where(first, a, c)
        return jnp.where(last, c, a), jnp.where(last, a, c)

    for q in range(19):
        c = VELOCITIES[q]
        old = [star[b, q, :, 128 * half : 128 * half + 128] for half in range(2)]
        new = list(old)
        if c[0]:
            side, p = side_of(q, 0)
            place = side * 8 + p
            for half in range(2):
                plane = halo[0, place : place + 1, 128 * half : 128 * half + 128]
                moved = roll(new[half], c[0], 0)
                new[half] = jnp.where(row == (0 if c[0] > 0 else 15), plane, moved)
        if c[1]:
            side, p = side_of(q, 1)
            border = halo[1, :, 128 * side : 128 * side + 128]
            border = roll(border, -16 * p if side == 0 else 112 - 16 * p, 1)
            if c[0]:
                border = roll(border, c[0], 0)
            a, d = roll(new[0], 16 * c[1], 1), roll(new[1], 16 * c[1], 1)
            if c[1] > 0:
                new = [jnp.where(first, border, a), jnp.where(first, a, d)]
            else:
                new = [jnp.where(last, d, a), jnp.where(last, border, d)]
        if c[2]:
            side, p = side_of(q, 2)
            borders = []
            for half in range(2):
                border = halo[2, :, 128 * half : 128 * half + 128]
                border = roll(border, -p if side == 0 else 7 - p, 1)
                if c[0]:
                    border = roll(border, c[0], 0)
                borders.append(border)
            if c[1]:
                borders = ring(borders[0], borders[1], c[1])
            for half in range(2):
                new[half] = jnp.where(
                    within == (0 if c[2] > 0 else 15), borders[half], roll(new[half], c[2], 1)
                )
        for half in range(2):
            out[b, q, :, 128 * half : 128 * half + 128] = pick(advances, new[half], old[half])


def kernel(
    pop,
    mask_ref,
    level,
    nbr,
    link,
    out,
    star,
    middle,
    faces_a,
    faces_b,
    up_send_a,
    up_send_b,
    up_a,
    up_b,
    down_send,
    down,
    halo,
    wanted_own,
    wanted,
    meta_ss,
    meta_rs,
    mem_ss,
    mem_rs,
    up_ss,
    up_rs,
    down_ss,
    down_rs,
):
    s = lax.axis_index("section")
    m = lax.axis_index("member")
    own = level[s]
    rate = jnp.where(
        own == 0, F32(1.0 / 0.55), jnp.where(own == 1, F32(1.0 / 0.6), F32(1.0 / 0.7))
    )
    has = {-1: m > 0, 0: None, 1: m < NMEM - 1}

    def if_member(dm, do):
        if has[dm] is None:
            do()
        else:
            pl.when(has[dm])(do)

    barrier = pltpu.get_barrier_semaphore()

    def greet(other, dm):
        pl.semaphore_signal(barrier, inc=1, device_id=(other, m + dm), device_id_type=MESH)

    def greet_section(other, carry):
        @pl.when(other != s)
        def _():
            greet(other, 0)

        for dm in (-1, 1):
            if_member(dm, lambda dm=dm: greet(other, dm))
        return carry

    lax.fori_loop(0, NSEC, greet_section, 0)
    for i in range(12):
        code = jnp.int32(-1)
        for k in range(4):
            block = link[i * 4 + k]
            code = jnp.maximum(code, jnp.where(block >= 0, block * 4 + k, -1))
        wanted_own[i] = code

    def first_part(b, carry):
        collide(pop, mask_ref, star, b, rate, own >= 1)
        export(star, faces_a, b)
        restrict(faces_a, down_send, b)
        return carry

    lax.fori_loop(0, 2, first_part, 0)

    one = jnp.int32(1)
    there = jnp.where(m > 0, one, 0) + jnp.where(m < NMEM - 1, one, 0)
    pl.semaphore_wait(barrier, NSEC * (there + 1) - 1)

    def meta_copy(place, other):
        return pltpu.make_async_remote_copy(
            src_ref=wanted_own,
            dst_ref=wanted.at[place],
            send_sem=meta_ss.at[other],
            recv_sem=meta_rs.at[place],
            device_id=(other, m),
            device_id_type=MESH,
        )

    def mem_copy(faces, step, dm, arriving):
        into = (2 + 2 * dm) if arriving else (2 - 2 * dm)
        return pltpu.make_async_remote_copy(
            src_ref=faces.at[pl.ds(2, 2)],
            dst_ref=faces.at[pl.ds(into, 2)],
            send_sem=mem_ss.at[step, (dm + 1) // 2],
            recv_sem=mem_rs.at[step, into // 4],
            device_id=(s, m + dm),
            device_id_type=MESH,
        )

    def up_copy(sends, receives, step, other, place):
        return pltpu.make_async_remote_copy(
            src_ref=sends.at[other],
            dst_ref=receives.at[place],
            send_sem=up_ss.at[step, other],
            recv_sem=up_rs.at[step, place],
            device_id=(other, m),
            device_id_type=MESH,
        )

    def down_copy(other, dm, place, offset):
        return pltpu.make_async_remote_copy(
            src_ref=down_send,
            dst_ref=down.at[place, offset],
            send_sem=down_ss.at[other, dm + 1],
            recv_sem=down_rs.at[place, offset],
            device_id=(other, m + dm),
            device_id_type=MESH,
        )

    def each(low, high, do):
        def step(i, carry):
            do(i)
            return carry

        lax.fori_loop(low, high, step, 0)

    each(0, s, lambda other: meta_copy(s, other).start())
    for dm in (-1, 1):
        if_member(dm, lambda dm=dm: mem_copy(faces_a, 0, dm, False).start())

    def start_down(other):
        for dm in (-1, 0, 1):
            if_member(dm, lambda dm=dm: down_copy(other, dm, s, 1 - dm).start())

    each(1, s, start_down)

    def exchange(faces, sends, receives, step, low, high):
        for dm in (-1, 1):
            if_member(dm, lambda dm=dm: mem_copy(faces, step, dm, True).wait_recv())
        if step == 0:
            each(s + 1, NSEC, lambda other: meta_copy(other, s).wait_recv())

        def send(other):
            select_quadrants(faces, wanted, sends, other, m)
            up_copy(sends, receives, step, other, s).start()

        each(high, NSEC, send)
        each(low, s, lambda other: up_copy(sends, receives, step, s, other).wait_recv())

    exchange(faces_a, up_send_a, up_a, 0, 0, s + 1)

    def wait_down(other):
        for dm in (-1, 0, 1):
            if_member(dm, lambda dm=dm: down_copy(s, dm, other, dm + 1).wait_recv())

    each(jnp.where(s == 0, NSEC, s + 1), NSEC, wait_down)

    def second_part(b, carry):
        build_halo(faces_a, up_a, down, halo, b, nbr, link, wanted_own, level, own, m)
        stream(star, halo, middle, b, own >= 1)
        return carry

    lax.fori_loop(0, 2, second_part, 0)

    def third_part(b, carry):
        collide(middle, mask_ref, star, b, rate, own == 2)
        export(star, faces_b, b)
        return carry

    lax.fori_loop(0, 2, third_part, 0)
    for dm in (-1, 1):
        if_member(dm, lambda dm=dm: mem_copy(faces_b, 1, dm, False).start())
    exchange(faces_b, up_send_b, up_b, 1, 1, jnp.where(s == 0, NSEC, s + 1))

    def fourth_part(b, carry):
        build_halo(faces_b, up_b, None, halo, b, nbr, link, wanted_own, level, own, m)
        stream(star, halo, out, b, own == 2)
        return carry

    lax.fori_loop(0, 2, fourth_part, 0)

    each(0, s, lambda other: meta_copy(s, other).wait_send())
    for dm in (-1, 1):
        if_member(dm, lambda dm=dm: mem_copy(faces_a, 0, dm, False).wait_send())
        if_member(dm, lambda dm=dm: mem_copy(faces_b, 1, dm, False).wait_send())

    def end_down(other):
        for dm in (-1, 0, 1):
            if_member(dm, lambda dm=dm: down_copy(other, dm, s, 1 - dm).wait_send())

    each(1, s, end_down)
    each(s + 1, NSEC, lambda other: up_copy(up_send_a, up_a, 0, other, s).wait_send())
    each(
        jnp.where(s == 0, NSEC, s + 1),
        NSEC,
        lambda other: up_copy(up_send_b, up_b, 1, other, s).wait_send(),
    )


def body(populations, fluid_mask, section_level, neighbours, interface):
    state = pltpu.VMEM((2, 19, 16, 256), F32)
    faces = pltpu.VMEM((6, 3, 4, 8, 128), F32)
    ups = pltpu.VMEM((NSEC, 6, 8, 128), F32)
    vmem = pl.BlockSpec(memory_space=pltpu.VMEM)
    smem = pl.BlockSpec(memory_space=pltpu.SMEM)
    dma = pltpu.SemaphoreType.DMA
    out = pl.pallas_call(
        kernel,
        out_shape=jax.ShapeDtypeStruct((2, 19, 16, 256), F32),
        in_specs=[vmem, vmem, smem, smem, smem],
        out_specs=vmem,
        scratch_shapes=[
            state,
            state,
            faces,
            faces,
            ups,
            ups,
            ups,
            ups,
            pltpu.VMEM((6, 8, 128), F32),
            pltpu.VMEM((NSEC, 3, 6, 8, 128), F32),
            pltpu.VMEM((3, 16, 256), F32),
            pltpu.SMEM((12,), jnp.int32),
            pltpu.SMEM((NSEC, 12), jnp.int32),
            dma((NSEC,)),
            dma((NSEC,)),
            dma((2, 2)),
            dma((2, 2)),
            dma((2, NSEC)),
            dma((2, NSEC)),
            dma((NSEC, 3)),
            dma((NSEC, 3)),
        ],
        compiler_params=pltpu.CompilerParams(
            collective_id=0, has_side_effects=True, vmem_limit_bytes=32 * 1024 * 1024
        ),
        name="lattice_step",
    )(
        populations.reshape(2, 19, 16, 256),
        fluid_mask.reshape(2, 16, 256),
        section_level,
        neighbours.reshape(36),
        interface.reshape(48),
    )
    return out.reshape(2, 19, 4096)


def solution(mesh):
    return jax.shard_map(
        body,
        mesh=mesh,
        in_specs=(
            P(("section", "member"), None, None),
            P(("section", "member"), None),
            P(),
            P(("section", "member"), None),
            P(("section", "member"), None, None),
        ),
        out_specs=P(("section", "member"), None, None),
        check_vma=False,
    )
```

```python
import jax
import jax.numpy as jnp
from jax import lax
from jax.experimental import pallas as pl
from jax.experimental.pallas import tpu as pltpu
from jax.sharding import PartitionSpec as P

MESH = pl.DeviceIdType.MESH
F32 = jnp.float32
NSEC = 8
NMEM = 32

VELOCITIES = (
    (0, 0, 0),
    (1, 0, 0),
    (-1, 0, 0),
    (0, 1, 0),
    (0, -1, 0),
    (0, 0, 1),
    (0, 0, -1),
    (1, 1, 0),
    (-1, -1, 0),
    (1, -1, 0),
    (-1, 1, 0),
    (1, 0, 1),
    (-1, 0, -1),
    (1, 0, -1),
    (-1, 0, 1),
    (0, 1, 1),
    (0, -1, -1),
    (0, 1, -1),
    (0, -1, 1),
)
OPPOSITE = (0, 2, 1, 4, 3, 6, 5, 8, 7, 10, 9, 12, 11, 14, 13, 16, 15, 18, 17)
SIDE_LISTS = tuple(
    tuple(tuple(q for q in range(19) if VELOCITIES[q][axis] == sign) for sign in (1, -1))
    for axis in range(3)
)


def side_of(q, axis):
    side = 0 if VELOCITIES[q][axis] > 0 else 1
    return side, SIDE_LISTS[axis][side].index(q)


def iotas(shape=(8, 128)):
    return lax.broadcasted_iota(jnp.int32, shape, 0), lax.broadcasted_iota(jnp.int32, shape, 1)


def lanes_from(x, index):
    return jnp.take_along_axis(x, index, axis=1)


def rows_from(x, index):
    return jnp.take_along_axis(x, index, axis=0)


def pick(cond, a, b):
    return lax.select(cond, a, b)


def tile_slices(axis, tile):
    first, second = 8 * (tile // 2), 128 * (tile % 2)
    return slice(first, first + 8), slice(second, second + 128)


def woven(b, tile):
    return pl.ds(32 * (tile // 2) + 2 * (tile % 2) + b, 8, stride=4)


def collide(cur, mask_ref, star, b, rate, advances, first):
    for tile in range(4):
        rows, lanes = tile_slices(0, tile)
        if first:
            f = [cur[q, woven(b, tile), :] for q in range(19)]
        else:
            f = [cur[b, q, rows, lanes] for q in range(19)]
        density = f[0]
        for q in range(1, 19):
            density = density + f[q]
        velocity = []
        for axis in range(3):
            plus, minus = SIDE_LISTS[axis]
            momentum = f[plus[0]] - f[minus[0]]
            for i in range(1, 5):
                momentum = momentum + f[plus[i]]
            for i in range(1, 5):
                momentum = momentum - f[minus[i]]
            velocity.append(momentum / density)
        base = 1.0 - 1.5 * (
            velocity[0] * velocity[0] + velocity[1] * velocity[1] + velocity[2] * velocity[2]
        )
        fluid = mask_ref[woven(b, tile), :] == 1
        keep = 1.0 - rate
        scaled = rate * density

        def put(q, relaxed):
            star[b, q, rows, lanes] = pick(
                advances, jnp.where(fluid, relaxed, f[OPPOSITE[q]]), f[q]
            )

        put(0, keep * f[0] + scaled * (1.0 / 3.0) * base)
        axis_weight = scaled * (1.0 / 18.0)
        edge_weight = scaled * (1.0 / 36.0)
        for q in range(1, 19, 2):
            c = VELOCITIES[q]
            along = None
            for axis in range(3):
                if c[axis]:
                    term = velocity[axis] if c[axis] > 0 else -velocity[axis]
                    along = term if along is None else along + term
            weight = axis_weight if q < 7 else edge_weight
            even = weight * (base + 4.5 * along * along)
            odd = weight * (3.0 * along)
            put(q, keep * f[q] + (even + odd))
            put(q + 1, keep * f[q + 1] + (even - odd))


def export(star, faces, b):
    row, lane = iotas()
    group, within = lane // 16, lane % 16
    for side in range(2):
        for p, q in enumerate(SIDE_LISTS[0][side]):
            layer = 15 if side == 0 else 0
            for half in range(2):
                faces[2 + b, 0, side * 2 + half, p : p + 1, :] = star[
                    b, q, layer : layer + 1, 128 * half : 128 * half + 128
                ]
    zero = jnp.zeros((8, 128), F32)
    for a in range(2):
        for side in range(2):
            total = zero
            for p, q in enumerate(SIDE_LISTS[1][side]):
                half = 1 - side
                x = star[b, q, 8 * a : 8 * a + 8, 128 * half : 128 * half + 128]
                shift = (16 * p + 16 if side == 0 else 16 * p) % 128
                x = pltpu.roll(x, shift, 1) if shift else x
                total = jnp.where(group == p, x, total)
            faces[2 + b, 1, a * 2 + side] = total
        for half in range(2):
            total = zero
            for side in range(2):
                for p, q in enumerate(SIDE_LISTS[2][side]):
                    x = star[b, q, 8 * a : 8 * a + 8, 128 * half : 128 * half + 128]
                    shift = 113 + p if side == 0 else 8 + p
                    x = pltpu.roll(x, shift, 1)
                    total = jnp.where(within == side * 8 + p, x, total)
            faces[2 + b, 2, a * 2 + half] = total


def restrict(faces, down, b):
    row, lane = iotas()
    group, within, low = lane // 16, lane % 16, lane % 8
    second = (lane // 8) % 2
    fine = group * 16 + 2 * low
    coarse = (2 * (group % 4)) * 16
    pair_rows = 2 * (row % 4)
    parts = []
    for side in range(2):
        halves = []
        for half in range(2):
            t = faces[2 + b, 0, side * 2 + half]
            t = t + pltpu.roll(t, 127, 1)
            t = t + pltpu.roll(t, 112, 1)
            halves.append(lanes_from(t, coarse + 2 * low))
        parts.append(jnp.where(group < 4, halves[0], halves[1]))
    down[3 * b] = 0.25 * jnp.where(second == 0, parts[0], parts[1])
    parts = []
    for side in range(2):
        rows = []
        for a in range(2):
            t = faces[2 + b, 1, a * 2 + side]
            t = t + pltpu.roll(t, 127, 1)
            t = t + pltpu.roll(t, 7, 0)
            rows.append(rows_from(lanes_from(t, fine), pair_rows))
        parts.append(jnp.where(row < 4, rows[0], rows[1]))
    down[3 * b + 1] = 0.25 * jnp.where(second == 0, parts[0], parts[1])
    rows = []
    for a in range(2):
        halves = []
        for half in range(2):
            t = faces[2 + b, 2, a * 2 + half]
            t = t + pltpu.roll(t, 112, 1)
            halves.append(lanes_from(t, coarse + within))
        t = jnp.where(group < 4, halves[0], halves[1])
        t = t + pltpu.roll(t, 7, 0)
        rows.append(rows_from(t, pair_rows))
    down[3 * b + 2] = 0.25 * jnp.where(row < 4, rows[0], rows[1])


def slot_of(block, member):
    safe = jnp.maximum(block, 0)
    offset = lax.rem(lax.div(safe, 2), NMEM) - member + 1
    return jnp.clip(offset * 2 + lax.rem(safe, 2), 0, 5)


def select_quadrants(faces, wanted, out, other, member):
    row, lane = iotas()
    second = (lane // 8) % 2
    for b in range(2):
        for axis in range(3):
            parts = []
            for side in range(2):
                code = jnp.maximum(wanted[other, b * 6 + 2 * axis + 1 - side], 0)
                quadrant = lax.rem(code, 4)
                first, last = lax.div(quadrant, 2), lax.rem(quadrant, 2)
                slot = slot_of(lax.div(code, 4), member)
                if axis == 0:
                    tile = side * 2 + first
                elif axis == 1:
                    tile = first * 2 + side
                else:
                    tile = quadrant
                t = faces[slot, axis, tile]
                if axis < 2:
                    t = pick(last == side, t, pltpu.roll(t, 8 if side else 120, 1))
                parts.append(t)
            out[other, b * 3 + axis] = jnp.where(second == 0, parts[0], parts[1])


def build_halo(faces, up, down, halo, b, nbr, link, wanted, level, own, member):
    row, lane = iotas()
    group, within, low = lane // 16, lane % 16, lane % 8
    second = (lane // 8) % 2
    spread_rows = [4 * a + row // 2 for a in range(2)]

    def link_state(j):
        code = wanted[b * 6 + j]
        section = lax.div(lax.div(jnp.maximum(code, 0), 4), 2 * NMEM)
        any_link = code >= 0
        coarse = level[section] < own
        return section, any_link, coarse

    def means(axis, j, k):
        block = link[b, k, j]
        safe = jnp.maximum(block, 0)
        section = lax.div(safe, 2 * NMEM)
        offset = jnp.clip(lax.rem(lax.div(safe, 2), NMEM) - member + 1, 0, 2)
        t = down[section, offset, lax.rem(safe, 2) * 3 + axis]
        return pick(block >= 0, t, jnp.zeros_like(t))

    for axis in range(3):
        states, near, quads, ups = [], [], [], []
        for side in range(2):
            j = 2 * axis + 1 - side
            section, any_link, coarse = link_state(j)
            states.append((nbr[b, j] >= 0, any_link, coarse))
            near.append(slot_of(nbr[b, j], member))
            ups.append(up[section, b * 3 + axis])
            if down is not None:
                quads.append([means(axis, j, k) for k in range(4)])
        if axis == 0:
            rest = jnp.where(row == 0, F32(1.0 / 18.0), F32(1.0 / 36.0))
        elif axis == 1:
            rest = jnp.where(group == 0, F32(1.0 / 18.0), F32(1.0 / 36.0))
        else:
            rest = jnp.where(low == 0, F32(1.0 / 18.0), F32(1.0 / 36.0))

        def choose(side, tile, from_up, from_down):
            is_near, any_link, coarse = states[side]
            linked = from_up if from_down is None else pick(coarse, from_up, from_down)
            far = pick(any_link, linked, rest)
            return pick(is_near, faces[near[side], axis, tile], far)

        if axis < 2:
            for side in range(2):
                if axis == 1:
                    wide = lanes_from(ups[side], group * 16 + side * 8 + within // 2)
                for a in range(2):
                    if axis == 0:
                        tile = side * 2 + a
                        from_up = lanes_from(
                            ups[side], (4 * a + group // 2) * 16 + side * 8 + within // 2
                        )
                    else:
                        tile = a * 2 + side
                        from_up = rows_from(wide, spread_rows[a])
                    from_down = None
                    if down is not None:
                        low_part, high_part = quads[side][2 * a], quads[side][2 * a + 1]
                        if side:
                            low_part = pltpu.roll(low_part, 120, 1)
                        else:
                            high_part = pltpu.roll(high_part, 8, 1)
                        from_down = jnp.where(second == 0, low_part, high_part)
                    rows, lanes = tile_slices(axis, tile)
                    halo[axis, rows, lanes] = choose(side, tile, from_up, from_down)
        else:
            both = jnp.where(second == 0, ups[0], ups[1])
            for half in range(2):
                wide = lanes_from(both, (4 * half + group // 2) * 16 + within)
                for a in range(2):
                    tile = a * 2 + half
                    from_up = rows_from(wide, spread_rows[a])
                    parts = [
                        choose(side, tile, from_up, quads[side][tile] if down is not None else None)
                        for side in range(2)
                    ]
                    rows, lanes = tile_slices(axis, tile)
                    halo[axis, rows, lanes] = jnp.where(second == 0, parts[0], parts[1])

    for q in range(7, 19):
        c = VELOCITIES[q]
        one, two = [axis for axis in range(3) if c[axis]]
        side, p = side_of(q, two)
        block = nbr[b, OPPOSITE[q] - 1]
        slot = slot_of(block, member)
        far_end = c[one] > 0
        if two == 1:
            tiles = [(1 if far_end else 0) * 2 + side]
            where = (row == (7 if far_end else 0)) & (group == p)
        elif one == 0:
            tiles = [(1 if far_end else 0) * 2 + half for half in range(2)]
            where = (row == (7 if far_end else 0)) & (within == side * 8 + p)
        else:
            tiles = [a * 2 + (1 if far_end else 0) for a in range(2)]
            where = lane == (7 if far_end else 0) * 16 + side * 8 + p
        for tile in tiles:
            rows, lanes = tile_slices(two, tile)
            line = faces[slot, two, tile]
            line = pick(block >= 0, line, jnp.full_like(line, 1.0 / 36.0))
            halo[two, rows, lanes] = jnp.where(where, line, halo[two, rows, lanes])


def stream(star, halo, out, b, advances, final):
    row, lane = iotas((16, 128))
    within = lane % 16
    first, last = lane < 16, lane >= 112

    def roll(x, shift, axis):
        shift %= x.shape[axis]
        return pltpu.roll(x, shift, axis) if shift else x

    def ring(left, right, sign):
        a, c = roll(left, 16 * sign, 1), roll(right, 16 * sign, 1)
        if sign > 0:
            return jnp.where(first, c, a), jnp.where(first, a, c)
        return jnp.where(last, c, a), jnp.where(last, a, c)

    for q in range(19):
        c = VELOCITIES[q]
        old = [star[b, q, :, 128 * half : 128 * half + 128] for half in range(2)]
        new = list(old)
        if c[0]:
            side, p = side_of(q, 0)
            place = side * 8 + p
            for half in range(2):
                plane = halo[0, place : place + 1, 128 * half : 128 * half + 128]
                moved = roll(new[half], c[0], 0)
                new[half] = jnp.where(row == (0 if c[0] > 0 else 15), plane, moved)
        if c[1]:
            side, p = side_of(q, 1)
            border = halo[1, :, 128 * side : 128 * side + 128]
            border = roll(border, -16 * p if side == 0 else 112 - 16 * p, 1)
            if c[0]:
                border = roll(border, c[0], 0)
            a, d = roll(new[0], 16 * c[1], 1), roll(new[1], 16 * c[1], 1)
            if c[1] > 0:
                new = [jnp.where(first, border, a), jnp.where(first, a, d)]
            else:
                new = [jnp.where(last, d, a), jnp.where(last, border, d)]
        if c[2]:
            side, p = side_of(q, 2)
            borders = []
            for half in range(2):
                border = halo[2, :, 128 * half : 128 * half + 128]
                border = roll(border, -p if side == 0 else 7 - p, 1)
                if c[0]:
                    border = roll(border, c[0], 0)
                borders.append(border)
            if c[1]:
                borders = ring(borders[0], borders[1], c[1])
            for half in range(2):
                new[half] = jnp.where(
                    within == (0 if c[2] > 0 else 15), borders[half], roll(new[half], c[2], 1)
                )
        for half in range(2):
            result = pick(advances, new[half], old[half])
            if final:
                for a in range(2):
                    out[q, woven(b, 2 * a + half), :] = result[8 * a : 8 * a + 8]
            else:
                out[b, q, :, 128 * half : 128 * half + 128] = result


def kernel(
    pop_hbm,
    mask_hbm,
    level_hbm,
    nbr_hbm,
    link_hbm,
    out,
    pop,
    mask_ref,
    level,
    nbr,
    link,
    in_sems,
    star,
    middle,
    faces_a,
    faces_b,
    up_send_a,
    up_send_b,
    up_a,
    up_b,
    down_send,
    down,
    halo,
    wanted_own,
    wanted,
    meta_ss,
    meta_rs,
    mem_ss,
    mem_rs,
    up_ss,
    up_rs,
    down_ss,
    down_rs,
):
    s = lax.axis_index("section")
    m = lax.axis_index("member")
    loads = [
        pltpu.make_async_copy(src, dst, in_sems.at[i])
        for i, (src, dst) in enumerate(
            [
                (level_hbm, level),
                (link_hbm, link),
                (nbr_hbm, nbr),
                (pop_hbm, pop),
                (mask_hbm, mask_ref),
            ]
        )
    ]
    for load in loads:
        load.start()
    has = {-1: m > 0, 0: None, 1: m < NMEM - 1}

    def if_member(dm, do):
        if has[dm] is None:
            do()
        else:
            pl.when(has[dm])(do)

    barrier = pltpu.get_barrier_semaphore()

    def greet(other, dm):
        pl.semaphore_signal(barrier, inc=1, device_id=(other, m + dm), device_id_type=MESH)

    def greet_section(other, carry):
        @pl.when(other != s)
        def _():
            greet(other, 0)

        for dm in (-1, 1):
            if_member(dm, lambda dm=dm: greet(other, dm))
        return carry

    lax.fori_loop(0, NSEC, greet_section, 0)
    for load in loads:
        load.wait()
    own = level[s]
    rate = jnp.where(
        own == 0, F32(1.0 / 0.55), jnp.where(own == 1, F32(1.0 / 0.6), F32(1.0 / 0.7))
    )
    for i in range(12):
        code = jnp.int32(-1)
        for k in range(4):
            block = link[i // 6, k, i % 6]
            code = jnp.maximum(code, jnp.where(block >= 0, block * 4 + k, -1))
        wanted_own[i] = code

    def first_part(b, carry):
        collide(pop, mask_ref, star, b, rate, own >= 1, True)
        export(star, faces_a, b)
        restrict(faces_a, down_send, b)
        return carry

    lax.fori_loop(0, 2, first_part, 0)

    one = jnp.int32(1)
    there = jnp.where(m > 0, one, 0) + jnp.where(m < NMEM - 1, one, 0)
    pl.semaphore_wait(barrier, NSEC * (there + 1) - 1)

    def meta_copy(place, other):
        return pltpu.make_async_remote_copy(
            src_ref=wanted_own,
            dst_ref=wanted.at[place],
            send_sem=meta_ss.at[other],
            recv_sem=meta_rs.at[place],
            device_id=(other, m),
            device_id_type=MESH,
        )

    def mem_copy(faces, step, dm, arriving):
        into = (2 + 2 * dm) if arriving else (2 - 2 * dm)
        return pltpu.make_async_remote_copy(
            src_ref=faces.at[pl.ds(2, 2)],
            dst_ref=faces.at[pl.ds(into, 2)],
            send_sem=mem_ss.at[step, (dm + 1) // 2],
            recv_sem=mem_rs.at[step, into // 4],
            device_id=(s, m + dm),
            device_id_type=MESH,
        )

    def up_copy(sends, receives, step, other, place):
        return pltpu.make_async_remote_copy(
            src_ref=sends.at[other],
            dst_ref=receives.at[place],
            send_sem=up_ss.at[step, other],
            recv_sem=up_rs.at[step, place],
            device_id=(other, m),
            device_id_type=MESH,
        )

    def down_copy(other, dm, place, offset):
        return pltpu.make_async_remote_copy(
            src_ref=down_send,
            dst_ref=down.at[place, offset],
            send_sem=down_ss.at[other, dm + 1],
            recv_sem=down_rs.at[place, offset],
            device_id=(other, m + dm),
            device_id_type=MESH,
        )

    def each(low, high, do):
        def step(i, carry):
            do(i)
            return carry

        lax.fori_loop(low, high, step, 0)

    each(0, s, lambda other: meta_copy(s, other).start())
    for dm in (-1, 1):
        if_member(dm, lambda dm=dm: mem_copy(faces_a, 0, dm, False).start())

    def start_down(other):
        for dm in (-1, 0, 1):
            if_member(dm, lambda dm=dm: down_copy(other, dm, s, 1 - dm).start())

    each(1, s, start_down)

    def exchange(faces, sends, receives, step, low, high):
        for dm in (-1, 1):
            if_member(dm, lambda dm=dm: mem_copy(faces, step, dm, True).wait_recv())
        if step == 0:
            each(s + 1, NSEC, lambda other: meta_copy(other, s).wait_recv())

        def send(other):
            select_quadrants(faces, wanted, sends, other, m)
            up_copy(sends, receives, step, other, s).start()

        each(high, NSEC, send)
        each(low, s, lambda other: up_copy(sends, receives, step, s, other).wait_recv())

    exchange(faces_a, up_send_a, up_a, 0, 0, s + 1)

    def wait_down(other):
        for dm in (-1, 0, 1):
            if_member(dm, lambda dm=dm: down_copy(s, dm, other, dm + 1).wait_recv())

    each(jnp.where(s == 0, NSEC, s + 1), NSEC, wait_down)

    def second_part(b, carry):
        build_halo(faces_a, up_a, down, halo, b, nbr, link, wanted_own, level, own, m)
        stream(star, halo, middle, b, own >= 1, False)
        return carry

    lax.fori_loop(0, 2, second_part, 0)

    def third_part(b, carry):
        collide(middle, mask_ref, star, b, rate, own == 2, False)
        export(star, faces_b, b)
        return carry

    lax.fori_loop(0, 2, third_part, 0)
    for dm in (-1, 1):
        if_member(dm, lambda dm=dm: mem_copy(faces_b, 1, dm, False).start())
    exchange(faces_b, up_send_b, up_b, 1, 1, jnp.where(s == 0, NSEC, s + 1))

    def fourth_part(b, carry):
        build_halo(faces_b, up_b, None, halo, b, nbr, link, wanted_own, level, own, m)
        stream(star, halo, out, b, own == 2, True)
        return carry

    lax.fori_loop(0, 2, fourth_part, 0)

    each(0, s, lambda other: meta_copy(s, other).wait_send())
    for dm in (-1, 1):
        if_member(dm, lambda dm=dm: mem_copy(faces_a, 0, dm, False).wait_send())
        if_member(dm, lambda dm=dm: mem_copy(faces_b, 1, dm, False).wait_send())

    def end_down(other):
        for dm in (-1, 0, 1):
            if_member(dm, lambda dm=dm: down_copy(other, dm, s, 1 - dm).wait_send())

    each(1, s, end_down)
    each(s + 1, NSEC, lambda other: up_copy(up_send_a, up_a, 0, other, s).wait_send())
    each(
        jnp.where(s == 0, NSEC, s + 1),
        NSEC,
        lambda other: up_copy(up_send_b, up_b, 1, other, s).wait_send(),
    )


def body(populations, fluid_mask, section_level, neighbours, interface):
    state = pltpu.VMEM((2, 19, 16, 256), F32)
    faces = pltpu.VMEM((6, 3, 4, 8, 128), F32)
    ups = pltpu.VMEM((NSEC, 6, 8, 128), F32)
    vmem = pl.BlockSpec(memory_space=pltpu.VMEM)
    hbm = pl.BlockSpec(memory_space=pltpu.HBM)
    dma = pltpu.SemaphoreType.DMA
    out = pl.pallas_call(
        kernel,
        out_shape=jax.ShapeDtypeStruct((19, 64, 128), F32),
        in_specs=[hbm] * 5,
        out_specs=vmem,
        scratch_shapes=[
            pltpu.VMEM((19, 64, 128), F32),
            pltpu.VMEM((64, 128), jnp.int32),
            pltpu.SMEM((NSEC,), jnp.int32),
            pltpu.SMEM((2, 18), jnp.int32),
            pltpu.SMEM((2, 4, 6), jnp.int32),
            dma((5,)),
            state,
            state,
            faces,
            faces,
            ups,
            ups,
            ups,
            ups,
            pltpu.VMEM((6, 8, 128), F32),
            pltpu.VMEM((NSEC, 3, 6, 8, 128), F32),
            pltpu.VMEM((3, 16, 256), F32),
            pltpu.SMEM((12,), jnp.int32),
            pltpu.SMEM((NSEC, 12), jnp.int32),
            dma((NSEC,)),
            dma((NSEC,)),
            dma((2, 2)),
            dma((2, 2)),
            dma((2, NSEC)),
            dma((2, NSEC)),
            dma((NSEC, 3)),
            dma((NSEC, 3)),
        ],
        compiler_params=pltpu.CompilerParams(
            collective_id=0, has_side_effects=True, vmem_limit_bytes=62 * 1024 * 1024
        ),
        name="lattice_step",
    )(
        populations.reshape(2, 19, 32, 128).transpose(1, 2, 0, 3).reshape(19, 64, 128),
        fluid_mask.reshape(2, 32, 128).transpose(1, 0, 2).reshape(64, 128),
        section_level,
        neighbours,
        interface.transpose(0, 2, 1),
    )
    return out.reshape(19, 32, 2, 128).transpose(2, 0, 1, 3).reshape(2, 19, 4096)


def solution(mesh):
    return jax.shard_map(
        body,
        mesh=mesh,
        in_specs=(
            P(("section", "member"), None, None),
            P(("section", "member"), None),
            P(),
            P(("section", "member"), None),
            P(("section", "member"), None, None),
        ),
        out_specs=P(("section", "member"), None, None),
        check_vma=False,
    )
```

```python
import jax
import jax.numpy as jnp
from jax import lax
from jax.experimental import pallas as pl
from jax.experimental.pallas import tpu as pltpu
from jax.sharding import PartitionSpec as P

MESH = pl.DeviceIdType.MESH
F32 = jnp.float32
NSEC = 8
NMEM = 32

VELOCITIES = (
    (0, 0, 0),
    (1, 0, 0),
    (-1, 0, 0),
    (0, 1, 0),
    (0, -1, 0),
    (0, 0, 1),
    (0, 0, -1),
    (1, 1, 0),
    (-1, -1, 0),
    (1, -1, 0),
    (-1, 1, 0),
    (1, 0, 1),
    (-1, 0, -1),
    (1, 0, -1),
    (-1, 0, 1),
    (0, 1, 1),
    (0, -1, -1),
    (0, 1, -1),
    (0, -1, 1),
)
OPPOSITE = (0, 2, 1, 4, 3, 6, 5, 8, 7, 10, 9, 12, 11, 14, 13, 16, 15, 18, 17)
SIDE_LISTS = tuple(
    tuple(tuple(q for q in range(19) if VELOCITIES[q][axis] == sign) for sign in (1, -1))
    for axis in range(3)
)


def side_of(q, axis):
    side = 0 if VELOCITIES[q][axis] > 0 else 1
    return side, SIDE_LISTS[axis][side].index(q)


def iotas(shape=(8, 128)):
    return lax.broadcasted_iota(jnp.int32, shape, 0), lax.broadcasted_iota(jnp.int32, shape, 1)


def lanes_from(x, index):
    return jnp.take_along_axis(x, index, axis=1)


def rows_from(x, index):
    return jnp.take_along_axis(x, index, axis=0)


def pick(cond, a, b):
    return lax.select(cond, a, b)


def tile_slices(axis, tile):
    first, second = 8 * (tile // 2), 128 * (tile % 2)
    return slice(first, first + 8), slice(second, second + 128)


def packing(count):
    packed = -(-count * 5 // 8)
    spare = [(d, g) for d in range(packed) for g in (5, 6, 7)]
    runs = []
    for source in range(packed, count):
        for group in range(5):
            d, g = spare.pop(0)
            last = runs[-1] if runs else None
            if last and last[0] == source and last[2] == d and last[3] + last[4] == g:
                runs[-1] = last[:4] + (last[4] + 1,)
            else:
                runs.append((source, group, d, g, 1))
    return packed, runs


def lane_roll(x, shift):
    shift %= 128
    return pltpu.roll(x, shift, 1) if shift else x


def pack(tiles):
    lane = iotas()[1]
    packed, runs = packing(len(tiles))
    result = list(tiles[:packed])
    for source, group, d, g, length in runs:
        moved = lane_roll(tiles[source], 16 * (g - group))
        inside = (lane >= 16 * g) & (lane < 16 * (g + length))
        result[d] = jnp.where(inside, moved, result[d])
    return result


def unpack(load, source, count):
    lane = iotas()[1]
    packed, runs = packing(count)
    if source < packed:
        return load(source)
    result = None
    for which, group, d, g, length in runs:
        if which == source:
            moved = lane_roll(load(d), 16 * (group - g))
            result = moved if result is None else jnp.where(lane >= 16 * group, moved, result)
    return result


def store_message(tiles, put):
    for d, t in enumerate(pack([tiles[1], tiles[2], tiles[4], tiles[5]])):
        put(8 * d, t)
    for b in range(2):
        put(24 + 5 * b, tiles[3 * b][0:5])


def message_tile(load, axis, block):
    if axis == 0:
        pair = load(24), load(29)
    else:
        pair = tuple(unpack(lambda d: load(8 * d), 2 * b + axis - 1, 4) for b in range(2))
    return pick(block == 0, pair[0], pair[1])


def face_order(lane):
    return (lane % 8) * 16 + lane // 8 % 2 * 8 + lane // 16


def woven(b, tile):
    return pl.ds(32 * (tile // 2) + 2 * (tile % 2) + b, 8, stride=4)


def collide(cur, mask_ref, star, b, rate, advances, first):
    for tile in range(4):
        rows, lanes = tile_slices(0, tile)
        if first:
            f = [cur[q, woven(b, tile), :] for q in range(19)]
        else:
            f = [cur[b, q, rows, lanes] for q in range(19)]
        density = f[0]
        for q in range(1, 19):
            density = density + f[q]
        velocity = []
        for axis in range(3):
            plus, minus = SIDE_LISTS[axis]
            momentum = f[plus[0]] - f[minus[0]]
            for i in range(1, 5):
                momentum = momentum + f[plus[i]]
            for i in range(1, 5):
                momentum = momentum - f[minus[i]]
            velocity.append(momentum / density)
        base = 1.0 - 1.5 * (
            velocity[0] * velocity[0] + velocity[1] * velocity[1] + velocity[2] * velocity[2]
        )
        fluid = mask_ref[woven(b, tile), :] == 1
        keep = 1.0 - rate
        scaled = rate * density

        def put(q, relaxed):
            star[b, q, rows, lanes] = pick(
                advances, jnp.where(fluid, relaxed, f[OPPOSITE[q]]), f[q]
            )

        put(0, keep * f[0] + scaled * (1.0 / 3.0) * base)
        axis_weight = scaled * (1.0 / 18.0)
        edge_weight = scaled * (1.0 / 36.0)
        for q in range(1, 19, 2):
            c = VELOCITIES[q]
            along = None
            for axis in range(3):
                if c[axis]:
                    term = velocity[axis] if c[axis] > 0 else -velocity[axis]
                    along = term if along is None else along + term
            weight = axis_weight if q < 7 else edge_weight
            even = weight * (base + 4.5 * along * along)
            odd = weight * (3.0 * along)
            put(q, keep * f[q] + (even + odd))
            put(q + 1, keep * f[q + 1] + (even - odd))


def export(star, faces, message, b):
    row, lane = iotas()
    group, within = lane // 16, lane % 16
    for side in range(2):
        for p, q in enumerate(SIDE_LISTS[0][side]):
            layer = 15 if side == 0 else 0
            for half in range(2):
                line = star[b, q, layer : layer + 1, 128 * half : 128 * half + 128]
                place = side * 2 + half
                faces[2 + b, 0, place, p : p + 1, :] = line
                message[b, 40 + 5 * place + p : 41 + 5 * place + p, :] = line
    zero = jnp.zeros((8, 128), F32)
    tiles = [None] * 8
    order = face_order(lane)
    for a in range(2):
        for side in range(2):
            total = zero
            for p, q in enumerate(SIDE_LISTS[1][side]):
                half = 1 - side
                x = star[b, q, 8 * a : 8 * a + 8, 128 * half : 128 * half + 128]
                shift = (16 * p + 16 if side == 0 else 16 * p) % 128
                x = pltpu.roll(x, shift, 1) if shift else x
                total = jnp.where(group == p, x, total)
            tiles[a * 2 + side] = total
        for half in range(2):
            total = zero
            for side in range(2):
                for p, q in enumerate(SIDE_LISTS[2][side]):
                    x = star[b, q, 8 * a : 8 * a + 8, 128 * half : 128 * half + 128]
                    shift = 113 + p if side == 0 else 8 + p
                    x = pltpu.roll(x, shift, 1)
                    total = jnp.where(within == side * 8 + p, x, total)
            tiles[4 + a * 2 + half] = lanes_from(total, order)
    for i, t in enumerate(tiles):
        faces[2 + b, 1 + i // 4, i % 4] = t
    for d, t in enumerate(pack(tiles)):
        message[b, 8 * d : 8 * d + 8, :] = t


def open_message(message, faces, place):
    def one(b, carry):
        for i in range(8):
            faces[place + b, 1 + i // 4, i % 4] = unpack(
                lambda d: message[b, 8 * d : 8 * d + 8, :], i, 8
            )
        for tile in range(4):
            faces[place + b, 0, tile, 0:5, :] = message[b, 40 + 5 * tile : 45 + 5 * tile, :]
        return carry

    lax.fori_loop(0, 2, one, 0)


def restrict(faces, down):
    tiles = [t for b in range(2) for t in restrict_block(faces, b)]

    def put(row, t):
        down[row : row + t.shape[0], :] = t

    store_message(tiles, put)


def restrict_block(faces, b):
    row, lane = iotas()
    group, within, low = lane // 16, lane % 16, lane % 8
    second = (lane // 8) % 2
    fine = group * 16 + 2 * low
    coarse = (2 * (group % 4)) * 16
    pair_rows = 2 * (row % 4)
    parts = []
    for side in range(2):
        halves = []
        for half in range(2):
            t = faces[2 + b, 0, side * 2 + half]
            t = t + pltpu.roll(t, 127, 1)
            t = t + pltpu.roll(t, 112, 1)
            halves.append(lanes_from(t, coarse + 2 * low))
        parts.append(jnp.where(group < 4, halves[0], halves[1]))
    tiles = [0.25 * jnp.where(second == 0, parts[0], parts[1])]
    parts = []
    for side in range(2):
        rows = []
        for a in range(2):
            t = faces[2 + b, 1, a * 2 + side]
            t = t + pltpu.roll(t, 127, 1)
            t = t + pltpu.roll(t, 7, 0)
            rows.append(rows_from(lanes_from(t, fine), pair_rows))
        parts.append(jnp.where(row < 4, rows[0], rows[1]))
    tiles.append(0.25 * jnp.where(second == 0, parts[0], parts[1]))
    rows = []
    for a in range(2):
        halves = []
        for half in range(2):
            t = faces[2 + b, 2, a * 2 + half]
            t = t + pltpu.roll(t, 127, 1)
            halves.append(lanes_from(t, group * 16 + second * 8 + 2 * (low % 4)))
        t = jnp.where(low < 4, halves[0], halves[1])
        t = t + pltpu.roll(t, 7, 0)
        rows.append(rows_from(t, pair_rows))
    tiles.append(0.25 * jnp.where(row < 4, rows[0], rows[1]))
    return tiles


def member_offset(block, member):
    return jnp.clip(lax.rem(lax.div(block, 2), NMEM) - member + 1, 0, 2)


def slot_of(block, member):
    safe = jnp.maximum(block, 0)
    offset = lax.rem(lax.div(safe, 2), NMEM) - member + 1
    return jnp.clip(offset * 2 + lax.rem(safe, 2), 0, 5)


def select_quadrants(faces, wanted, out, other, asker, member, direct):
    row, lane = iotas()
    second = (lane // 8) % 2
    tiles = []
    for b in range(2):
        for axis in range(3):
            parts = []
            for side in range(2):
                code = jnp.maximum(wanted[other, asker, b * 6 + 2 * axis + 1 - side], 0)
                quadrant = lax.rem(code, 4)
                first, last = lax.div(quadrant, 2), lax.rem(quadrant, 2)
                block = lax.div(code, 4)
                slot = 2 + lax.rem(block, 2) if direct else slot_of(block, member)
                if axis == 0:
                    tile = side * 2 + first
                elif axis == 1:
                    tile = first * 2 + side
                else:
                    tile = quadrant
                t = faces[slot, axis, tile]
                if axis < 2:
                    t = pick(last == side, t, pltpu.roll(t, 8 if side else 120, 1))
                parts.append(t)
            tiles.append(jnp.where(second == 0, parts[0], parts[1]))

    def put(row, t):
        out[other, asker, row : row + t.shape[0], :] = t

    store_message(tiles, put)


def build_halo(faces, up, down, halo, b, nbr, link, wanted, level, own, member, direct):
    row, lane = iotas()
    group, within, low = lane // 16, lane % 16, lane % 8
    second = (lane // 8) % 2
    spread_rows = [4 * a + row // 2 for a in range(2)]

    def link_state(j):
        code = wanted[b * 6 + j]
        block = lax.div(jnp.maximum(code, 0), 4)
        section = lax.div(block, 2 * NMEM)
        offset = member_offset(block, member) if direct else 1
        any_link = code >= 0
        coarse = level[section] < own
        return section, offset, any_link, coarse

    def means(axis, j, k):
        block = link[b, k, j]
        safe = jnp.maximum(block, 0)
        section = lax.div(safe, 2 * NMEM)
        offset = member_offset(safe, member)
        t = message_tile(
            lambda row: down[section, offset, row : row + 8, :], axis, lax.rem(safe, 2)
        )
        return pick(block >= 0, t, jnp.zeros_like(t))

    for axis in range(3):
        states, near, quads, ups = [], [], [], []
        for side in range(2):
            j = 2 * axis + 1 - side
            section, offset, any_link, coarse = link_state(j)
            states.append((nbr[b, j] >= 0, any_link, coarse))
            near.append(slot_of(nbr[b, j], member))
            ups.append(
                message_tile(
                    lambda row, section=section, offset=offset: up[section, offset, row : row + 8, :],
                    axis,
                    b,
                )
            )
            if down is not None:
                quads.append([means(axis, j, k) for k in range(4)])
        if axis == 0:
            rest = jnp.where(row == 0, F32(1.0 / 18.0), F32(1.0 / 36.0))
        else:
            rest = jnp.where(group == 0, F32(1.0 / 18.0), F32(1.0 / 36.0))

        def choose(side, tile, from_up, from_down):
            is_near, any_link, coarse = states[side]
            linked = from_up if from_down is None else pick(coarse, from_up, from_down)
            far = pick(any_link, linked, rest)
            return pick(is_near, faces[near[side], axis, tile], far)

        if axis < 2:
            for side in range(2):
                if axis == 1:
                    wide = lanes_from(ups[side], group * 16 + side * 8 + within // 2)
                for a in range(2):
                    if axis == 0:
                        tile = side * 2 + a
                        from_up = lanes_from(
                            ups[side], (4 * a + group // 2) * 16 + side * 8 + within // 2
                        )
                    else:
                        tile = a * 2 + side
                        from_up = rows_from(wide, spread_rows[a])
                    from_down = None
                    if down is not None:
                        low_part, high_part = quads[side][2 * a], quads[side][2 * a + 1]
                        if side:
                            low_part = pltpu.roll(low_part, 120, 1)
                        else:
                            high_part = pltpu.roll(high_part, 8, 1)
                        from_down = jnp.where(second == 0, low_part, high_part)
                    rows, lanes = tile_slices(axis, tile)
                    halo[axis, rows, lanes] = choose(side, tile, from_up, from_down)
        else:
            both = jnp.where(second == 0, ups[0], ups[1])
            for half in range(2):
                wide = lanes_from(both, group * 16 + second * 8 + 4 * half + low // 2)
                for a in range(2):
                    tile = a * 2 + half
                    from_up = rows_from(wide, spread_rows[a])
                    parts = [
                        choose(side, tile, from_up, quads[side][tile] if down is not None else None)
                        for side in range(2)
                    ]
                    rows, lanes = tile_slices(axis, tile)
                    halo[axis, rows, lanes] = jnp.where(second == 0, parts[0], parts[1])

    for q in range(7, 19):
        c = VELOCITIES[q]
        one, two = [axis for axis in range(3) if c[axis]]
        side, p = side_of(q, two)
        block = nbr[b, OPPOSITE[q] - 1]
        slot = slot_of(block, member)
        far_end = c[one] > 0
        if two == 1:
            tiles = [(1 if far_end else 0) * 2 + side]
            where = (row == (7 if far_end else 0)) & (group == p)
        elif one == 0:
            tiles = [(1 if far_end else 0) * 2 + half for half in range(2)]
            where = (row == (7 if far_end else 0)) & (group == p) & (second == side)
        else:
            tiles = [a * 2 + (1 if far_end else 0) for a in range(2)]
            where = lane == p * 16 + side * 8 + (7 if far_end else 0)
        for tile in tiles:
            rows, lanes = tile_slices(two, tile)
            line = faces[slot, two, tile]
            line = pick(block >= 0, line, jnp.full_like(line, 1.0 / 36.0))
            halo[two, rows, lanes] = jnp.where(where, line, halo[two, rows, lanes])
    order = face_order(lane)
    for tile in range(4):
        rows, lanes = tile_slices(2, tile)
        halo[2, rows, lanes] = lanes_from(halo[2, rows, lanes], order)


def stream(star, halo, out, b, advances, final):
    row, lane = iotas((16, 128))
    within = lane % 16
    first, last = lane < 16, lane >= 112

    def roll(x, shift, axis):
        shift %= x.shape[axis]
        return pltpu.roll(x, shift, axis) if shift else x

    def ring(left, right, sign):
        a, c = roll(left, 16 * sign, 1), roll(right, 16 * sign, 1)
        if sign > 0:
            return jnp.where(first, c, a), jnp.where(first, a, c)
        return jnp.where(last, c, a), jnp.where(last, a, c)

    for q in range(19):
        c = VELOCITIES[q]
        old = [star[b, q, :, 128 * half : 128 * half + 128] for half in range(2)]
        new = list(old)
        if c[0]:
            side, p = side_of(q, 0)
            place = side * 8 + p
            for half in range(2):
                plane = halo[0, place : place + 1, 128 * half : 128 * half + 128]
                moved = roll(new[half], c[0], 0)
                new[half] = jnp.where(row == (0 if c[0] > 0 else 15), plane, moved)
        if c[1]:
            side, p = side_of(q, 1)
            border = halo[1, :, 128 * side : 128 * side + 128]
            border = roll(border, -16 * p if side == 0 else 112 - 16 * p, 1)
            if c[0]:
                border = roll(border, c[0], 0)
            a, d = roll(new[0], 16 * c[1], 1), roll(new[1], 16 * c[1], 1)
            if c[1] > 0:
                new = [jnp.where(first, border, a), jnp.where(first, a, d)]
            else:
                new = [jnp.where(last, d, a), jnp.where(last, border, d)]
        if c[2]:
            side, p = side_of(q, 2)
            borders = []
            for half in range(2):
                border = halo[2, :, 128 * half : 128 * half + 128]
                border = roll(border, -p if side == 0 else 7 - p, 1)
                if c[0]:
                    border = roll(border, c[0], 0)
                borders.append(border)
            if c[1]:
                borders = ring(borders[0], borders[1], c[1])
            for half in range(2):
                new[half] = jnp.where(
                    within == (0 if c[2] > 0 else 15), borders[half], roll(new[half], c[2], 1)
                )
        for half in range(2):
            result = pick(advances, new[half], old[half])
            if final:
                for a in range(2):
                    out[q, woven(b, 2 * a + half), :] = result[8 * a : 8 * a + 8]
            else:
                out[b, q, :, 128 * half : 128 * half + 128] = result


def kernel(
    pop_hbm,
    mask_hbm,
    level_hbm,
    nbr_hbm,
    link_hbm,
    out,
    pop,
    mask_ref,
    level,
    nbr,
    link,
    in_sems,
    star,
    middle,
    faces_a,
    faces_b,
    out_a,
    out_b,
    in_a,
    in_b,
    up_send_a,
    up_send_b,
    up_a,
    up_b,
    down_send,
    down,
    halo,
    wanted_own,
    wanted,
    meta_ss,
    meta_rs,
    mem_ss,
    mem_rs,
    up_ss,
    up_rs,
    down_ss,
    down_rs,
):
    s = lax.axis_index("section")
    m = lax.axis_index("member")
    loads = [
        pltpu.make_async_copy(src, dst, in_sems.at[i])
        for i, (src, dst) in enumerate(
            [
                (level_hbm, level),
                (link_hbm, link),
                (nbr_hbm, nbr),
                (pop_hbm, pop),
                (mask_hbm, mask_ref),
            ]
        )
    ]
    for load in loads:
        load.start()
    has = {-1: m > 0, 0: None, 1: m < NMEM - 1}

    def if_member(dm, do):
        if has[dm] is None:
            do()
        else:
            pl.when(has[dm])(do)

    barrier = pltpu.get_barrier_semaphore()

    def greet(other, dm):
        pl.semaphore_signal(barrier, inc=1, device_id=(other, m + dm), device_id_type=MESH)

    def greet_section(other, carry):
        @pl.when(other != s)
        def _():
            greet(other, 0)

        for dm in (-1, 1):
            if_member(dm, lambda dm=dm: greet(other, dm))
        return carry

    lax.fori_loop(0, NSEC, greet_section, 0)
    for load in loads:
        load.wait()
    own = level[s]
    rate = jnp.where(
        own == 0, F32(1.0 / 0.55), jnp.where(own == 1, F32(1.0 / 0.6), F32(1.0 / 0.7))
    )
    for i in range(12):
        code = jnp.int32(-1)
        for k in range(4):
            block = link[i // 6, k, i % 6]
            code = jnp.maximum(code, jnp.where(block >= 0, block * 4 + k, -1))
        wanted_own[i] = code

    def first_part(b, carry):
        collide(pop, mask_ref, star, b, rate, own >= 1, True)
        export(star, faces_a, out_a, b)
        return carry

    lax.fori_loop(0, 2, first_part, 0)
    restrict(faces_a, down_send)

    one = jnp.int32(1)
    there = jnp.where(m > 0, one, 0) + jnp.where(m < NMEM - 1, one, 0)
    pl.semaphore_wait(barrier, NSEC * (there + 1) - 1)

    def meta_copy(place, offset, other, dm):
        return pltpu.make_async_remote_copy(
            src_ref=wanted_own,
            dst_ref=wanted.at[place, offset],
            send_sem=meta_ss.at[other, dm + 1],
            recv_sem=meta_rs.at[place, offset],
            device_id=(other, m + dm),
            device_id_type=MESH,
        )

    def mem_copy(sends, receives, step, dm, arriving):
        into = (1 + dm) // 2 if arriving else (1 - dm) // 2
        return pltpu.make_async_remote_copy(
            src_ref=sends,
            dst_ref=receives.at[into],
            send_sem=mem_ss.at[step, (dm + 1) // 2],
            recv_sem=mem_rs.at[step, into],
            device_id=(s, m + dm),
            device_id_type=MESH,
        )

    def up_copy(sends, receives, step, other, dm, place, offset):
        return pltpu.make_async_remote_copy(
            src_ref=sends.at[other, dm + 1, pl.ds(0, 34)],
            dst_ref=receives.at[place, offset, pl.ds(0, 34)],
            send_sem=up_ss.at[step, other, dm + 1],
            recv_sem=up_rs.at[step, place, offset],
            device_id=(other, m + dm),
            device_id_type=MESH,
        )

    def down_copy(other, dm, place, offset):
        return pltpu.make_async_remote_copy(
            src_ref=down_send.at[pl.ds(0, 34)],
            dst_ref=down.at[place, offset, pl.ds(0, 34)],
            send_sem=down_ss.at[other, dm + 1],
            recv_sem=down_rs.at[place, offset],
            device_id=(other, m + dm),
            device_id_type=MESH,
        )

    def each(low, high, do):
        def step(i, carry):
            do(i)
            return carry

        lax.fori_loop(low, high, step, 0)

    each(0, s, lambda other: meta_copy(s, 1, other, 0).start())
    for dm in (-1, 1):
        if_member(dm, lambda dm=dm: mem_copy(out_a, in_a, 0, dm, False).start())

    def start_down(other):
        for dm in (-1, 0, 1):
            if_member(dm, lambda dm=dm: down_copy(other, dm, s, 1 - dm).start())

    each(1, s, start_down)

    def side_meta(do):
        def both(other):
            for dm in (-1, 1):
                if_member(dm, lambda dm=dm: do(other, dm))

        return both

    each(1, s, side_meta(lambda other, dm: meta_copy(s, 1 - dm, other, dm).start()))

    def receive_members(faces, receives, step):
        for dm in (-1, 1):

            def take(dm=dm):
                mem_copy(out_a, receives, step, dm, True).wait_recv()
                open_message(receives.at[(1 + dm) // 2], faces, 2 + 2 * dm)

            if_member(dm, take)

    receive_members(faces_a, in_a, 0)
    each(s + 1, NSEC, lambda other: meta_copy(other, 1, s, 0).wait_recv())

    def send_up(other):
        select_quadrants(faces_a, wanted, up_send_a, other, 1, m, False)
        up_copy(up_send_a, up_a, 0, other, 0, s, 1).start()

    each(s + 1, NSEC, send_up)
    each(0, s, lambda other: up_copy(up_send_a, up_a, 0, s, 0, other, 1).wait_recv())

    def wait_down(other):
        for dm in (-1, 0, 1):
            if_member(dm, lambda dm=dm: down_copy(s, dm, other, dm + 1).wait_recv())

    above = jnp.where(s == 0, NSEC, s + 1)
    each(above, NSEC, wait_down)

    def second_part(b, carry):
        build_halo(faces_a, up_a, down, halo, b, nbr, link, wanted_own, level, own, m, False)
        stream(star, halo, middle, b, own >= 1, False)
        return carry

    lax.fori_loop(0, 2, second_part, 0)

    def third_part(b, carry):
        collide(middle, mask_ref, star, b, rate, own == 2, False)
        export(star, faces_b, out_b, b)
        return carry

    lax.fori_loop(0, 2, third_part, 0)
    for dm in (-1, 1):
        if_member(dm, lambda dm=dm: mem_copy(out_b, in_b, 1, dm, False).start())
    each(above, NSEC, side_meta(lambda other, dm: meta_copy(other, dm + 1, s, dm).wait_recv()))

    def send_direct(other):
        for dm in (-1, 0, 1):

            def send(dm=dm):
                select_quadrants(faces_b, wanted, up_send_b, other, dm + 1, m, True)
                up_copy(up_send_b, up_b, 1, other, dm, s, 1 - dm).start()

            if_member(dm, send)

    each(above, NSEC, send_direct)
    receive_members(faces_b, in_b, 1)

    def wait_direct(other):
        for dm in (-1, 0, 1):
            if_member(
                dm, lambda dm=dm: up_copy(up_send_b, up_b, 1, s, dm, other, dm + 1).wait_recv()
            )

    each(1, s, wait_direct)

    def fourth_part(b, carry):
        build_halo(faces_b, up_b, None, halo, b, nbr, link, wanted_own, level, own, m, True)
        stream(star, halo, out, b, own == 2, True)
        return carry

    lax.fori_loop(0, 2, fourth_part, 0)

    each(0, s, lambda other: meta_copy(s, 1, other, 0).wait_send())
    each(1, s, side_meta(lambda other, dm: meta_copy(s, 1 - dm, other, dm).wait_send()))
    for dm in (-1, 1):
        if_member(dm, lambda dm=dm: mem_copy(out_a, in_a, 0, dm, False).wait_send())
        if_member(dm, lambda dm=dm: mem_copy(out_b, in_b, 1, dm, False).wait_send())

    def end_down(other):
        for dm in (-1, 0, 1):
            if_member(dm, lambda dm=dm: down_copy(other, dm, s, 1 - dm).wait_send())

    each(1, s, end_down)
    each(s + 1, NSEC, lambda other: up_copy(up_send_a, up_a, 0, other, 0, s, 1).wait_send())

    def end_direct(other):
        for dm in (-1, 0, 1):
            if_member(
                dm, lambda dm=dm: up_copy(up_send_b, up_b, 1, other, dm, s, 1 - dm).wait_send()
            )

    each(above, NSEC, end_direct)


def body(populations, fluid_mask, section_level, neighbours, interface):
    state = pltpu.VMEM((2, 19, 16, 256), F32)
    faces = pltpu.VMEM((6, 3, 4, 8, 128), F32)
    ups = pltpu.VMEM((NSEC, 3, 40, 128), F32)
    members = pltpu.VMEM((2, 60, 128), F32)
    arrived = pltpu.VMEM((2, 2, 60, 128), F32)
    vmem = pl.BlockSpec(memory_space=pltpu.VMEM)
    hbm = pl.BlockSpec(memory_space=pltpu.HBM)
    dma = pltpu.SemaphoreType.DMA
    out = pl.pallas_call(
        kernel,
        out_shape=jax.ShapeDtypeStruct((19, 64, 128), F32),
        in_specs=[hbm] * 5,
        out_specs=vmem,
        scratch_shapes=[
            pltpu.VMEM((19, 64, 128), F32),
            pltpu.VMEM((64, 128), jnp.int32),
            pltpu.SMEM((NSEC,), jnp.int32),
            pltpu.SMEM((2, 18), jnp.int32),
            pltpu.SMEM((2, 4, 6), jnp.int32),
            dma((5,)),
            state,
            state,
            faces,
            faces,
            members,
            members,
            arrived,
            arrived,
            ups,
            ups,
            ups,
            ups,
            pltpu.VMEM((40, 128), F32),
            ups,
            pltpu.VMEM((3, 16, 256), F32),
            pltpu.SMEM((12,), jnp.int32),
            pltpu.SMEM((NSEC, 3, 12), jnp.int32),
            dma((NSEC, 3)),
            dma((NSEC, 3)),
            dma((2, 2)),
            dma((2, 2)),
            dma((2, NSEC, 3)),
            dma((2, NSEC, 3)),
            dma((NSEC, 3)),
            dma((NSEC, 3)),
        ],
        compiler_params=pltpu.CompilerParams(
            collective_id=0, has_side_effects=True, vmem_limit_bytes=62 * 1024 * 1024
        ),
        name="lattice_step",
    )(
        populations.reshape(2, 19, 32, 128).transpose(1, 2, 0, 3).reshape(19, 64, 128),
        fluid_mask.reshape(2, 32, 128).transpose(1, 0, 2).reshape(64, 128),
        section_level,
        neighbours,
        interface.transpose(0, 2, 1),
    )
    return out.reshape(19, 32, 2, 128).transpose(2, 0, 1, 3).reshape(2, 19, 4096)


def solution(mesh):
    return jax.shard_map(
        body,
        mesh=mesh,
        in_specs=(
            P(("section", "member"), None, None),
            P(("section", "member"), None),
            P(),
            P(("section", "member"), None),
            P(("section", "member"), None, None),
        ),
        out_specs=P(("section", "member"), None, None),
        check_vma=False,
    )
```

```python
import jax
import jax.numpy as jnp
from jax import lax
from jax.experimental import pallas as pl
from jax.experimental.pallas import tpu as pltpu
from jax.sharding import PartitionSpec as P

MESH = pl.DeviceIdType.MESH
F32 = jnp.float32
NSEC = 8
NMEM = 32

VELOCITIES = (
    (0, 0, 0),
    (1, 0, 0),
    (-1, 0, 0),
    (0, 1, 0),
    (0, -1, 0),
    (0, 0, 1),
    (0, 0, -1),
    (1, 1, 0),
    (-1, -1, 0),
    (1, -1, 0),
    (-1, 1, 0),
    (1, 0, 1),
    (-1, 0, -1),
    (1, 0, -1),
    (-1, 0, 1),
    (0, 1, 1),
    (0, -1, -1),
    (0, 1, -1),
    (0, -1, 1),
)
OPPOSITE = (0, 2, 1, 4, 3, 6, 5, 8, 7, 10, 9, 12, 11, 14, 13, 16, 15, 18, 17)
SIDE_LISTS = tuple(
    tuple(tuple(q for q in range(19) if VELOCITIES[q][axis] == sign) for sign in (1, -1))
    for axis in range(3)
)


def side_of(q, axis):
    side = 0 if VELOCITIES[q][axis] > 0 else 1
    return side, SIDE_LISTS[axis][side].index(q)


def iotas(shape=(8, 128)):
    return lax.broadcasted_iota(jnp.int32, shape, 0), lax.broadcasted_iota(jnp.int32, shape, 1)


def lanes_from(x, index):
    return jnp.take_along_axis(x, index, axis=1)


def rows_from(x, index):
    return jnp.take_along_axis(x, index, axis=0)


def pick(cond, a, b):
    return lax.select(cond, a, b)


def tile_slices(axis, tile):
    first, second = 8 * (tile // 2), 128 * (tile % 2)
    return slice(first, first + 8), slice(second, second + 128)


def packing(count):
    packed = -(-count * 5 // 8)
    spare = [(d, g) for d in range(packed) for g in (5, 6, 7)]
    runs = []
    for source in range(packed, count):
        for group in range(5):
            d, g = spare.pop(0)
            last = runs[-1] if runs else None
            if last and last[0] == source and last[2] == d and last[3] + last[4] == g:
                runs[-1] = last[:4] + (last[4] + 1,)
            else:
                runs.append((source, group, d, g, 1))
    return packed, runs


def lane_roll(x, shift):
    shift %= 128
    return pltpu.roll(x, shift, 1) if shift else x


def pack(tiles):
    lane = iotas()[1]
    packed, runs = packing(len(tiles))
    result = list(tiles[:packed])
    for source, group, d, g, length in runs:
        moved = lane_roll(tiles[source], 16 * (g - group))
        inside = (lane >= 16 * g) & (lane < 16 * (g + length))
        result[d] = jnp.where(inside, moved, result[d])
    return result


def unpack(load, source, count):
    lane = iotas()[1]
    packed, runs = packing(count)
    if source < packed:
        return load(source)
    result = None
    for which, group, d, g, length in runs:
        if which == source:
            moved = lane_roll(load(d), 16 * (group - g))
            result = moved if result is None else jnp.where(lane >= 16 * group, moved, result)
    return result


def store_message(tiles, put):
    for d, t in enumerate(pack([tiles[1], tiles[2], tiles[4], tiles[5]])):
        put(8 * d, t)
    for b in range(2):
        put(24 + 5 * b, tiles[3 * b][0:5])


def message_tile(load, axis, block):
    if axis == 0:
        pair = load(24), load(29)
    else:
        pair = tuple(unpack(lambda d: load(8 * d), 2 * b + axis - 1, 4) for b in range(2))
    return pick(block == 0, pair[0], pair[1])


def face_order(lane):
    return (lane % 8) * 16 + lane // 8 % 2 * 8 + lane // 16


def woven(b, tile):
    return pl.ds(32 * (tile // 2) + 2 * (tile % 2) + b, 8, stride=4)


def collide(cur, mask_ref, star, b, rate, advances, first):
    for tile in range(4):
        rows, lanes = tile_slices(0, tile)
        if first:
            f = [cur[q, woven(b, tile), :] for q in range(19)]
        else:
            f = [cur[b, q, rows, lanes] for q in range(19)]
        density = f[0]
        for q in range(1, 19):
            density = density + f[q]
        velocity = []
        for axis in range(3):
            plus, minus = SIDE_LISTS[axis]
            momentum = f[plus[0]] - f[minus[0]]
            for i in range(1, 5):
                momentum = momentum + f[plus[i]]
            for i in range(1, 5):
                momentum = momentum - f[minus[i]]
            velocity.append(momentum / density)
        base = 1.0 - 1.5 * (
            velocity[0] * velocity[0] + velocity[1] * velocity[1] + velocity[2] * velocity[2]
        )
        fluid = mask_ref[woven(b, tile), :] == 1
        keep = 1.0 - rate
        scaled = rate * density

        def put(q, relaxed):
            star[b, q, rows, lanes] = pick(
                advances, jnp.where(fluid, relaxed, f[OPPOSITE[q]]), f[q]
            )

        put(0, keep * f[0] + scaled * (1.0 / 3.0) * base)
        axis_weight = scaled * (1.0 / 18.0)
        edge_weight = scaled * (1.0 / 36.0)
        for q in range(1, 19, 2):
            c = VELOCITIES[q]
            along = None
            for axis in range(3):
                if c[axis]:
                    term = velocity[axis] if c[axis] > 0 else -velocity[axis]
                    along = term if along is None else along + term
            weight = axis_weight if q < 7 else edge_weight
            even = weight * (base + 4.5 * along * along)
            odd = weight * (3.0 * along)
            put(q, keep * f[q] + (even + odd))
            put(q + 1, keep * f[q + 1] + (even - odd))


def export(star, faces, message, b):
    row, lane = iotas()
    group, within = lane // 16, lane % 16
    for side in range(2):
        for p, q in enumerate(SIDE_LISTS[0][side]):
            layer = 15 if side == 0 else 0
            for half in range(2):
                line = star[b, q, layer : layer + 1, 128 * half : 128 * half + 128]
                place = side * 2 + half
                faces[(2 + b) * 12 + place, p : p + 1, :] = line
                message[b, 40 + 5 * place + p : 41 + 5 * place + p, :] = line
    zero = jnp.zeros((8, 128), F32)
    tiles = [None] * 8
    order = face_order(lane)
    for a in range(2):
        for side in range(2):
            total = zero
            for p, q in enumerate(SIDE_LISTS[1][side]):
                half = 1 - side
                x = star[b, q, 8 * a : 8 * a + 8, 128 * half : 128 * half + 128]
                shift = (16 * p + 16 if side == 0 else 16 * p) % 128
                x = pltpu.roll(x, shift, 1) if shift else x
                total = jnp.where(group == p, x, total)
            tiles[a * 2 + side] = total
        for half in range(2):
            total = zero
            for side in range(2):
                for p, q in enumerate(SIDE_LISTS[2][side]):
                    x = star[b, q, 8 * a : 8 * a + 8, 128 * half : 128 * half + 128]
                    shift = 113 + p if side == 0 else 8 + p
                    x = pltpu.roll(x, shift, 1)
                    total = jnp.where(within == side * 8 + p, x, total)
            tiles[4 + a * 2 + half] = lanes_from(total, order)
    for i, t in enumerate(tiles):
        faces[(2 + b) * 12 + 4 + i] = t
    for d, t in enumerate(pack(tiles)):
        message[b, 8 * d : 8 * d + 8, :] = t


def open_message(message, faces, place):
    def one(b, carry):
        for i in range(8):
            faces[(place + b) * 12 + 4 + i] = unpack(
                lambda d: message[b, 8 * d : 8 * d + 8, :], i, 8
            )
        for tile in range(4):
            faces[(place + b) * 12 + tile, 0:5, :] = message[b, 40 + 5 * tile : 45 + 5 * tile, :]
        return carry

    lax.fori_loop(0, 2, one, 0)


def restrict(faces, down):
    tiles = [t for b in range(2) for t in restrict_block(faces, b)]

    def put(row, t):
        down[row : row + t.shape[0], :] = t

    store_message(tiles, put)


def restrict_block(faces, b):
    row, lane = iotas()
    group, within, low = lane // 16, lane % 16, lane % 8
    second = (lane // 8) % 2
    fine = group * 16 + 2 * low
    coarse = (2 * (group % 4)) * 16
    pair_rows = 2 * (row % 4)
    parts = []
    for side in range(2):
        halves = []
        for half in range(2):
            t = faces[(2 + b) * 12 + side * 2 + half]
            t = t + pltpu.roll(t, 127, 1)
            t = t + pltpu.roll(t, 112, 1)
            halves.append(lanes_from(t, coarse + 2 * low))
        parts.append(jnp.where(group < 4, halves[0], halves[1]))
    tiles = [0.25 * jnp.where(second == 0, parts[0], parts[1])]
    parts = []
    for side in range(2):
        rows = []
        for a in range(2):
            t = faces[(2 + b) * 12 + 4 + a * 2 + side]
            t = t + pltpu.roll(t, 127, 1)
            t = t + pltpu.roll(t, 7, 0)
            rows.append(rows_from(lanes_from(t, fine), pair_rows))
        parts.append(jnp.where(row < 4, rows[0], rows[1]))
    tiles.append(0.25 * jnp.where(second == 0, parts[0], parts[1]))
    rows = []
    for a in range(2):
        halves = []
        for half in range(2):
            t = faces[(2 + b) * 12 + 8 + a * 2 + half]
            t = t + pltpu.roll(t, 127, 1)
            halves.append(lanes_from(t, group * 16 + second * 8 + 2 * (low % 4)))
        t = jnp.where(low < 4, halves[0], halves[1])
        t = t + pltpu.roll(t, 7, 0)
        rows.append(rows_from(t, pair_rows))
    tiles.append(0.25 * jnp.where(row < 4, rows[0], rows[1]))
    return tiles


def member_offset(block, member):
    return jnp.clip(((block >> 1) & (NMEM - 1)) - member + 1, 0, 2)


def slot_of(block, member):
    return member_offset(block, member) * 2 + (block & 1)


NEAR, STATE, UP_SAME, UP_DIRECT, DOWN, DOWN_BLOCK, EDGE, EDGE_THERE, TABLE = (
    0,
    6,
    12,
    18,
    24,
    48,
    72,
    84,
    96,
)


def read_links(nbr, link, level, own, member, wanted, table, b):
    section_shift = NMEM.bit_length()
    for axis in range(3):
        for side in range(2):
            i, j = axis * 2 + side, axis * 2 + 1 - side
            code = jnp.int32(-1)
            for k in range(4):
                block = link[b, k, j]
                code = jnp.maximum(code, jnp.where(block >= 0, block * 4 + k, -1))
                safe = jnp.maximum(block, 0)
                place = (safe >> section_shift) * 3 + member_offset(safe, member)
                table[b * TABLE + DOWN + i * 4 + k] = place
                table[b * TABLE + DOWN_BLOCK + i * 4 + k] = jnp.where(block >= 0, safe & 1, -1)
            safe = jnp.maximum(code, 0)
            k, block = safe & 3, safe >> 2
            section = block >> section_shift
            first, last = k >> 1, k & 1
            if axis == 0:
                tile = side * 2 + first
            elif axis == 1:
                tile = 4 + first * 2 + side
            else:
                tile = 8 + k
            wanted[b * 6 + i] = slot_of(block, member) * 12 + tile
            wanted[12 + b * 6 + i] = (2 + (block & 1)) * 12 + tile
            wanted[24 + b * 6 + i] = last
            near = nbr[b, j]
            table[b * TABLE + NEAR + i] = slot_of(jnp.maximum(near, 0), member) * 12
            linked = jnp.where(code < 0, 3, jnp.where(level[section] < own, 1, 2))
            table[b * TABLE + STATE + i] = jnp.where(near >= 0, 0, linked)
            table[b * TABLE + UP_SAME + i] = section * 3 + 1
            table[b * TABLE + UP_DIRECT + i] = section * 3 + member_offset(block, member)
    for q in range(7, 19):
        block = nbr[b, OPPOSITE[q] - 1]
        table[b * TABLE + EDGE + q - 7] = slot_of(jnp.maximum(block, 0), member) * 12
        table[b * TABLE + EDGE_THERE + q - 7] = block


def select_quadrants(faces, wanted, out, other, asker, direct):
    lane = iotas()[1]
    second = (lane // 8) % 2
    tiles = []
    for b in range(2):
        for axis in range(3):
            parts = []
            for side in range(2):
                i = b * 6 + axis * 2 + side
                t = faces[wanted[other, asker, (12 if direct else 0) + i]]
                if axis < 2:
                    in_place = wanted[other, asker, 24 + i] == side
                    t = pick(in_place, t, pltpu.roll(t, 8 if side else 120, 1))
                parts.append(t)
            tiles.append(jnp.where(second == 0, parts[0], parts[1]))

    def put(row, t):
        out[other, asker, row : row + t.shape[0], :] = t

    store_message(tiles, put)


def build_halo(faces, up, down, halo, b, table, direct):
    row, lane = iotas()
    group, within, low = lane // 16, lane % 16, lane % 8
    second = (lane // 8) % 2
    spread_rows = [4 * a + row // 2 for a in range(2)]

    def entry(place):
        return table[b * TABLE + place]

    def means(axis, i, k):
        place, block = entry(DOWN + i * 4 + k), entry(DOWN_BLOCK + i * 4 + k)
        t = message_tile(lambda row: down[place, row : row + 8, :], axis, block)
        return pick(block >= 0, t, jnp.zeros_like(t))

    for axis in range(3):
        states, near, quads, ups = [], [], [], []
        for side in range(2):
            i = axis * 2 + side
            states.append(entry(STATE + i))
            near.append(entry(NEAR + i) + axis * 4)
            place = entry((UP_DIRECT if direct else UP_SAME) + i)
            ups.append(
                message_tile(lambda row, place=place: up[place, row : row + 8, :], axis, b)
            )
            if down is not None:
                quads.append([means(axis, i, k) for k in range(4)])
        if axis == 0:
            rest = jnp.where(row == 0, F32(1.0 / 18.0), F32(1.0 / 36.0))
        else:
            rest = jnp.where(group == 0, F32(1.0 / 18.0), F32(1.0 / 36.0))

        def choose(side, tile, from_up, from_down):
            state = states[side]
            far = rest if from_down is None else pick(state == 2, from_down, rest)
            far = pick(state == 1, from_up, far)
            return pick(state == 0, faces[near[side] + tile], far)

        if axis < 2:
            for side in range(2):
                if axis == 1:
                    wide = lanes_from(ups[side], group * 16 + side * 8 + within // 2)
                for a in range(2):
                    if axis == 0:
                        tile = side * 2 + a
                        from_up = lanes_from(
                            ups[side], (4 * a + group // 2) * 16 + side * 8 + within // 2
                        )
                    else:
                        tile = a * 2 + side
                        from_up = rows_from(wide, spread_rows[a])
                    from_down = None
                    if down is not None:
                        low_part, high_part = quads[side][2 * a], quads[side][2 * a + 1]
                        if side:
                            low_part = pltpu.roll(low_part, 120, 1)
                        else:
                            high_part = pltpu.roll(high_part, 8, 1)
                        from_down = jnp.where(second == 0, low_part, high_part)
                    rows, lanes = tile_slices(axis, tile)
                    halo[axis, rows, lanes] = choose(side, tile, from_up, from_down)
        else:
            both = jnp.where(second == 0, ups[0], ups[1])
            for half in range(2):
                wide = lanes_from(both, group * 16 + second * 8 + 4 * half + low // 2)
                for a in range(2):
                    tile = a * 2 + half
                    from_up = rows_from(wide, spread_rows[a])
                    parts = [
                        choose(side, tile, from_up, quads[side][tile] if down is not None else None)
                        for side in range(2)
                    ]
                    rows, lanes = tile_slices(axis, tile)
                    halo[axis, rows, lanes] = jnp.where(second == 0, parts[0], parts[1])

    for q in range(7, 19):
        c = VELOCITIES[q]
        one, two = [axis for axis in range(3) if c[axis]]
        side, p = side_of(q, two)
        near, there = entry(EDGE + q - 7) + two * 4, entry(EDGE_THERE + q - 7) >= 0
        far_end = c[one] > 0
        if two == 1:
            tiles = [(1 if far_end else 0) * 2 + side]
            where = (row == (7 if far_end else 0)) & (group == p)
        elif one == 0:
            tiles = [(1 if far_end else 0) * 2 + half for half in range(2)]
            where = (row == (7 if far_end else 0)) & (group == p) & (second == side)
        else:
            tiles = [a * 2 + (1 if far_end else 0) for a in range(2)]
            where = lane == p * 16 + side * 8 + (7 if far_end else 0)
        for tile in tiles:
            rows, lanes = tile_slices(two, tile)
            line = faces[near + tile]
            line = pick(there, line, jnp.full_like(line, 1.0 / 36.0))
            halo[two, rows, lanes] = jnp.where(where, line, halo[two, rows, lanes])
    order = face_order(lane)
    for tile in range(4):
        rows, lanes = tile_slices(2, tile)
        halo[2, rows, lanes] = lanes_from(halo[2, rows, lanes], order)


def stream(star, halo, out, b, advances, final):
    row, lane = iotas((16, 128))
    within = lane % 16
    first, last = lane < 16, lane >= 112

    def roll(x, shift, axis):
        shift %= x.shape[axis]
        return pltpu.roll(x, shift, axis) if shift else x

    def ring(left, right, sign):
        a, c = roll(left, 16 * sign, 1), roll(right, 16 * sign, 1)
        if sign > 0:
            return jnp.where(first, c, a), jnp.where(first, a, c)
        return jnp.where(last, c, a), jnp.where(last, a, c)

    for q in range(19):
        c = VELOCITIES[q]
        old = [star[b, q, :, 128 * half : 128 * half + 128] for half in range(2)]
        new = list(old)
        if c[0]:
            side, p = side_of(q, 0)
            place = side * 8 + p
            for half in range(2):
                plane = halo[0, place : place + 1, 128 * half : 128 * half + 128]
                moved = roll(new[half], c[0], 0)
                new[half] = jnp.where(row == (0 if c[0] > 0 else 15), plane, moved)
        if c[1]:
            side, p = side_of(q, 1)
            border = halo[1, :, 128 * side : 128 * side + 128]
            border = roll(border, -16 * p if side == 0 else 112 - 16 * p, 1)
            if c[0]:
                border = roll(border, c[0], 0)
            a, d = roll(new[0], 16 * c[1], 1), roll(new[1], 16 * c[1], 1)
            if c[1] > 0:
                new = [jnp.where(first, border, a), jnp.where(first, a, d)]
            else:
                new = [jnp.where(last, d, a), jnp.where(last, border, d)]
        if c[2]:
            side, p = side_of(q, 2)
            borders = []
            for half in range(2):
                border = halo[2, :, 128 * half : 128 * half + 128]
                border = roll(border, -p if side == 0 else 7 - p, 1)
                if c[0]:
                    border = roll(border, c[0], 0)
                borders.append(border)
            if c[1]:
                borders = ring(borders[0], borders[1], c[1])
            for half in range(2):
                new[half] = jnp.where(
                    within == (0 if c[2] > 0 else 15), borders[half], roll(new[half], c[2], 1)
                )
        for half in range(2):
            result = pick(advances, new[half], old[half])
            if final:
                for a in range(2):
                    out[q, woven(b, 2 * a + half), :] = result[8 * a : 8 * a + 8]
            else:
                out[b, q, :, 128 * half : 128 * half + 128] = result


def kernel(
    pop_hbm,
    mask_hbm,
    level_hbm,
    nbr_hbm,
    link_hbm,
    out,
    pop,
    mask_ref,
    level,
    nbr,
    link,
    in_sems,
    star,
    middle,
    faces_a,
    faces_b,
    out_a,
    out_b,
    in_a,
    in_b,
    up_send_a,
    up_send_b,
    up_a,
    up_b,
    down_send,
    down,
    halo,
    table,
    wanted_own,
    wanted,
    meta_ss,
    meta_rs,
    mem_ss,
    mem_rs,
    up_ss,
    up_rs,
    down_ss,
    down_rs,
):
    s = lax.axis_index("section")
    m = lax.axis_index("member")
    loads = [
        pltpu.make_async_copy(src, dst, in_sems.at[i])
        for i, (src, dst) in enumerate(
            [
                (level_hbm, level),
                (link_hbm, link),
                (nbr_hbm, nbr),
                (pop_hbm, pop),
                (mask_hbm, mask_ref),
            ]
        )
    ]
    for load in loads:
        load.start()
    has = {-1: m > 0, 0: None, 1: m < NMEM - 1}

    def if_member(dm, do):
        if has[dm] is None:
            do()
        else:
            pl.when(has[dm])(do)

    barrier = pltpu.get_barrier_semaphore()

    def greet(other, dm):
        pl.semaphore_signal(barrier, inc=1, device_id=(other, m + dm), device_id_type=MESH)

    def greet_section(other, carry):
        @pl.when(other != s)
        def _():
            greet(other, 0)

        for dm in (-1, 1):
            if_member(dm, lambda dm=dm: greet(other, dm))
        return carry

    lax.fori_loop(0, NSEC, greet_section, 0)
    for load in loads:
        load.wait()
    own = level[s]
    rate = jnp.where(
        own == 0, F32(1.0 / 0.55), jnp.where(own == 1, F32(1.0 / 0.6), F32(1.0 / 0.7))
    )

    def first_part(b, carry):
        collide(pop, mask_ref, star, b, rate, own >= 1, True)
        export(star, faces_a, out_a, b)
        return carry

    lax.fori_loop(0, 2, first_part, 0)
    restrict(faces_a, down_send)

    def read(b, carry):
        read_links(nbr, link, level, own, m, wanted_own, table, b)
        return carry

    lax.fori_loop(0, 2, read, 0)

    one = jnp.int32(1)
    there = jnp.where(m > 0, one, 0) + jnp.where(m < NMEM - 1, one, 0)
    pl.semaphore_wait(barrier, NSEC * (there + 1) - 1)

    def meta_copy(place, offset, other, dm):
        return pltpu.make_async_remote_copy(
            src_ref=wanted_own,
            dst_ref=wanted.at[place, offset],
            send_sem=meta_ss.at[other, dm + 1],
            recv_sem=meta_rs.at[place, offset],
            device_id=(other, m + dm),
            device_id_type=MESH,
        )

    def mem_copy(sends, receives, step, dm, arriving):
        into = (1 + dm) // 2 if arriving else (1 - dm) // 2
        return pltpu.make_async_remote_copy(
            src_ref=sends,
            dst_ref=receives.at[into],
            send_sem=mem_ss.at[step, (dm + 1) // 2],
            recv_sem=mem_rs.at[step, into],
            device_id=(s, m + dm),
            device_id_type=MESH,
        )

    def up_copy(sends, receives, step, other, dm, place, offset):
        return pltpu.make_async_remote_copy(
            src_ref=sends.at[other, dm + 1, pl.ds(0, 34)],
            dst_ref=receives.at[place * 3 + offset, pl.ds(0, 34)],
            send_sem=up_ss.at[step, other, dm + 1],
            recv_sem=up_rs.at[step, place, offset],
            device_id=(other, m + dm),
            device_id_type=MESH,
        )

    def down_copy(other, dm, place, offset):
        return pltpu.make_async_remote_copy(
            src_ref=down_send.at[pl.ds(0, 34)],
            dst_ref=down.at[place * 3 + offset, pl.ds(0, 34)],
            send_sem=down_ss.at[other, dm + 1],
            recv_sem=down_rs.at[place, offset],
            device_id=(other, m + dm),
            device_id_type=MESH,
        )

    def each(low, high, do):
        def step(i, carry):
            do(i)
            return carry

        lax.fori_loop(low, high, step, 0)

    each(0, s, lambda other: meta_copy(s, 1, other, 0).start())
    for dm in (-1, 1):
        if_member(dm, lambda dm=dm: mem_copy(out_a, in_a, 0, dm, False).start())

    def start_down(other):
        for dm in (-1, 0, 1):
            if_member(dm, lambda dm=dm: down_copy(other, dm, s, 1 - dm).start())

    each(1, s, start_down)

    def side_meta(do):
        def both(other):
            for dm in (-1, 1):
                if_member(dm, lambda dm=dm: do(other, dm))

        return both

    each(1, s, side_meta(lambda other, dm: meta_copy(s, 1 - dm, other, dm).start()))

    def receive_members(faces, receives, step):
        for dm in (-1, 1):

            def take(dm=dm):
                mem_copy(out_a, receives, step, dm, True).wait_recv()
                open_message(receives.at[(1 + dm) // 2], faces, 2 + 2 * dm)

            if_member(dm, take)

    receive_members(faces_a, in_a, 0)
    each(s + 1, NSEC, lambda other: meta_copy(other, 1, s, 0).wait_recv())

    def send_up(other):
        select_quadrants(faces_a, wanted, up_send_a, other, 1, False)
        up_copy(up_send_a, up_a, 0, other, 0, s, 1).start()

    each(s + 1, NSEC, send_up)
    each(0, s, lambda other: up_copy(up_send_a, up_a, 0, s, 0, other, 1).wait_recv())

    def wait_down(other):
        for dm in (-1, 0, 1):
            if_member(dm, lambda dm=dm: down_copy(s, dm, other, dm + 1).wait_recv())

    above = jnp.where(s == 0, NSEC, s + 1)
    each(above, NSEC, wait_down)

    def second_part(b, carry):
        build_halo(faces_a, up_a, down, halo, b, table, False)
        stream(star, halo, middle, b, own >= 1, False)
        return carry

    lax.fori_loop(0, 2, second_part, 0)

    def third_part(b, carry):
        collide(middle, mask_ref, star, b, rate, own == 2, False)
        export(star, faces_b, out_b, b)
        return carry

    lax.fori_loop(0, 2, third_part, 0)
    for dm in (-1, 1):
        if_member(dm, lambda dm=dm: mem_copy(out_b, in_b, 1, dm, False).start())
    each(above, NSEC, side_meta(lambda other, dm: meta_copy(other, dm + 1, s, dm).wait_recv()))

    def send_direct(other):
        for dm in (-1, 0, 1):

            def send(dm=dm):
                select_quadrants(faces_b, wanted, up_send_b, other, dm + 1, True)
                up_copy(up_send_b, up_b, 1, other, dm, s, 1 - dm).start()

            if_member(dm, send)

    each(above, NSEC, send_direct)
    receive_members(faces_b, in_b, 1)

    def wait_direct(other):
        for dm in (-1, 0, 1):
            if_member(
                dm, lambda dm=dm: up_copy(up_send_b, up_b, 1, s, dm, other, dm + 1).wait_recv()
            )

    each(0, s, lambda other: meta_copy(s, 1, other, 0).wait_send())
    each(1, s, side_meta(lambda other, dm: meta_copy(s, 1 - dm, other, dm).wait_send()))
    for dm in (-1, 1):
        if_member(dm, lambda dm=dm: mem_copy(out_a, in_a, 0, dm, False).wait_send())
        if_member(dm, lambda dm=dm: mem_copy(out_b, in_b, 1, dm, False).wait_send())

    def end_down(other):
        for dm in (-1, 0, 1):
            if_member(dm, lambda dm=dm: down_copy(other, dm, s, 1 - dm).wait_send())

    each(1, s, end_down)
    each(s + 1, NSEC, lambda other: up_copy(up_send_a, up_a, 0, other, 0, s, 1).wait_send())

    def end_direct(other):
        for dm in (-1, 0, 1):
            if_member(
                dm, lambda dm=dm: up_copy(up_send_b, up_b, 1, other, dm, s, 1 - dm).wait_send()
            )

    each(above, NSEC, end_direct)
    each(1, s, wait_direct)

    def fourth_part(b, carry):
        build_halo(faces_b, up_b, None, halo, b, table, True)
        stream(star, halo, out, b, own == 2, True)
        return carry

    lax.fori_loop(0, 2, fourth_part, 0)


def body(populations, fluid_mask, section_level, neighbours, interface):
    state = pltpu.VMEM((2, 19, 16, 256), F32)
    faces = pltpu.VMEM((72, 8, 128), F32)
    ups = pltpu.VMEM((NSEC, 3, 40, 128), F32)
    came = pltpu.VMEM((NSEC * 3, 40, 128), F32)
    members = pltpu.VMEM((2, 60, 128), F32)
    arrived = pltpu.VMEM((2, 2, 60, 128), F32)
    vmem = pl.BlockSpec(memory_space=pltpu.VMEM)
    hbm = pl.BlockSpec(memory_space=pltpu.HBM)
    dma = pltpu.SemaphoreType.DMA
    out = pl.pallas_call(
        kernel,
        out_shape=jax.ShapeDtypeStruct((19, 64, 128), F32),
        in_specs=[hbm] * 5,
        out_specs=vmem,
        scratch_shapes=[
            pltpu.VMEM((19, 64, 128), F32),
            pltpu.VMEM((64, 128), jnp.int32),
            pltpu.SMEM((NSEC,), jnp.int32),
            pltpu.SMEM((2, 18), jnp.int32),
            pltpu.SMEM((2, 4, 6), jnp.int32),
            dma((5,)),
            state,
            state,
            faces,
            faces,
            members,
            members,
            arrived,
            arrived,
            ups,
            ups,
            came,
            came,
            pltpu.VMEM((40, 128), F32),
            came,
            pltpu.VMEM((3, 16, 256), F32),
            pltpu.SMEM((2 * TABLE,), jnp.int32),
            pltpu.SMEM((36,), jnp.int32),
            pltpu.SMEM((NSEC, 3, 36), jnp.int32),
            dma((NSEC, 3)),
            dma((NSEC, 3)),
            dma((2, 2)),
            dma((2, 2)),
            dma((2, NSEC, 3)),
            dma((2, NSEC, 3)),
            dma((NSEC, 3)),
            dma((NSEC, 3)),
        ],
        compiler_params=pltpu.CompilerParams(
            collective_id=0, has_side_effects=True, vmem_limit_bytes=62 * 1024 * 1024
        ),
        name="lattice_step",
    )(
        populations.reshape(2, 19, 32, 128).transpose(1, 2, 0, 3).reshape(19, 64, 128),
        fluid_mask.reshape(2, 32, 128).transpose(1, 0, 2).reshape(64, 128),
        section_level,
        neighbours,
        interface.transpose(0, 2, 1),
    )
    return out.reshape(19, 32, 2, 128).transpose(2, 0, 1, 3).reshape(2, 19, 4096)


def solution(mesh):
    return jax.shard_map(
        body,
        mesh=mesh,
        in_specs=(
            P(("section", "member"), None, None),
            P(("section", "member"), None),
            P(),
            P(("section", "member"), None),
            P(("section", "member"), None, None),
        ),
        out_specs=P(("section", "member"), None, None),
        check_vma=False,
    )
```

```python
import jax
import jax.numpy as jnp
from jax import lax
from jax.experimental import pallas as pl
from jax.experimental.pallas import tpu as pltpu
from jax.sharding import PartitionSpec as P

MESH = pl.DeviceIdType.MESH
F32 = jnp.float32
NSEC = 8
NMEM = 32

VELOCITIES = (
    (0, 0, 0),
    (1, 0, 0),
    (-1, 0, 0),
    (0, 1, 0),
    (0, -1, 0),
    (0, 0, 1),
    (0, 0, -1),
    (1, 1, 0),
    (-1, -1, 0),
    (1, -1, 0),
    (-1, 1, 0),
    (1, 0, 1),
    (-1, 0, -1),
    (1, 0, -1),
    (-1, 0, 1),
    (0, 1, 1),
    (0, -1, -1),
    (0, 1, -1),
    (0, -1, 1),
)
OPPOSITE = (0, 2, 1, 4, 3, 6, 5, 8, 7, 10, 9, 12, 11, 14, 13, 16, 15, 18, 17)
SIDE_LISTS = tuple(
    tuple(tuple(q for q in range(19) if VELOCITIES[q][axis] == sign) for sign in (1, -1))
    for axis in range(3)
)


def side_of(q, axis):
    side = 0 if VELOCITIES[q][axis] > 0 else 1
    return side, SIDE_LISTS[axis][side].index(q)


def iotas(shape=(8, 128)):
    return lax.broadcasted_iota(jnp.int32, shape, 0), lax.broadcasted_iota(jnp.int32, shape, 1)


def lanes_from(x, index):
    return jnp.take_along_axis(x, index, axis=1)


def rows_from(x, index):
    return jnp.take_along_axis(x, index, axis=0)


def pick(cond, a, b):
    return lax.select(cond, a, b)


def tile_slices(axis, tile):
    first, second = 8 * (tile // 2), 128 * (tile % 2)
    return slice(first, first + 8), slice(second, second + 128)


def packing(count):
    packed = -(-count * 5 // 8)
    spare = [(d, g) for d in range(packed) for g in (5, 6, 7)]
    runs = []
    for source in range(packed, count):
        for group in range(5):
            d, g = spare.pop(0)
            last = runs[-1] if runs else None
            if last and last[0] == source and last[2] == d and last[3] + last[4] == g:
                runs[-1] = last[:4] + (last[4] + 1,)
            else:
                runs.append((source, group, d, g, 1))
    return packed, runs


def lane_roll(x, shift):
    shift %= 128
    return pltpu.roll(x, shift, 1) if shift else x


def pack(tiles):
    lane = iotas()[1]
    packed, runs = packing(len(tiles))
    result = list(tiles[:packed])
    for source, group, d, g, length in runs:
        moved = lane_roll(tiles[source], 16 * (g - group))
        inside = (lane >= 16 * g) & (lane < 16 * (g + length))
        result[d] = jnp.where(inside, moved, result[d])
    return result


def unpack(load, source, count):
    lane = iotas()[1]
    packed, runs = packing(count)
    if source < packed:
        return load(source)
    result = None
    for which, group, d, g, length in runs:
        if which == source:
            moved = lane_roll(load(d), 16 * (group - g))
            result = moved if result is None else jnp.where(lane >= 16 * group, moved, result)
    return result


def store_message(tiles, put):
    for d, t in enumerate(pack([tiles[1], tiles[2], tiles[4], tiles[5]])):
        put(8 * d, t)
    for b in range(2):
        put(24 + 5 * b, tiles[3 * b][0:5])


def message_tile(load, axis, block):
    if axis == 0:
        pair = load(24), load(29)
    else:
        pair = tuple(unpack(lambda d: load(8 * d), 2 * b + axis - 1, 4) for b in range(2))
    return pick(block == 0, pair[0], pair[1])


def face_order(lane):
    return (lane % 8) * 16 + lane // 8 % 2 * 8 + lane // 16


def woven(b, tile):
    return pl.ds(32 * (tile // 2) + 2 * (tile % 2) + b, 8, stride=4)


def collide(cur, mask_ref, star, b, rate, advances, first):
    for tile in range(4):
        rows, lanes = tile_slices(0, tile)
        if first:
            f = [cur[q, woven(b, tile), :] for q in range(19)]
        else:
            f = [cur[b, q, rows, lanes] for q in range(19)]
        density = f[0]
        for q in range(1, 19):
            density = density + f[q]
        velocity = []
        for axis in range(3):
            plus, minus = SIDE_LISTS[axis]
            momentum = f[plus[0]] - f[minus[0]]
            for i in range(1, 5):
                momentum = momentum + f[plus[i]]
            for i in range(1, 5):
                momentum = momentum - f[minus[i]]
            velocity.append(momentum / density)
        base = 1.0 - 1.5 * (
            velocity[0] * velocity[0] + velocity[1] * velocity[1] + velocity[2] * velocity[2]
        )
        fluid = mask_ref[woven(b, tile), :] == 1
        keep = 1.0 - rate
        scaled = rate * density

        def put(q, relaxed):
            star[b, q, rows, lanes] = pick(
                advances, jnp.where(fluid, relaxed, f[OPPOSITE[q]]), f[q]
            )

        put(0, keep * f[0] + scaled * (1.0 / 3.0) * base)
        axis_weight = scaled * (1.0 / 18.0)
        edge_weight = scaled * (1.0 / 36.0)
        for q in range(1, 19, 2):
            c = VELOCITIES[q]
            along = None
            for axis in range(3):
                if c[axis]:
                    term = velocity[axis] if c[axis] > 0 else -velocity[axis]
                    along = term if along is None else along + term
            weight = axis_weight if q < 7 else edge_weight
            even = weight * (base + 4.5 * along * along)
            odd = weight * (3.0 * along)
            put(q, keep * f[q] + (even + odd))
            put(q + 1, keep * f[q + 1] + (even - odd))


def export(star, faces, message, b):
    row, lane = iotas()
    group, within = lane // 16, lane % 16
    for side in range(2):
        for p, q in enumerate(SIDE_LISTS[0][side]):
            layer = 15 if side == 0 else 0
            for half in range(2):
                line = star[b, q, layer : layer + 1, 128 * half : 128 * half + 128]
                place = side * 2 + half
                faces[(2 + b) * 12 + place, p : p + 1, :] = line
                message[b, 40 + 5 * place + p : 41 + 5 * place + p, :] = line
    zero = jnp.zeros((8, 128), F32)
    tiles = [None] * 8
    order = face_order(lane)
    for a in range(2):
        for side in range(2):
            total = zero
            for p, q in enumerate(SIDE_LISTS[1][side]):
                half = 1 - side
                x = star[b, q, 8 * a : 8 * a + 8, 128 * half : 128 * half + 128]
                shift = (16 * p + 16 if side == 0 else 16 * p) % 128
                x = pltpu.roll(x, shift, 1) if shift else x
                total = jnp.where(group == p, x, total)
            tiles[a * 2 + side] = total
        for half in range(2):
            total = zero
            for side in range(2):
                for p, q in enumerate(SIDE_LISTS[2][side]):
                    x = star[b, q, 8 * a : 8 * a + 8, 128 * half : 128 * half + 128]
                    shift = 113 + p if side == 0 else 8 + p
                    x = pltpu.roll(x, shift, 1)
                    total = jnp.where(within == side * 8 + p, x, total)
            tiles[4 + a * 2 + half] = lanes_from(total, order)
    for i, t in enumerate(tiles):
        faces[(2 + b) * 12 + 4 + i] = t
    for d, t in enumerate(pack(tiles)):
        message[b, 8 * d : 8 * d + 8, :] = t


def open_message(message, faces, place):
    def one(b, carry):
        for i in range(8):
            faces[(place + b) * 12 + 4 + i] = unpack(
                lambda d: message[b, 8 * d : 8 * d + 8, :], i, 8
            )
        for tile in range(4):
            faces[(place + b) * 12 + tile, 0:5, :] = message[b, 40 + 5 * tile : 45 + 5 * tile, :]
        return carry

    lax.fori_loop(0, 2, one, 0)


def restrict(faces, down):
    tiles = [t for b in range(2) for t in restrict_block(faces, b)]

    def put(row, t):
        down[row : row + t.shape[0], :] = t

    store_message(tiles, put)


def restrict_block(faces, b):
    row, lane = iotas()
    group, within, low = lane // 16, lane % 16, lane % 8
    second = (lane // 8) % 2
    fine = group * 16 + 2 * low
    coarse = (2 * (group % 4)) * 16
    pair_rows = 2 * (row % 4)
    parts = []
    for side in range(2):
        halves = []
        for half in range(2):
            t = faces[(2 + b) * 12 + side * 2 + half]
            t = t + pltpu.roll(t, 127, 1)
            t = t + pltpu.roll(t, 112, 1)
            halves.append(lanes_from(t, coarse + 2 * low))
        parts.append(jnp.where(group < 4, halves[0], halves[1]))
    tiles = [0.25 * jnp.where(second == 0, parts[0], parts[1])]
    parts = []
    for side in range(2):
        rows = []
        for a in range(2):
            t = faces[(2 + b) * 12 + 4 + a * 2 + side]
            t = t + pltpu.roll(t, 127, 1)
            t = t + pltpu.roll(t, 7, 0)
            rows.append(rows_from(lanes_from(t, fine), pair_rows))
        parts.append(jnp.where(row < 4, rows[0], rows[1]))
    tiles.append(0.25 * jnp.where(second == 0, parts[0], parts[1]))
    rows = []
    for a in range(2):
        halves = []
        for half in range(2):
            t = faces[(2 + b) * 12 + 8 + a * 2 + half]
            t = t + pltpu.roll(t, 127, 1)
            halves.append(lanes_from(t, group * 16 + second * 8 + 2 * (low % 4)))
        t = jnp.where(low < 4, halves[0], halves[1])
        t = t + pltpu.roll(t, 7, 0)
        rows.append(rows_from(t, pair_rows))
    tiles.append(0.25 * jnp.where(row < 4, rows[0], rows[1]))
    return tiles


def member_offset(block, member):
    return jnp.clip(((block >> 1) & (NMEM - 1)) - member + 1, 0, 2)


def slot_of(block, member):
    return member_offset(block, member) * 2 + (block & 1)


NEAR, STATE, UP_SAME, UP_DIRECT, DOWN, DOWN_BLOCK, EDGE, EDGE_THERE, TABLE = (
    0,
    6,
    12,
    18,
    24,
    48,
    72,
    84,
    96,
)


SECTION_SHIFT = NMEM.bit_length()


def read_wanted(link, member, wanted, table, b):
    for axis in range(3):
        for side in range(2):
            i, j = axis * 2 + side, axis * 2 + 1 - side
            code = jnp.int32(-1)
            for k in range(4):
                block = link[b, k, j]
                code = jnp.maximum(code, jnp.where(block >= 0, block * 4 + k, -1))
            table[b * TABLE + STATE + i] = code
            safe = jnp.maximum(code, 0)
            k, block = safe & 3, safe >> 2
            first, last = k >> 1, k & 1
            if axis == 0:
                tile = side * 2 + first
            elif axis == 1:
                tile = 4 + first * 2 + side
            else:
                tile = 8 + k
            wanted[b * 6 + i] = slot_of(block, member) * 12 + tile
            wanted[12 + b * 6 + i] = (2 + (block & 1)) * 12 + tile
            wanted[24 + b * 6 + i] = last


def read_links(nbr, link, level, own, member, table, b):
    for axis in range(3):
        for side in range(2):
            i, j = axis * 2 + side, axis * 2 + 1 - side
            for k in range(4):
                block = link[b, k, j]
                safe = jnp.maximum(block, 0)
                place = (safe >> SECTION_SHIFT) * 3 + member_offset(safe, member)
                table[b * TABLE + DOWN + i * 4 + k] = place
                table[b * TABLE + DOWN_BLOCK + i * 4 + k] = jnp.where(block >= 0, safe & 1, -1)
            code = table[b * TABLE + STATE + i]
            block = jnp.maximum(code, 0) >> 2
            section = block >> SECTION_SHIFT
            near = nbr[b, j]
            table[b * TABLE + NEAR + i] = slot_of(jnp.maximum(near, 0), member) * 12
            linked = jnp.where(code < 0, 3, jnp.where(level[section] < own, 1, 2))
            table[b * TABLE + STATE + i] = jnp.where(near >= 0, 0, linked)
            table[b * TABLE + UP_SAME + i] = section
            table[b * TABLE + UP_DIRECT + i] = section * 3 + member_offset(block, member)
    for q in range(7, 19):
        block = nbr[b, OPPOSITE[q] - 1]
        table[b * TABLE + EDGE + q - 7] = slot_of(jnp.maximum(block, 0), member) * 12
        table[b * TABLE + EDGE_THERE + q - 7] = block


def select_quadrants(faces, ask, out, place, direct):
    lane = iotas()[1]
    second = (lane // 8) % 2
    tiles = []
    for b in range(2):
        for axis in range(3):
            parts = []
            for side in range(2):
                i = b * 6 + axis * 2 + side
                t = faces[ask((12 if direct else 0) + i)]
                if axis < 2:
                    t = pick(ask(24 + i) == side, t, pltpu.roll(t, 8 if side else 120, 1))
                parts.append(t)
            tiles.append(jnp.where(second == 0, parts[0], parts[1]))

    def put(row, t):
        out[place, row : row + t.shape[0], :] = t

    store_message(tiles, put)


def build_halo(faces, up, down, halo, b, table, direct):
    row, lane = iotas()
    group, within, low = lane // 16, lane % 16, lane % 8
    second = (lane // 8) % 2
    spread_rows = [4 * a + row // 2 for a in range(2)]

    def entry(place):
        return table[b * TABLE + place]

    def means(axis, i, k):
        place, block = entry(DOWN + i * 4 + k), entry(DOWN_BLOCK + i * 4 + k)
        t = message_tile(lambda row: down[place, row : row + 8, :], axis, block)
        return pick(block >= 0, t, jnp.zeros_like(t))

    for axis in range(3):
        states, near, quads, ups = [], [], [], []
        for side in range(2):
            i = axis * 2 + side
            states.append(entry(STATE + i))
            near.append(entry(NEAR + i) + axis * 4)
            place = entry((UP_DIRECT if direct else UP_SAME) + i)
            ups.append(
                message_tile(lambda row, place=place: up[place, row : row + 8, :], axis, b)
            )
            if down is not None:
                quads.append([means(axis, i, k) for k in range(4)])
        if axis == 0:
            rest = jnp.where(row == 0, F32(1.0 / 18.0), F32(1.0 / 36.0))
        else:
            rest = jnp.where(group == 0, F32(1.0 / 18.0), F32(1.0 / 36.0))

        def choose(side, tile, from_up, from_down):
            state = states[side]
            far = rest if from_down is None else pick(state == 2, from_down, rest)
            far = pick(state == 1, from_up, far)
            return pick(state == 0, faces[near[side] + tile], far)

        if axis < 2:
            for side in range(2):
                if axis == 1:
                    wide = lanes_from(ups[side], group * 16 + side * 8 + within // 2)
                for a in range(2):
                    if axis == 0:
                        tile = side * 2 + a
                        from_up = lanes_from(
                            ups[side], (4 * a + group // 2) * 16 + side * 8 + within // 2
                        )
                    else:
                        tile = a * 2 + side
                        from_up = rows_from(wide, spread_rows[a])
                    from_down = None
                    if down is not None:
                        low_part, high_part = quads[side][2 * a], quads[side][2 * a + 1]
                        if side:
                            low_part = pltpu.roll(low_part, 120, 1)
                        else:
                            high_part = pltpu.roll(high_part, 8, 1)
                        from_down = jnp.where(second == 0, low_part, high_part)
                    rows, lanes = tile_slices(axis, tile)
                    halo[axis, rows, lanes] = choose(side, tile, from_up, from_down)
        else:
            both = jnp.where(second == 0, ups[0], ups[1])
            for half in range(2):
                wide = lanes_from(both, group * 16 + second * 8 + 4 * half + low // 2)
                for a in range(2):
                    tile = a * 2 + half
                    from_up = rows_from(wide, spread_rows[a])
                    parts = [
                        choose(side, tile, from_up, quads[side][tile] if down is not None else None)
                        for side in range(2)
                    ]
                    rows, lanes = tile_slices(axis, tile)
                    halo[axis, rows, lanes] = jnp.where(second == 0, parts[0], parts[1])

    for q in range(7, 19):
        c = VELOCITIES[q]
        one, two = [axis for axis in range(3) if c[axis]]
        side, p = side_of(q, two)
        near, there = entry(EDGE + q - 7) + two * 4, entry(EDGE_THERE + q - 7) >= 0
        far_end = c[one] > 0
        if two == 1:
            tiles = [(1 if far_end else 0) * 2 + side]
            where = (row == (7 if far_end else 0)) & (group == p)
        elif one == 0:
            tiles = [(1 if far_end else 0) * 2 + half for half in range(2)]
            where = (row == (7 if far_end else 0)) & (group == p) & (second == side)
        else:
            tiles = [a * 2 + (1 if far_end else 0) for a in range(2)]
            where = lane == p * 16 + side * 8 + (7 if far_end else 0)
        for tile in tiles:
            rows, lanes = tile_slices(two, tile)
            line = faces[near + tile]
            line = pick(there, line, jnp.full_like(line, 1.0 / 36.0))
            halo[two, rows, lanes] = jnp.where(where, line, halo[two, rows, lanes])
    order = face_order(lane)
    for tile in range(4):
        rows, lanes = tile_slices(2, tile)
        halo[2, rows, lanes] = lanes_from(halo[2, rows, lanes], order)


def stream(star, halo, out, b, advances, final):
    row, lane = iotas((16, 128))
    within = lane % 16
    first, last = lane < 16, lane >= 112

    def roll(x, shift, axis):
        shift %= x.shape[axis]
        return pltpu.roll(x, shift, axis) if shift else x

    def ring(left, right, sign):
        a, c = roll(left, 16 * sign, 1), roll(right, 16 * sign, 1)
        if sign > 0:
            return jnp.where(first, c, a), jnp.where(first, a, c)
        return jnp.where(last, c, a), jnp.where(last, a, c)

    for q in range(19):
        c = VELOCITIES[q]
        old = [star[b, q, :, 128 * half : 128 * half + 128] for half in range(2)]
        new = list(old)
        if c[0]:
            side, p = side_of(q, 0)
            place = side * 8 + p
            for half in range(2):
                plane = halo[0, place : place + 1, 128 * half : 128 * half + 128]
                moved = roll(new[half], c[0], 0)
                new[half] = jnp.where(row == (0 if c[0] > 0 else 15), plane, moved)
        if c[1]:
            side, p = side_of(q, 1)
            border = halo[1, :, 128 * side : 128 * side + 128]
            border = roll(border, -16 * p if side == 0 else 112 - 16 * p, 1)
            if c[0]:
                border = roll(border, c[0], 0)
            a, d = roll(new[0], 16 * c[1], 1), roll(new[1], 16 * c[1], 1)
            if c[1] > 0:
                new = [jnp.where(first, border, a), jnp.where(first, a, d)]
            else:
                new = [jnp.where(last, d, a), jnp.where(last, border, d)]
        if c[2]:
            side, p = side_of(q, 2)
            borders = []
            for half in range(2):
                border = halo[2, :, 128 * half : 128 * half + 128]
                border = roll(border, -p if side == 0 else 7 - p, 1)
                if c[0]:
                    border = roll(border, c[0], 0)
                borders.append(border)
            if c[1]:
                borders = ring(borders[0], borders[1], c[1])
            for half in range(2):
                new[half] = jnp.where(
                    within == (0 if c[2] > 0 else 15), borders[half], roll(new[half], c[2], 1)
                )
        for half in range(2):
            result = pick(advances, new[half], old[half])
            if final:
                for a in range(2):
                    out[q, woven(b, 2 * a + half), :] = result[8 * a : 8 * a + 8]
            else:
                out[b, q, :, 128 * half : 128 * half + 128] = result


def kernel(
    pop_hbm,
    mask_hbm,
    level_hbm,
    nbr_hbm,
    link_hbm,
    out,
    pop,
    mask_ref,
    level,
    nbr,
    link,
    in_sems,
    star,
    middle,
    faces_a,
    faces_b,
    out_a,
    out_b,
    in_a,
    in_b,
    up_send_a,
    up_send_b,
    up_a,
    up_b,
    down_send,
    down,
    halo,
    table,
    wanted_own,
    wanted,
    wanted_side,
    mem_ss,
    mem_rs,
    side_ss,
    side_rs,
    meta_ss,
    meta_rs,
    up_a_ss,
    up_a_rs,
    up_b_ss,
    up_b_rs,
    down_ss,
    down_rs,
):
    s = lax.axis_index("section")
    m = lax.axis_index("member")
    loads = [
        pltpu.make_async_copy(src, dst, in_sems.at[i])
        for i, (src, dst) in enumerate(
            [
                (link_hbm, link),
                (level_hbm, level),
                (nbr_hbm, nbr),
                (pop_hbm, pop),
                (mask_hbm, mask_ref),
            ]
        )
    ]
    for load in loads:
        load.start()
    has = {-1: m > 0, 0: None, 1: m < NMEM - 1}
    one = jnp.int32(1)
    around = 1 + jnp.where(has[-1], one, 0) + jnp.where(has[1], one, 0)

    def if_member(dm, do):
        if has[dm] is None:
            do()
        else:
            pl.when(has[dm])(do)

    def each(low, high, do):
        def step(i, carry):
            do(i)
            return carry

        lax.fori_loop(low, high, step, 0)

    def blocks(do):
        each(0, 2, do)

    barrier = pltpu.get_barrier_semaphore()

    def greet(other):
        def signal(dm):
            pl.semaphore_signal(barrier, inc=1, device_id=(other, m + dm), device_id_type=MESH)

        pl.when(other != s)(lambda: signal(0))
        for dm in (-1, 1):
            if_member(dm, lambda dm=dm: signal(dm))

    each(0, NSEC, greet)

    def remote(src, dst, send_sem, recv_sem, other, dm):
        return pltpu.make_async_remote_copy(
            src_ref=src,
            dst_ref=dst,
            send_sem=send_sem,
            recv_sem=recv_sem,
            device_id=(other, m + dm),
            device_id_type=MESH,
        )

    def message(ref, place):
        return ref.at[place, pl.ds(0, 34)]

    def meta_copy(src, dst, other):
        return remote(src, dst, meta_ss, meta_rs, other, 0)

    def side_copy(dm, arriving):
        into = (1 + dm) // 2 if arriving else (1 - dm) // 2
        return remote(
            wanted, wanted_side.at[into], side_ss.at[(dm + 1) // 2], side_rs.at[into], s, dm
        )

    def mem_copy(sends, receives, step, dm, arriving):
        into = (1 + dm) // 2 if arriving else (1 - dm) // 2
        return remote(
            sends,
            receives.at[into],
            mem_ss.at[step, (dm + 1) // 2],
            mem_rs.at[step, into],
            s,
            dm,
        )

    def up_a_copy(src, dst, other):
        return remote(src, dst, up_a_ss, up_a_rs, other, 0)

    def up_b_copy(src, dst, other, dm):
        return remote(src, dst, up_b_ss, up_b_rs, other, dm)

    def down_copy(src, dst, other, dm):
        return remote(src, dst, down_ss, down_rs, other, dm)

    singles = tuple(range(1, NSEC))
    groups = tuple(sorted({k * e for k in range(1, NSEC - 1) for e in (2, 3)}))

    def wait_group(count, cases, ref, copy, receive):
        for n in cases:

            @pl.when(count == n)
            def _(n=n):
                whole = ref.at[pl.ds(0, n), pl.ds(0, 34)] if len(ref.shape) == 3 else ref.at[pl.ds(0, n)]
                both = copy(whole, whole)
                both.wait_recv() if receive else both.wait_send()

    below = s
    higher = NSEC - 1 - s
    below_direct = jnp.maximum(s - 1, 0)
    above = jnp.where(s == 0, NSEC, s + 1)
    higher_direct = NSEC - above

    for load in loads[:3]:
        load.wait()
    own = level[s]
    rate = jnp.where(
        own == 0, F32(1.0 / 0.55), jnp.where(own == 1, F32(1.0 / 0.6), F32(1.0 / 0.7))
    )
    blocks(lambda b: read_wanted(link, m, wanted_own, table, b))
    for load in loads[3:]:
        load.wait()

    def first_part(b):
        collide(pop, mask_ref, star, b, rate, own >= 1, True)
        export(star, faces_a, out_a, b)

    blocks(first_part)
    pl.semaphore_wait(barrier, NSEC * around - 1)

    def start_members(sends, receives, step):
        for dm in (-1, 1):
            if_member(dm, lambda dm=dm: mem_copy(sends, receives, step, dm, False).start())

    def receive_members(faces, receives, step):
        for dm in (-1, 1):

            def take(dm=dm):
                mem_copy(out_a, receives, step, dm, True).wait_recv()
                open_message(receives.at[(1 + dm) // 2], faces, 2 + 2 * dm)

            if_member(dm, take)

    each(0, s, lambda other: meta_copy(wanted_own, wanted.at[s], other).start())
    start_members(out_a, in_a, 0)
    restrict(faces_a, down_send)

    def start_down(other):
        for dm in (-1, 0, 1):
            if_member(
                dm,
                lambda dm=dm: down_copy(
                    down_send.at[pl.ds(0, 34)], message(down, s * 3 + 1 - dm), other, dm
                ).start(),
            )

    each(1, s, start_down)
    blocks(lambda b: read_links(nbr, link, level, own, m, table, b))
    receive_members(faces_a, in_a, 0)
    wait_group(higher, singles, wanted, lambda x, y: meta_copy(x, y, s), True)

    def send_up(other):
        select_quadrants(faces_a, lambda i: wanted[other, i], up_send_a, other, False)
        up_a_copy(message(up_send_a, other), message(up_a, s), other).start()

    each(s + 1, NSEC, send_up)
    for dm in (-1, 1):
        if_member(dm, lambda dm=dm: side_copy(dm, False).start())
    wait_group(below, singles, up_a, lambda x, y: up_a_copy(x, y, s), True)
    wait_group(
        jnp.where(s == 0, 0, higher) * around,
        groups,
        down,
        lambda x, y: down_copy(x, y, s, 0),
        True,
    )

    def second_part(b):
        build_halo(faces_a, up_a, down, halo, b, table, False)
        stream(star, halo, middle, b, own >= 1, False)

    blocks(second_part)

    def third_part(b):
        collide(middle, mask_ref, star, b, rate, own == 2, False)
        export(star, faces_b, out_b, b)

    blocks(third_part)
    start_members(out_b, in_b, 1)
    for dm in (-1, 1):
        if_member(dm, lambda dm=dm: side_copy(dm, True).wait_recv())

    def send_direct(other):
        for dm in (-1, 0, 1):

            def send(dm=dm):
                def ask(i):
                    return wanted[other, i] if dm == 0 else wanted_side[(1 + dm) // 2, other, i]

                place = other * 3 + dm + 1
                select_quadrants(faces_b, ask, up_send_b, place, True)
                up_b_copy(
                    message(up_send_b, place), message(up_b, s * 3 + 1 - dm), other, dm
                ).start()

            if_member(dm, send)

    each(above, NSEC, send_direct)
    wait_group(below, singles, wanted, lambda x, y: meta_copy(x, y, s), False)
    for dm in (-1, 1):
        if_member(dm, lambda dm=dm: mem_copy(out_a, in_a, 0, dm, False).wait_send())
        if_member(dm, lambda dm=dm: side_copy(dm, False).wait_send())
    wait_group(
        below_direct * around, groups, down, lambda x, y: down_copy(x, y, s, 0), False
    )
    wait_group(higher, singles, up_send_a, lambda x, y: up_a_copy(x, y, s), False)
    receive_members(faces_b, in_b, 1)
    for dm in (-1, 1):
        if_member(dm, lambda dm=dm: mem_copy(out_b, in_b, 1, dm, False).wait_send())
    wait_group(
        higher_direct * around, groups, up_send_b, lambda x, y: up_b_copy(x, y, s, 0), False
    )
    wait_group(
        below_direct * around, groups, up_b, lambda x, y: up_b_copy(x, y, s, 0), True
    )

    def fourth_part(b):
        build_halo(faces_b, up_b, None, halo, b, table, True)
        stream(star, halo, out, b, own == 2, True)

    blocks(fourth_part)


def body(populations, fluid_mask, section_level, neighbours, interface):
    state = pltpu.VMEM((2, 19, 16, 256), F32)
    faces = pltpu.VMEM((72, 8, 128), F32)
    by_section = pltpu.VMEM((NSEC, 40, 128), F32)
    by_device = pltpu.VMEM((NSEC * 3, 40, 128), F32)
    members = pltpu.VMEM((2, 60, 128), F32)
    arrived = pltpu.VMEM((2, 2, 60, 128), F32)
    vmem = pl.BlockSpec(memory_space=pltpu.VMEM)
    hbm = pl.BlockSpec(memory_space=pltpu.HBM)
    dma = pltpu.SemaphoreType.DMA
    out = pl.pallas_call(
        kernel,
        out_shape=jax.ShapeDtypeStruct((19, 64, 128), F32),
        in_specs=[hbm] * 5,
        out_specs=vmem,
        scratch_shapes=[
            pltpu.VMEM((19, 64, 128), F32),
            pltpu.VMEM((64, 128), jnp.int32),
            pltpu.SMEM((NSEC,), jnp.int32),
            pltpu.SMEM((2, 18), jnp.int32),
            pltpu.SMEM((2, 4, 6), jnp.int32),
            dma((5,)),
            state,
            state,
            faces,
            faces,
            members,
            members,
            arrived,
            arrived,
            by_section,
            by_device,
            by_section,
            by_device,
            pltpu.VMEM((40, 128), F32),
            by_device,
            pltpu.VMEM((3, 16, 256), F32),
            pltpu.SMEM((2 * TABLE,), jnp.int32),
            pltpu.SMEM((128,), jnp.int32),
            pltpu.SMEM((NSEC, 128), jnp.int32),
            pltpu.SMEM((2, NSEC, 128), jnp.int32),
            dma((2, 2)),
            dma((2, 2)),
            dma((2,)),
            dma((2,)),
        ]
        + [dma] * 8,
        compiler_params=pltpu.CompilerParams(
            collective_id=0, has_side_effects=True, vmem_limit_bytes=54400 * 1024
        ),
        name="lattice_step",
    )(
        populations.reshape(2, 19, 32, 128).transpose(1, 2, 0, 3).reshape(19, 64, 128),
        fluid_mask.reshape(2, 32, 128).transpose(1, 0, 2).reshape(64, 128),
        section_level,
        neighbours,
        interface.transpose(0, 2, 1),
    )
    return out.reshape(19, 32, 2, 128).transpose(2, 0, 1, 3).reshape(2, 19, 4096)


def solution(mesh):
    return jax.shard_map(
        body,
        mesh=mesh,
        in_specs=(
            P(("section", "member"), None, None),
            P(("section", "member"), None),
            P(),
            P(("section", "member"), None),
            P(("section", "member"), None, None),
        ),
        out_specs=P(("section", "member"), None, None),
        check_vma=False,
    )
```

```python
import jax
import jax.numpy as jnp
from jax import lax
from jax.experimental import pallas as pl
from jax.experimental.pallas import tpu as pltpu
from jax.sharding import PartitionSpec as P

MESH = pl.DeviceIdType.MESH
F32 = jnp.float32
NSEC = 8
NMEM = 32

VELOCITIES = (
    (0, 0, 0),
    (1, 0, 0),
    (-1, 0, 0),
    (0, 1, 0),
    (0, -1, 0),
    (0, 0, 1),
    (0, 0, -1),
    (1, 1, 0),
    (-1, -1, 0),
    (1, -1, 0),
    (-1, 1, 0),
    (1, 0, 1),
    (-1, 0, -1),
    (1, 0, -1),
    (-1, 0, 1),
    (0, 1, 1),
    (0, -1, -1),
    (0, 1, -1),
    (0, -1, 1),
)
OPPOSITE = (0, 2, 1, 4, 3, 6, 5, 8, 7, 10, 9, 12, 11, 14, 13, 16, 15, 18, 17)
SIDE_LISTS = tuple(
    tuple(tuple(q for q in range(19) if VELOCITIES[q][axis] == sign) for sign in (1, -1))
    for axis in range(3)
)


def side_of(q, axis):
    side = 0 if VELOCITIES[q][axis] > 0 else 1
    return side, SIDE_LISTS[axis][side].index(q)


def iotas(shape=(8, 128)):
    return lax.broadcasted_iota(jnp.int32, shape, 0), lax.broadcasted_iota(jnp.int32, shape, 1)


def lanes_from(x, index):
    return jnp.take_along_axis(x, index, axis=1)


def rows_from(x, index):
    return jnp.take_along_axis(x, index, axis=0)


def pick(cond, a, b):
    return lax.select(cond, a, b)


def tile_slices(axis, tile):
    first, second = 8 * (tile // 2), 128 * (tile % 2)
    return slice(first, first + 8), slice(second, second + 128)


def packing(count):
    packed = -(-count * 5 // 8)
    spare = [(d, g) for d in range(packed) for g in (5, 6, 7)]
    runs = []
    for source in range(packed, count):
        for group in range(5):
            d, g = spare.pop(0)
            last = runs[-1] if runs else None
            if last and last[0] == source and last[2] == d and last[3] + last[4] == g:
                runs[-1] = last[:4] + (last[4] + 1,)
            else:
                runs.append((source, group, d, g, 1))
    return packed, runs


def lane_roll(x, shift):
    shift %= 128
    return pltpu.roll(x, shift, 1) if shift else x


def pack(tiles):
    lane = iotas()[1]
    packed, runs = packing(len(tiles))
    result = list(tiles[:packed])
    for source, group, d, g, length in runs:
        moved = lane_roll(tiles[source], 16 * (g - group))
        inside = (lane >= 16 * g) & (lane < 16 * (g + length))
        result[d] = jnp.where(inside, moved, result[d])
    return result


def unpack(load, source, count):
    lane = iotas()[1]
    packed, runs = packing(count)
    if source < packed:
        return load(source)
    result = None
    for which, group, d, g, length in runs:
        if which == source:
            moved = lane_roll(load(d), 16 * (group - g))
            result = moved if result is None else jnp.where(lane >= 16 * group, moved, result)
    return result


def store_message(tiles, put):
    for d, t in enumerate(pack([tiles[1], tiles[2], tiles[4], tiles[5]])):
        put(8 * d, t)
    for b in range(2):
        put(24 + 5 * b, tiles[3 * b][0:5])


def message_tile(load, axis, block):
    if axis == 0:
        pair = load(24), load(29)
    else:
        pair = tuple(unpack(lambda d: load(8 * d), 2 * b + axis - 1, 4) for b in range(2))
    return pick(block == 0, pair[0], pair[1])


def face_order(lane):
    return (lane % 8) * 16 + lane // 8 % 2 * 8 + lane // 16


def woven(b, tile):
    return pl.ds(32 * (tile // 2) + 2 * (tile % 2) + b, 8, stride=4)


def collide(cur, mask_ref, star, b, rate, advances, first):
    for tile in range(4):
        rows, lanes = tile_slices(0, tile)
        if first:
            f = [cur[q, woven(b, tile), :] for q in range(19)]
        else:
            f = [cur[b, q, rows, lanes] for q in range(19)]
        density = f[0]
        for q in range(1, 19):
            density = density + f[q]
        velocity = []
        for axis in range(3):
            plus, minus = SIDE_LISTS[axis]
            momentum = f[plus[0]] - f[minus[0]]
            for i in range(1, 5):
                momentum = momentum + f[plus[i]]
            for i in range(1, 5):
                momentum = momentum - f[minus[i]]
            velocity.append(momentum / density)
        base = 1.0 - 1.5 * (
            velocity[0] * velocity[0] + velocity[1] * velocity[1] + velocity[2] * velocity[2]
        )
        fluid = mask_ref[woven(b, tile), :] == 1
        keep = 1.0 - rate
        scaled = rate * density

        def put(q, relaxed):
            star[b, q, rows, lanes] = pick(
                advances, jnp.where(fluid, relaxed, f[OPPOSITE[q]]), f[q]
            )

        put(0, keep * f[0] + scaled * (1.0 / 3.0) * base)
        axis_weight = scaled * (1.0 / 18.0)
        edge_weight = scaled * (1.0 / 36.0)
        for q in range(1, 19, 2):
            c = VELOCITIES[q]
            along = None
            for axis in range(3):
                if c[axis]:
                    term = velocity[axis] if c[axis] > 0 else -velocity[axis]
                    along = term if along is None else along + term
            weight = axis_weight if q < 7 else edge_weight
            even = weight * (base + 4.5 * along * along)
            odd = weight * (3.0 * along)
            put(q, keep * f[q] + (even + odd))
            put(q + 1, keep * f[q + 1] + (even - odd))


def export(star, faces, message, b):
    row, lane = iotas()
    group, within = lane // 16, lane % 16
    for side in range(2):
        for p, q in enumerate(SIDE_LISTS[0][side]):
            layer = 15 if side == 0 else 0
            for half in range(2):
                line = star[b, q, layer : layer + 1, 128 * half : 128 * half + 128]
                place = side * 2 + half
                faces[(2 + b) * 12 + place, p : p + 1, :] = line
                message[b, 40 + 5 * place + p : 41 + 5 * place + p, :] = line
    zero = jnp.zeros((8, 128), F32)
    tiles = [None] * 8
    order = face_order(lane)
    for a in range(2):
        for side in range(2):
            total = zero
            for p, q in enumerate(SIDE_LISTS[1][side]):
                half = 1 - side
                x = star[b, q, 8 * a : 8 * a + 8, 128 * half : 128 * half + 128]
                shift = (16 * p + 16 if side == 0 else 16 * p) % 128
                x = pltpu.roll(x, shift, 1) if shift else x
                total = jnp.where(group == p, x, total)
            tiles[a * 2 + side] = total
        for half in range(2):
            total = zero
            for side in range(2):
                for p, q in enumerate(SIDE_LISTS[2][side]):
                    x = star[b, q, 8 * a : 8 * a + 8, 128 * half : 128 * half + 128]
                    shift = 113 + p if side == 0 else 8 + p
                    x = pltpu.roll(x, shift, 1)
                    total = jnp.where(within == side * 8 + p, x, total)
            tiles[4 + a * 2 + half] = lanes_from(total, order)
    for i, t in enumerate(tiles):
        faces[(2 + b) * 12 + 4 + i] = t
    for d, t in enumerate(pack(tiles)):
        message[b, 8 * d : 8 * d + 8, :] = t


def open_message(message, faces, place):
    def one(b, carry):
        for i in range(8):
            faces[(place + b) * 12 + 4 + i] = unpack(
                lambda d: message[b, 8 * d : 8 * d + 8, :], i, 8
            )
        for tile in range(4):
            faces[(place + b) * 12 + tile, 0:5, :] = message[b, 40 + 5 * tile : 45 + 5 * tile, :]
        return carry

    lax.fori_loop(0, 2, one, 0)


def restrict(faces, down):
    tiles = [t for b in range(2) for t in restrict_block(faces, b)]

    def put(row, t):
        down[row : row + t.shape[0], :] = t

    store_message(tiles, put)


def restrict_block(faces, b):
    row, lane = iotas()
    group, within, low = lane // 16, lane % 16, lane % 8
    second = (lane // 8) % 2
    fine = group * 16 + 2 * low
    coarse = (2 * (group % 4)) * 16
    pair_rows = 2 * (row % 4)
    parts = []
    for side in range(2):
        halves = []
        for half in range(2):
            t = faces[(2 + b) * 12 + side * 2 + half]
            t = t + pltpu.roll(t, 127, 1)
            t = t + pltpu.roll(t, 112, 1)
            halves.append(lanes_from(t, coarse + 2 * low))
        parts.append(jnp.where(group < 4, halves[0], halves[1]))
    tiles = [0.25 * jnp.where(second == 0, parts[0], parts[1])]
    parts = []
    for side in range(2):
        rows = []
        for a in range(2):
            t = faces[(2 + b) * 12 + 4 + a * 2 + side]
            t = t + pltpu.roll(t, 127, 1)
            t = t + pltpu.roll(t, 7, 0)
            rows.append(rows_from(lanes_from(t, fine), pair_rows))
        parts.append(jnp.where(row < 4, rows[0], rows[1]))
    tiles.append(0.25 * jnp.where(second == 0, parts[0], parts[1]))
    rows = []
    for a in range(2):
        halves = []
        for half in range(2):
            t = faces[(2 + b) * 12 + 8 + a * 2 + half]
            t = t + pltpu.roll(t, 127, 1)
            halves.append(lanes_from(t, group * 16 + second * 8 + 2 * (low % 4)))
        t = jnp.where(low < 4, halves[0], halves[1])
        t = t + pltpu.roll(t, 7, 0)
        rows.append(rows_from(t, pair_rows))
    tiles.append(0.25 * jnp.where(row < 4, rows[0], rows[1]))
    return tiles


def member_offset(block, member):
    return jnp.clip(((block >> 1) & (NMEM - 1)) - member + 1, 0, 2)


def slot_of(block, member):
    return member_offset(block, member) * 2 + (block & 1)


NEAR, STATE, UP_SAME, UP_DIRECT, DOWN, DOWN_BLOCK, EDGE, EDGE_THERE, TABLE = (
    0,
    6,
    12,
    18,
    24,
    48,
    72,
    84,
    96,
)


SECTION_SHIFT = NMEM.bit_length()


def read_wanted(link, member, wanted, table, b):
    for axis in range(3):
        for side in range(2):
            i, j = axis * 2 + side, axis * 2 + 1 - side
            code = jnp.int32(-1)
            for k in range(4):
                block = link[b, k, j]
                code = jnp.maximum(code, jnp.where(block >= 0, block * 4 + k, -1))
            table[b * TABLE + STATE + i] = code
            safe = jnp.maximum(code, 0)
            k, block = safe & 3, safe >> 2
            first, last = k >> 1, k & 1
            if axis == 0:
                tile = side * 2 + first
            elif axis == 1:
                tile = 4 + first * 2 + side
            else:
                tile = 8 + k
            wanted[b * 6 + i] = slot_of(block, member) * 12 + tile
            wanted[12 + b * 6 + i] = (2 + (block & 1)) * 12 + tile
            wanted[24 + b * 6 + i] = last


def read_links(nbr, link, level, own, member, table, b):
    for axis in range(3):
        for side in range(2):
            i, j = axis * 2 + side, axis * 2 + 1 - side
            for k in range(4):
                block = link[b, k, j]
                safe = jnp.maximum(block, 0)
                place = (safe >> SECTION_SHIFT) * 3 + member_offset(safe, member)
                table[b * TABLE + DOWN + i * 4 + k] = place
                table[b * TABLE + DOWN_BLOCK + i * 4 + k] = jnp.where(block >= 0, safe & 1, -1)
            code = table[b * TABLE + STATE + i]
            block = jnp.maximum(code, 0) >> 2
            section = block >> SECTION_SHIFT
            near = nbr[b, j]
            table[b * TABLE + NEAR + i] = slot_of(jnp.maximum(near, 0), member) * 12
            linked = jnp.where(code < 0, 3, jnp.where(level[section] < own, 1, 2))
            table[b * TABLE + STATE + i] = jnp.where(near >= 0, 0, linked)
            table[b * TABLE + UP_SAME + i] = section
            table[b * TABLE + UP_DIRECT + i] = section * 3 + member_offset(block, member)
    for q in range(7, 19):
        block = nbr[b, OPPOSITE[q] - 1]
        table[b * TABLE + EDGE + q - 7] = slot_of(jnp.maximum(block, 0), member) * 12
        table[b * TABLE + EDGE_THERE + q - 7] = block


def select_quadrants(faces, ask, out, place, direct):
    lane = iotas()[1]
    second = (lane // 8) % 2
    tiles = []
    for b in range(2):
        for axis in range(3):
            parts = []
            for side in range(2):
                i = b * 6 + axis * 2 + side
                t = faces[ask((12 if direct else 0) + i)]
                if axis < 2:
                    t = pick(ask(24 + i) == side, t, pltpu.roll(t, 8 if side else 120, 1))
                parts.append(t)
            tiles.append(jnp.where(second == 0, parts[0], parts[1]))

    def put(row, t):
        out[place, row : row + t.shape[0], :] = t

    store_message(tiles, put)


def build_halo(faces, up, down, halo, b, table, direct):
    row, lane = iotas()
    group, within, low = lane // 16, lane % 16, lane % 8
    second = (lane // 8) % 2
    spread_rows = [4 * a + row // 2 for a in range(2)]

    def entry(place):
        return table[b * TABLE + place]

    def means(axis, i, k):
        place, block = entry(DOWN + i * 4 + k), entry(DOWN_BLOCK + i * 4 + k)
        t = message_tile(lambda row: down[place, row : row + 8, :], axis, block)
        return pick(block >= 0, t, jnp.zeros_like(t))

    for axis in range(3):
        states, near, quads, ups = [], [], [], []
        for side in range(2):
            i = axis * 2 + side
            states.append(entry(STATE + i))
            near.append(entry(NEAR + i) + axis * 4)
            place = entry((UP_DIRECT if direct else UP_SAME) + i)
            ups.append(
                message_tile(lambda row, place=place: up[place, row : row + 8, :], axis, b)
            )
            if down is not None:
                quads.append([means(axis, i, k) for k in range(4)])
        if axis == 0:
            rest = jnp.where(row == 0, F32(1.0 / 18.0), F32(1.0 / 36.0))
        else:
            rest = jnp.where(group == 0, F32(1.0 / 18.0), F32(1.0 / 36.0))

        def choose(side, tile, from_up, from_down):
            state = states[side]
            far = rest if from_down is None else pick(state == 2, from_down, rest)
            far = pick(state == 1, from_up, far)
            return pick(state == 0, faces[near[side] + tile], far)

        if axis < 2:
            for side in range(2):
                if axis == 1:
                    wide = lanes_from(ups[side], group * 16 + side * 8 + within // 2)
                for a in range(2):
                    if axis == 0:
                        tile = side * 2 + a
                        from_up = lanes_from(
                            ups[side], (4 * a + group // 2) * 16 + side * 8 + within // 2
                        )
                    else:
                        tile = a * 2 + side
                        from_up = rows_from(wide, spread_rows[a])
                    from_down = None
                    if down is not None:
                        low_part, high_part = quads[side][2 * a], quads[side][2 * a + 1]
                        if side:
                            low_part = pltpu.roll(low_part, 120, 1)
                        else:
                            high_part = pltpu.roll(high_part, 8, 1)
                        from_down = jnp.where(second == 0, low_part, high_part)
                    rows, lanes = tile_slices(axis, tile)
                    halo[axis, rows, lanes] = choose(side, tile, from_up, from_down)
        else:
            both = jnp.where(second == 0, ups[0], ups[1])
            for half in range(2):
                wide = lanes_from(both, group * 16 + second * 8 + 4 * half + low // 2)
                for a in range(2):
                    tile = a * 2 + half
                    from_up = rows_from(wide, spread_rows[a])
                    parts = [
                        choose(side, tile, from_up, quads[side][tile] if down is not None else None)
                        for side in range(2)
                    ]
                    rows, lanes = tile_slices(axis, tile)
                    halo[axis, rows, lanes] = jnp.where(second == 0, parts[0], parts[1])

    for q in range(7, 19):
        c = VELOCITIES[q]
        one, two = [axis for axis in range(3) if c[axis]]
        side, p = side_of(q, two)
        near, there = entry(EDGE + q - 7) + two * 4, entry(EDGE_THERE + q - 7) >= 0
        far_end = c[one] > 0
        if two == 1:
            tiles = [(1 if far_end else 0) * 2 + side]
            where = (row == (7 if far_end else 0)) & (group == p)
        elif one == 0:
            tiles = [(1 if far_end else 0) * 2 + half for half in range(2)]
            where = (row == (7 if far_end else 0)) & (group == p) & (second == side)
        else:
            tiles = [a * 2 + (1 if far_end else 0) for a in range(2)]
            where = lane == p * 16 + side * 8 + (7 if far_end else 0)
        for tile in tiles:
            rows, lanes = tile_slices(two, tile)
            line = faces[near + tile]
            line = pick(there, line, jnp.full_like(line, 1.0 / 36.0))
            halo[two, rows, lanes] = jnp.where(where, line, halo[two, rows, lanes])
    order = face_order(lane)
    for tile in range(4):
        rows, lanes = tile_slices(2, tile)
        halo[2, rows, lanes] = lanes_from(halo[2, rows, lanes], order)


def stream(star, halo, out, b, advances, final):
    row, lane = iotas((16, 128))
    within = lane % 16
    first, last = lane < 16, lane >= 112

    def roll(x, shift, axis):
        shift %= x.shape[axis]
        return pltpu.roll(x, shift, axis) if shift else x

    def ring(left, right, sign):
        a, c = roll(left, 16 * sign, 1), roll(right, 16 * sign, 1)
        if sign > 0:
            return jnp.where(first, c, a), jnp.where(first, a, c)
        return jnp.where(last, c, a), jnp.where(last, a, c)

    for q in range(19):
        c = VELOCITIES[q]
        old = [star[b, q, :, 128 * half : 128 * half + 128] for half in range(2)]
        new = list(old)
        if c[0]:
            side, p = side_of(q, 0)
            place = side * 8 + p
            for half in range(2):
                plane = halo[0, place : place + 1, 128 * half : 128 * half + 128]
                moved = roll(new[half], c[0], 0)
                new[half] = jnp.where(row == (0 if c[0] > 0 else 15), plane, moved)
        if c[1]:
            side, p = side_of(q, 1)
            border = halo[1, :, 128 * side : 128 * side + 128]
            border = roll(border, -16 * p if side == 0 else 112 - 16 * p, 1)
            if c[0]:
                border = roll(border, c[0], 0)
            a, d = roll(new[0], 16 * c[1], 1), roll(new[1], 16 * c[1], 1)
            if c[1] > 0:
                new = [jnp.where(first, border, a), jnp.where(first, a, d)]
            else:
                new = [jnp.where(last, d, a), jnp.where(last, border, d)]
        if c[2]:
            side, p = side_of(q, 2)
            borders = []
            for half in range(2):
                border = halo[2, :, 128 * half : 128 * half + 128]
                border = roll(border, -p if side == 0 else 7 - p, 1)
                if c[0]:
                    border = roll(border, c[0], 0)
                borders.append(border)
            if c[1]:
                borders = ring(borders[0], borders[1], c[1])
            for half in range(2):
                new[half] = jnp.where(
                    within == (0 if c[2] > 0 else 15), borders[half], roll(new[half], c[2], 1)
                )
        for half in range(2):
            result = pick(advances, new[half], old[half])
            if final:
                for a in range(2):
                    out[q, woven(b, 2 * a + half), :] = result[8 * a : 8 * a + 8]
            else:
                out[b, q, :, 128 * half : 128 * half + 128] = result


def kernel(
    pop_hbm,
    mask_hbm,
    level_hbm,
    nbr_hbm,
    link_hbm,
    out,
    pop,
    mask_ref,
    level,
    nbr,
    link,
    in_sems,
    star,
    middle,
    faces_a,
    faces_b,
    out_a,
    out_b,
    in_a,
    in_b,
    up_send_a,
    up_send_b,
    up_a,
    up_b,
    down_send,
    down,
    halo,
    table,
    wanted_own,
    wanted,
    wanted_side,
    mem_ss,
    mem_rs,
    side_ss,
    side_rs,
    meta_ss,
    meta_rs,
    up_a_ss,
    up_a_rs,
    up_b_ss,
    up_b_rs,
    down_ss,
    down_rs,
):
    s = lax.axis_index("section")
    m = lax.axis_index("member")
    loads = [
        pltpu.make_async_copy(src, dst, in_sems.at[i])
        for i, (src, dst) in enumerate(
            [
                (link_hbm, link),
                (level_hbm, level),
                (nbr_hbm, nbr),
                (pop_hbm, pop),
                (mask_hbm, mask_ref),
            ]
        )
    ]
    for load in loads:
        load.start()
    has = {-1: m > 0, 0: None, 1: m < NMEM - 1}
    one = jnp.int32(1)
    around = 1 + jnp.where(has[-1], one, 0) + jnp.where(has[1], one, 0)

    def if_member(dm, do):
        if has[dm] is None:
            do()
        else:
            pl.when(has[dm])(do)

    def each(low, high, do):
        def step(i, carry):
            do(i)
            return carry

        lax.fori_loop(low, high, step, 0)

    def blocks(do):
        each(0, 2, do)

    barrier = pltpu.get_barrier_semaphore()

    def greet(other):
        def signal(dm):
            pl.semaphore_signal(barrier, inc=1, device_id=(other, m + dm), device_id_type=MESH)

        pl.when(other != s)(lambda: signal(0))
        for dm in (-1, 1):
            if_member(dm, lambda dm=dm: signal(dm))

    each(0, NSEC, greet)

    def remote(src, dst, send_sem, recv_sem, other, dm):
        return pltpu.make_async_remote_copy(
            src_ref=src,
            dst_ref=dst,
            send_sem=send_sem,
            recv_sem=recv_sem,
            device_id=(other, m + dm),
            device_id_type=MESH,
        )

    def message(ref, place):
        return ref.at[place, pl.ds(0, 34)]

    def meta_copy(src, dst, other):
        return remote(src, dst, meta_ss, meta_rs, other, 0)

    def side_copy(dm, arriving):
        into = (1 + dm) // 2 if arriving else (1 - dm) // 2
        return remote(
            wanted, wanted_side.at[into], side_ss.at[(dm + 1) // 2], side_rs.at[into], s, dm
        )

    def mem_copy(sends, receives, step, dm, arriving):
        into = (1 + dm) // 2 if arriving else (1 - dm) // 2
        return remote(
            sends,
            receives.at[into],
            mem_ss.at[step, (dm + 1) // 2],
            mem_rs.at[step, into],
            s,
            dm,
        )

    def up_a_copy(src, dst, other):
        return remote(src, dst, up_a_ss, up_a_rs, other, 0)

    def up_b_copy(src, dst, other, dm):
        return remote(src, dst, up_b_ss, up_b_rs, other, dm)

    def down_copy(src, dst, other, dm):
        return remote(src, dst, down_ss, down_rs, other, dm)

    singles = tuple(range(1, NSEC))
    groups = tuple(sorted({k * e for k in range(1, NSEC - 1) for e in (2, 3)}))

    def wait_group(count, cases, ref, copy, receive):
        for n in cases:

            @pl.when(count == n)
            def _(n=n):
                whole = ref.at[pl.ds(0, n), pl.ds(0, 34)] if len(ref.shape) == 3 else ref.at[pl.ds(0, n)]
                both = copy(whole, whole)
                both.wait_recv() if receive else both.wait_send()

    below = s
    higher = NSEC - 1 - s
    below_direct = jnp.maximum(s - 1, 0)
    above = jnp.where(s == 0, NSEC, s + 1)
    higher_direct = NSEC - above

    for load in loads[:3]:
        load.wait()
    own = level[s]
    rate = jnp.where(
        own == 0, F32(1.0 / 0.55), jnp.where(own == 1, F32(1.0 / 0.6), F32(1.0 / 0.7))
    )
    blocks(lambda b: read_wanted(link, m, wanted_own, table, b))
    for load in loads[3:]:
        load.wait()

    def first_part(b):
        collide(pop, mask_ref, star, b, rate, own >= 1, True)
        export(star, faces_a, out_a, b)

    blocks(first_part)
    pl.semaphore_wait(barrier, NSEC * around - 1)

    def start_members(sends, receives, step):
        for dm in (-1, 1):
            if_member(dm, lambda dm=dm: mem_copy(sends, receives, step, dm, False).start())

    def receive_members(faces, receives, step):
        for dm in (-1, 1):

            def take(dm=dm):
                mem_copy(out_a, receives, step, dm, True).wait_recv()
                open_message(receives.at[(1 + dm) // 2], faces, 2 + 2 * dm)

            if_member(dm, take)

    each(0, s, lambda other: meta_copy(wanted_own, wanted.at[s], other).start())
    start_members(out_a, in_a, 0)
    restrict(faces_a, down_send)

    def start_down(other):
        for dm in (-1, 0, 1):
            if_member(
                dm,
                lambda dm=dm: down_copy(
                    down_send.at[pl.ds(0, 34)], message(down, s * 3 + 1 - dm), other, dm
                ).start(),
            )

    each(1, s, start_down)
    blocks(lambda b: read_links(nbr, link, level, own, m, table, b))
    receive_members(faces_a, in_a, 0)
    wait_group(higher, singles, wanted, lambda x, y: meta_copy(x, y, s), True)

    def send_up(other):
        select_quadrants(faces_a, lambda i: wanted[other, i], up_send_a, other, False)
        up_a_copy(message(up_send_a, other), message(up_a, s), other).start()

    each(s + 1, NSEC, send_up)
    for dm in (-1, 1):
        if_member(dm, lambda dm=dm: side_copy(dm, False).start())
    wait_group(below, singles, up_a, lambda x, y: up_a_copy(x, y, s), True)
    wait_group(
        jnp.where(s == 0, 0, higher) * around,
        groups,
        down,
        lambda x, y: down_copy(x, y, s, 0),
        True,
    )

    def second_part(b):
        build_halo(faces_a, up_a, down, halo, b, table, False)
        stream(star, halo, middle, b, own >= 1, False)

    blocks(second_part)

    def third_part(b):
        collide(middle, mask_ref, star, b, rate, own == 2, False)
        export(star, faces_b, out_b, b)

    blocks(third_part)
    start_members(out_b, in_b, 1)
    for dm in (-1, 1):
        if_member(dm, lambda dm=dm: side_copy(dm, True).wait_recv())

    def send_direct(other):
        for dm in (-1, 0, 1):

            def send(dm=dm):
                def ask(i):
                    return wanted[other, i] if dm == 0 else wanted_side[(1 + dm) // 2, other, i]

                place = other * 3 + dm + 1
                select_quadrants(faces_b, ask, up_send_b, place, True)
                up_b_copy(
                    message(up_send_b, place), message(up_b, s * 3 + 1 - dm), other, dm
                ).start()

            if_member(dm, send)

    each(above, NSEC, send_direct)
    wait_group(below, singles, wanted, lambda x, y: meta_copy(x, y, s), False)
    for dm in (-1, 1):
        if_member(dm, lambda dm=dm: mem_copy(out_a, in_a, 0, dm, False).wait_send())
        if_member(dm, lambda dm=dm: side_copy(dm, False).wait_send())
    wait_group(
        below_direct * around, groups, down, lambda x, y: down_copy(x, y, s, 0), False
    )
    wait_group(higher, singles, up_send_a, lambda x, y: up_a_copy(x, y, s), False)
    receive_members(faces_b, in_b, 1)
    for dm in (-1, 1):
        if_member(dm, lambda dm=dm: mem_copy(out_b, in_b, 1, dm, False).wait_send())
    wait_group(
        higher_direct * around, groups, up_send_b, lambda x, y: up_b_copy(x, y, s, 0), False
    )
    wait_group(
        below_direct * around, groups, up_b, lambda x, y: up_b_copy(x, y, s, 0), True
    )

    def fourth_part(b):
        build_halo(faces_b, up_b, None, halo, b, table, True)
        stream(star, halo, out, b, own == 2, True)

    blocks(fourth_part)


def body(populations, fluid_mask, section_level, neighbours, interface):
    state = pltpu.VMEM((2, 19, 16, 256), F32)
    faces = pltpu.VMEM((72, 8, 128), F32)
    by_section = pltpu.VMEM((NSEC, 40, 128), F32)
    by_device = pltpu.VMEM((NSEC * 3, 40, 128), F32)
    members = pltpu.VMEM((2, 60, 128), F32)
    arrived = pltpu.VMEM((2, 2, 60, 128), F32)
    vmem = pl.BlockSpec(memory_space=pltpu.VMEM)
    hbm = pl.BlockSpec(memory_space=pltpu.HBM)
    dma = pltpu.SemaphoreType.DMA
    out = pl.pallas_call(
        kernel,
        out_shape=pltpu.VMEM((19, 64, 128), F32),
        in_specs=[hbm] * 5,
        out_specs=vmem,
        scratch_shapes=[
            pltpu.VMEM((19, 64, 128), F32),
            pltpu.VMEM((64, 128), jnp.int32),
            pltpu.SMEM((NSEC,), jnp.int32),
            pltpu.SMEM((2, 18), jnp.int32),
            pltpu.SMEM((2, 4, 6), jnp.int32),
            dma((5,)),
            state,
            state,
            faces,
            faces,
            members,
            members,
            arrived,
            arrived,
            by_section,
            by_device,
            by_section,
            by_device,
            pltpu.VMEM((40, 128), F32),
            by_device,
            pltpu.VMEM((3, 16, 256), F32),
            pltpu.SMEM((2 * TABLE,), jnp.int32),
            pltpu.SMEM((128,), jnp.int32),
            pltpu.SMEM((NSEC, 128), jnp.int32),
            pltpu.SMEM((2, NSEC, 128), jnp.int32),
            dma((2, 2)),
            dma((2, 2)),
            dma((2,)),
            dma((2,)),
        ]
        + [dma] * 8,
        compiler_params=pltpu.CompilerParams(
            collective_id=0, has_side_effects=True, vmem_limit_bytes=54656 * 1024
        ),
        name="lattice_step",
    )(
        populations.reshape(2, 19, 32, 128).transpose(1, 2, 0, 3).reshape(19, 64, 128),
        fluid_mask.reshape(2, 32, 128).transpose(1, 0, 2).reshape(64, 128),
        section_level,
        neighbours,
        interface.transpose(0, 2, 1),
    )
    return out.reshape(19, 32, 2, 128).transpose(2, 0, 1, 3).reshape(2, 19, 4096)


def solution(mesh):
    return jax.shard_map(
        body,
        mesh=mesh,
        in_specs=(
            P(("section", "member"), None, None),
            P(("section", "member"), None),
            P(),
            P(("section", "member"), None),
            P(("section", "member"), None, None),
        ),
        out_specs=P(("section", "member"), None, None),
        check_vma=False,
    )
```

```python
import jax
import jax.numpy as jnp
from jax import lax
from jax.experimental import pallas as pl
from jax.experimental.pallas import tpu as pltpu
from jax.sharding import PartitionSpec as P

MESH = pl.DeviceIdType.MESH
F32 = jnp.float32
NSEC = 8
NMEM = 32

VELOCITIES = (
    (0, 0, 0),
    (1, 0, 0),
    (-1, 0, 0),
    (0, 1, 0),
    (0, -1, 0),
    (0, 0, 1),
    (0, 0, -1),
    (1, 1, 0),
    (-1, -1, 0),
    (1, -1, 0),
    (-1, 1, 0),
    (1, 0, 1),
    (-1, 0, -1),
    (1, 0, -1),
    (-1, 0, 1),
    (0, 1, 1),
    (0, -1, -1),
    (0, 1, -1),
    (0, -1, 1),
)
OPPOSITE = (0, 2, 1, 4, 3, 6, 5, 8, 7, 10, 9, 12, 11, 14, 13, 16, 15, 18, 17)
SIDE_LISTS = tuple(
    tuple(tuple(q for q in range(19) if VELOCITIES[q][axis] == sign) for sign in (1, -1))
    for axis in range(3)
)


def side_of(q, axis):
    side = 0 if VELOCITIES[q][axis] > 0 else 1
    return side, SIDE_LISTS[axis][side].index(q)


def iotas(shape=(8, 128)):
    return lax.broadcasted_iota(jnp.int32, shape, 0), lax.broadcasted_iota(jnp.int32, shape, 1)


def lanes_from(x, index):
    return jnp.take_along_axis(x, index, axis=1)


def rows_from(x, index):
    return jnp.take_along_axis(x, index, axis=0)


def pick(cond, a, b):
    return lax.select(cond, a, b)


def tile_slices(axis, tile):
    first, second = 8 * (tile // 2), 128 * (tile % 2)
    return slice(first, first + 8), slice(second, second + 128)


def packing(count):
    packed = -(-count * 5 // 8)
    spare = [(d, g) for d in range(packed) for g in (5, 6, 7)]
    runs = []
    for source in range(packed, count):
        for group in range(5):
            d, g = spare.pop(0)
            last = runs[-1] if runs else None
            if last and last[0] == source and last[2] == d and last[3] + last[4] == g:
                runs[-1] = last[:4] + (last[4] + 1,)
            else:
                runs.append((source, group, d, g, 1))
    return packed, runs


def lane_roll(x, shift):
    shift %= 128
    return pltpu.roll(x, shift, 1) if shift else x


def pack(tiles):
    lane = iotas()[1]
    packed, runs = packing(len(tiles))
    result = list(tiles[:packed])
    for source, group, d, g, length in runs:
        moved = lane_roll(tiles[source], 16 * (g - group))
        inside = (lane >= 16 * g) & (lane < 16 * (g + length))
        result[d] = jnp.where(inside, moved, result[d])
    return result


def unpack(load, source, count):
    lane = iotas()[1]
    packed, runs = packing(count)
    if source < packed:
        return load(source)
    result = None
    for which, group, d, g, length in runs:
        if which == source:
            moved = lane_roll(load(d), 16 * (group - g))
            result = moved if result is None else jnp.where(lane >= 16 * group, moved, result)
    return result


def store_message(tiles, put):
    for d, t in enumerate(pack([tiles[1], tiles[2], tiles[4], tiles[5]])):
        put(8 * d, t)
    for b in range(2):
        put(24 + 5 * b, tiles[3 * b][0:5])


def message_tile(load, axis, block):
    if axis == 0:
        pair = load(24), load(29)
    else:
        pair = tuple(unpack(lambda d: load(8 * d), 2 * b + axis - 1, 4) for b in range(2))
    return pick(block == 0, pair[0], pair[1])


def face_order(lane):
    return (lane % 8) * 16 + lane // 8 % 2 * 8 + lane // 16


def woven(b, tile):
    return pl.ds(32 * (tile // 2) + 2 * (tile % 2) + b, 8, stride=4)


def collide(cur, mask_ref, star, b, rate, advances, first):
    for tile in range(4):
        rows, lanes = tile_slices(0, tile)
        if first:
            f = [cur[q, woven(b, tile), :] for q in range(19)]
        else:
            f = [cur[b, q, rows, lanes] for q in range(19)]
        density = f[0]
        for q in range(1, 19):
            density = density + f[q]
        velocity = []
        for axis in range(3):
            plus, minus = SIDE_LISTS[axis]
            momentum = f[plus[0]] - f[minus[0]]
            for i in range(1, 5):
                momentum = momentum + f[plus[i]]
            for i in range(1, 5):
                momentum = momentum - f[minus[i]]
            velocity.append(momentum / density)
        base = 1.0 - 1.5 * (
            velocity[0] * velocity[0] + velocity[1] * velocity[1] + velocity[2] * velocity[2]
        )
        fluid = mask_ref[woven(b, tile), :] == 1
        keep = 1.0 - rate
        scaled = rate * density

        def put(q, relaxed):
            star[b, q, rows, lanes] = pick(
                advances, jnp.where(fluid, relaxed, f[OPPOSITE[q]]), f[q]
            )

        put(0, keep * f[0] + scaled * (1.0 / 3.0) * base)
        axis_weight = scaled * (1.0 / 18.0)
        edge_weight = scaled * (1.0 / 36.0)
        for q in range(1, 19, 2):
            c = VELOCITIES[q]
            along = None
            for axis in range(3):
                if c[axis]:
                    term = velocity[axis] if c[axis] > 0 else -velocity[axis]
                    along = term if along is None else along + term
            weight = axis_weight if q < 7 else edge_weight
            even = weight * (base + 4.5 * along * along)
            odd = weight * (3.0 * along)
            put(q, keep * f[q] + (even + odd))
            put(q + 1, keep * f[q + 1] + (even - odd))


def export(star, faces, message, b):
    row, lane = iotas()
    group, within = lane // 16, lane % 16
    for side in range(2):
        for p, q in enumerate(SIDE_LISTS[0][side]):
            layer = 15 if side == 0 else 0
            for half in range(2):
                line = star[b, q, layer : layer + 1, 128 * half : 128 * half + 128]
                place = side * 2 + half
                faces[(2 + b) * 12 + place, p : p + 1, :] = line
                message[b, 40 + 5 * place + p : 41 + 5 * place + p, :] = line
    zero = jnp.zeros((8, 128), F32)
    tiles = [None] * 8
    order = face_order(lane)
    for a in range(2):
        for side in range(2):
            total = zero
            for p, q in enumerate(SIDE_LISTS[1][side]):
                half = 1 - side
                x = star[b, q, 8 * a : 8 * a + 8, 128 * half : 128 * half + 128]
                shift = (16 * p + 16 if side == 0 else 16 * p) % 128
                x = pltpu.roll(x, shift, 1) if shift else x
                total = jnp.where(group == p, x, total)
            tiles[a * 2 + side] = total
        for half in range(2):
            total = zero
            for side in range(2):
                for p, q in enumerate(SIDE_LISTS[2][side]):
                    x = star[b, q, 8 * a : 8 * a + 8, 128 * half : 128 * half + 128]
                    shift = 113 + p if side == 0 else 8 + p
                    x = pltpu.roll(x, shift, 1)
                    total = jnp.where(within == side * 8 + p, x, total)
            tiles[4 + a * 2 + half] = lanes_from(total, order)
    for i, t in enumerate(tiles):
        faces[(2 + b) * 12 + 4 + i] = t
    for d, t in enumerate(pack(tiles)):
        message[b, 8 * d : 8 * d + 8, :] = t


def open_message(message, faces, place):
    def one(b, carry):
        for i in range(8):
            faces[(place + b) * 12 + 4 + i] = unpack(
                lambda d: message[b, 8 * d : 8 * d + 8, :], i, 8
            )
        for tile in range(4):
            faces[(place + b) * 12 + tile, 0:5, :] = message[b, 40 + 5 * tile : 45 + 5 * tile, :]
        return carry

    lax.fori_loop(0, 2, one, 0)


def restrict(faces, down):
    tiles = [t for b in range(2) for t in restrict_block(faces, b)]

    def put(row, t):
        down[row : row + t.shape[0], :] = t

    store_message(tiles, put)


def restrict_block(faces, b):
    row, lane = iotas()
    group, within, low = lane // 16, lane % 16, lane % 8
    second = (lane // 8) % 2
    fine = group * 16 + 2 * low
    coarse = (2 * (group % 4)) * 16
    pair_rows = 2 * (row % 4)
    parts = []
    for side in range(2):
        halves = []
        for half in range(2):
            t = faces[(2 + b) * 12 + side * 2 + half]
            t = t + pltpu.roll(t, 127, 1)
            t = t + pltpu.roll(t, 112, 1)
            halves.append(lanes_from(t, coarse + 2 * low))
        parts.append(jnp.where(group < 4, halves[0], halves[1]))
    tiles = [0.25 * jnp.where(second == 0, parts[0], parts[1])]
    parts = []
    for side in range(2):
        rows = []
        for a in range(2):
            t = faces[(2 + b) * 12 + 4 + a * 2 + side]
            t = t + pltpu.roll(t, 127, 1)
            t = t + pltpu.roll(t, 7, 0)
            rows.append(rows_from(lanes_from(t, fine), pair_rows))
        parts.append(jnp.where(row < 4, rows[0], rows[1]))
    tiles.append(0.25 * jnp.where(second == 0, parts[0], parts[1]))
    rows = []
    for a in range(2):
        halves = []
        for half in range(2):
            t = faces[(2 + b) * 12 + 8 + a * 2 + half]
            t = t + pltpu.roll(t, 127, 1)
            halves.append(lanes_from(t, group * 16 + second * 8 + 2 * (low % 4)))
        t = jnp.where(low < 4, halves[0], halves[1])
        t = t + pltpu.roll(t, 7, 0)
        rows.append(rows_from(t, pair_rows))
    tiles.append(0.25 * jnp.where(row < 4, rows[0], rows[1]))
    return tiles


def member_offset(block, member):
    return jnp.clip(((block >> 1) & (NMEM - 1)) - member + 1, 0, 2)


def slot_of(block, member):
    return member_offset(block, member) * 2 + (block & 1)


NEAR, STATE, UP_SAME, UP_DIRECT, DOWN, DOWN_BLOCK, EDGE, EDGE_THERE, TABLE = (
    0,
    6,
    12,
    18,
    24,
    48,
    72,
    84,
    96,
)


SECTION_SHIFT = NMEM.bit_length()


def read_wanted(link, member, wanted, table, b):
    for axis in range(3):
        for side in range(2):
            i, j = axis * 2 + side, axis * 2 + 1 - side
            code = jnp.int32(-1)
            for k in range(4):
                block = link[b, k, j]
                code = jnp.maximum(code, jnp.where(block >= 0, block * 4 + k, -1))
            table[b * TABLE + STATE + i] = code
            safe = jnp.maximum(code, 0)
            k, block = safe & 3, safe >> 2
            first, last = k >> 1, k & 1
            if axis == 0:
                tile = side * 2 + first
            elif axis == 1:
                tile = 4 + first * 2 + side
            else:
                tile = 8 + k
            wanted[b * 6 + i] = slot_of(block, member) * 12 + tile
            wanted[12 + b * 6 + i] = (2 + (block & 1)) * 12 + tile
            wanted[24 + b * 6 + i] = last


def read_links(nbr, link, level, own, member, table, b):
    for axis in range(3):
        for side in range(2):
            i, j = axis * 2 + side, axis * 2 + 1 - side
            for k in range(4):
                block = link[b, k, j]
                safe = jnp.maximum(block, 0)
                place = (safe >> SECTION_SHIFT) * 3 + member_offset(safe, member)
                table[b * TABLE + DOWN + i * 4 + k] = place
                table[b * TABLE + DOWN_BLOCK + i * 4 + k] = jnp.where(block >= 0, safe & 1, -1)
            code = table[b * TABLE + STATE + i]
            block = jnp.maximum(code, 0) >> 2
            section = block >> SECTION_SHIFT
            near = nbr[b, j]
            table[b * TABLE + NEAR + i] = slot_of(jnp.maximum(near, 0), member) * 12
            linked = jnp.where(code < 0, 3, jnp.where(level[section] < own, 1, 2))
            table[b * TABLE + STATE + i] = jnp.where(near >= 0, 0, linked)
            table[b * TABLE + UP_SAME + i] = section
            table[b * TABLE + UP_DIRECT + i] = section * 3 + member_offset(block, member)
    for q in range(7, 19):
        block = nbr[b, OPPOSITE[q] - 1]
        table[b * TABLE + EDGE + q - 7] = slot_of(jnp.maximum(block, 0), member) * 12
        table[b * TABLE + EDGE_THERE + q - 7] = block


def select_quadrants(faces, ask, out, place, direct):
    lane = iotas()[1]
    second = (lane // 8) % 2
    tiles = []
    for b in range(2):
        for axis in range(3):
            parts = []
            for side in range(2):
                i = b * 6 + axis * 2 + side
                t = faces[ask((12 if direct else 0) + i)]
                if axis < 2:
                    t = pick(ask(24 + i) == side, t, pltpu.roll(t, 8 if side else 120, 1))
                parts.append(t)
            tiles.append(jnp.where(second == 0, parts[0], parts[1]))

    def put(row, t):
        out[place, row : row + t.shape[0], :] = t

    store_message(tiles, put)


def edge_place(q):
    row, lane = iotas()
    group, second = lane // 16, (lane // 8) % 2
    c = VELOCITIES[q]
    one, two = [axis for axis in range(3) if c[axis]]
    side, p = side_of(q, two)
    end, line = (1, 7) if c[one] > 0 else (0, 0)
    if two == 1:
        return two, [(end * 2 + side, (row == line) & (group == p))]
    if one == 0:
        cells = (row == line) & (group == p) & (second == side)
        return two, [(end * 2 + half, cells) for half in range(2)]
    return two, [(a * 2 + end, lane == p * 16 + side * 8 + line) for a in range(2)]


def build_near(faces, halo, b, table):
    row, lane = iotas()
    group, second = lane // 16, (lane // 8) % 2

    def entry(place):
        return table[b * TABLE + place]

    for axis in range(3):
        rest = jnp.where((row if axis == 0 else group) == 0, F32(1.0 / 18.0), F32(1.0 / 36.0))
        for tile in range(4):
            sides = [tile // 2] if axis == 0 else [tile % 2] if axis == 1 else [0, 1]
            parts = []
            for side in sides:
                i = axis * 2 + side
                t = faces[entry(NEAR + i) + axis * 4 + tile]
                parts.append(pick(entry(STATE + i) == 0, t, rest))
            t = parts[0] if axis < 2 else jnp.where(second == 0, parts[0], parts[1])
            rows, lanes = tile_slices(axis, tile)
            halo[b, axis, rows, lanes] = t
    for q in range(7, 19):
        two, places = edge_place(q)
        near, there = entry(EDGE + q - 7) + two * 4, entry(EDGE_THERE + q - 7) >= 0
        for tile, cells in places:
            rows, lanes = tile_slices(two, tile)
            line = faces[near + tile]
            line = pick(there, line, jnp.full_like(line, 1.0 / 36.0))
            halo[b, two, rows, lanes] = jnp.where(cells, line, halo[b, two, rows, lanes])


def build_links(up, down, halo, b, table, direct):
    row, lane = iotas()
    group, within, low = lane // 16, lane % 16, lane % 8
    second = (lane // 8) % 2
    spread_rows = [4 * a + row // 2 for a in range(2)]
    edges = {}
    for q in range(7, 19):
        two, places = edge_place(q)
        for tile, cells in places:
            edges[two, tile] = edges[two, tile] | cells if (two, tile) in edges else cells

    def entry(place):
        return table[b * TABLE + place]

    def means(axis, i, k):
        place, block = entry(DOWN + i * 4 + k), entry(DOWN_BLOCK + i * 4 + k)
        t = message_tile(lambda row: down[place, row : row + 8, :], axis, block)
        return pick(block >= 0, t, jnp.zeros_like(t))

    for axis in range(3):
        states, quads, ups = [], [], []
        for side in range(2):
            i = axis * 2 + side
            states.append(entry(STATE + i))
            place = entry((UP_DIRECT if direct else UP_SAME) + i)
            ups.append(
                message_tile(lambda row, place=place: up[place, row : row + 8, :], axis, b)
            )
            if down is not None:
                quads.append([means(axis, i, k) for k in range(4)])

        def choose(side, old, from_up, from_down):
            state = states[side]
            t = old if from_down is None else pick(state == 2, from_down, old)
            return pick(state == 1, from_up, t)

        def put(tile, old, t):
            if (axis, tile) in edges:
                t = jnp.where(edges[axis, tile], old, t)
            if axis == 2:
                t = lanes_from(t, face_order(lane))
            rows, lanes = tile_slices(axis, tile)
            halo[b, axis, rows, lanes] = t

        def present(tile):
            rows, lanes = tile_slices(axis, tile)
            return halo[b, axis, rows, lanes]

        if axis < 2:
            for side in range(2):
                if axis == 1:
                    wide = lanes_from(ups[side], group * 16 + side * 8 + within // 2)
                for a in range(2):
                    if axis == 0:
                        tile = side * 2 + a
                        from_up = lanes_from(
                            ups[side], (4 * a + group // 2) * 16 + side * 8 + within // 2
                        )
                    else:
                        tile = a * 2 + side
                        from_up = rows_from(wide, spread_rows[a])
                    from_down = None
                    if down is not None:
                        low_part, high_part = quads[side][2 * a], quads[side][2 * a + 1]
                        if side:
                            low_part = pltpu.roll(low_part, 120, 1)
                        else:
                            high_part = pltpu.roll(high_part, 8, 1)
                        from_down = jnp.where(second == 0, low_part, high_part)
                    old = present(tile)
                    put(tile, old, choose(side, old, from_up, from_down))
        else:
            both = jnp.where(second == 0, ups[0], ups[1])
            for half in range(2):
                wide = lanes_from(both, group * 16 + second * 8 + 4 * half + low // 2)
                for a in range(2):
                    tile = a * 2 + half
                    from_up = rows_from(wide, spread_rows[a])
                    old = present(tile)
                    parts = [
                        choose(side, old, from_up, quads[side][tile] if down is not None else None)
                        for side in range(2)
                    ]
                    put(tile, old, jnp.where(second == 0, parts[0], parts[1]))


def roll(x, shift, axis):
    shift %= x.shape[axis]
    return pltpu.roll(x, shift, axis) if shift else x


def ring(left, right, sign):
    lane = iotas(left.shape)[1]
    a, c = roll(left, 16 * sign, 1), roll(right, 16 * sign, 1)
    if sign > 0:
        return [jnp.where(lane < 16, c, a), jnp.where(lane < 16, a, c)]
    return [jnp.where(lane >= 112, c, a), jnp.where(lane >= 112, a, c)]


def drift(star, moved, b, advances):
    for q in range(1, 19):
        c = VELOCITIES[q]
        old = [star[b, q, :, 128 * half : 128 * half + 128] for half in range(2)]
        new = [roll(t, c[0], 0) for t in old]
        if c[1]:
            new = ring(new[0], new[1], c[1])
        for half in range(2):
            t = roll(new[half], c[2], 1)
            moved[b, q, :, 128 * half : 128 * half + 128] = pick(advances, t, old[half])
    moved[b, 0] = star[b, 0]


def finish(moved, halo, out, b, advances, final):
    row, lane = iotas((16, 128))
    row = pick(advances, row, jnp.full_like(row, -1))
    within = pick(advances, lane % 16, jnp.full_like(lane, 8))
    lane = pick(advances, lane, jnp.full_like(lane, 64))
    first, last = lane < 16, lane >= 112

    for q in range(19):
        c = VELOCITIES[q]
        new = [moved[b, q, :, 128 * half : 128 * half + 128] for half in range(2)]
        if c[0]:
            side, p = side_of(q, 0)
            place = side * 8 + p
            plane = [
                halo[b, 0, place : place + 1, 128 * half : 128 * half + 128] for half in range(2)
            ]
            if c[1]:
                plane = ring(plane[0], plane[1], c[1])
            for half in range(2):
                line = roll(plane[half], c[2], 1)
                new[half] = jnp.where(row == (0 if c[0] > 0 else 15), line, new[half])
        if c[1]:
            side, p = side_of(q, 1)
            border = halo[b, 1, :, 128 * side : 128 * side + 128]
            border = roll(border, (-16 * p if side == 0 else 112 - 16 * p) + c[2], 1)
            border = roll(border, c[0], 0)
            new[side] = jnp.where(last if side else first, border, new[side])
        if c[2]:
            side, p = side_of(q, 2)
            borders = []
            for half in range(2):
                border = halo[b, 2, :, 128 * half : 128 * half + 128]
                border = roll(border, -p if side == 0 else 7 - p, 1)
                borders.append(roll(border, c[0], 0))
            if c[1]:
                borders = ring(borders[0], borders[1], c[1])
            for half in range(2):
                new[half] = jnp.where(
                    within == (0 if c[2] > 0 else 15), borders[half], new[half]
                )
        for half in range(2):
            if final:
                for a in range(2):
                    out[q, woven(b, 2 * a + half), :] = new[half][8 * a : 8 * a + 8]
            elif q:
                out[b, q, :, 128 * half : 128 * half + 128] = new[half]


def kernel(
    pop_hbm,
    mask_hbm,
    level_hbm,
    nbr_hbm,
    link_hbm,
    out,
    pop,
    mask_ref,
    level,
    nbr,
    link,
    in_sems,
    star,
    middle,
    faces_a,
    faces_b,
    out_a,
    out_b,
    in_a,
    in_b,
    up_send_a,
    up_send_b,
    up_a,
    up_b,
    down_send,
    down,
    halo,
    table,
    wanted_own,
    wanted,
    wanted_side,
    mem_ss,
    mem_rs,
    side_ss,
    side_rs,
    meta_ss,
    meta_rs,
    up_a_ss,
    up_a_rs,
    up_b_ss,
    up_b_rs,
    down_ss,
    down_rs,
):
    s = lax.axis_index("section")
    m = lax.axis_index("member")
    loads = [
        pltpu.make_async_copy(src, dst, in_sems.at[i])
        for i, (src, dst) in enumerate(
            [
                (link_hbm, link),
                (level_hbm, level),
                (nbr_hbm, nbr),
                (pop_hbm, pop),
                (mask_hbm, mask_ref),
            ]
        )
    ]
    for load in loads:
        load.start()
    has = {-1: m > 0, 0: None, 1: m < NMEM - 1}
    one = jnp.int32(1)
    around = 1 + jnp.where(has[-1], one, 0) + jnp.where(has[1], one, 0)

    def if_member(dm, do):
        if has[dm] is None:
            do()
        else:
            pl.when(has[dm])(do)

    def each(low, high, do):
        def step(i, carry):
            do(i)
            return carry

        lax.fori_loop(low, high, step, 0)

    def blocks(do):
        each(0, 2, do)

    barrier = pltpu.get_barrier_semaphore()

    def greet(other):
        def signal(dm):
            pl.semaphore_signal(barrier, inc=1, device_id=(other, m + dm), device_id_type=MESH)

        pl.when(other != s)(lambda: signal(0))
        for dm in (-1, 1):
            if_member(dm, lambda dm=dm: signal(dm))

    each(0, NSEC, greet)

    def remote(src, dst, send_sem, recv_sem, other, dm):
        return pltpu.make_async_remote_copy(
            src_ref=src,
            dst_ref=dst,
            send_sem=send_sem,
            recv_sem=recv_sem,
            device_id=(other, m + dm),
            device_id_type=MESH,
        )

    def message(ref, place):
        return ref.at[place, pl.ds(0, 34)]

    def meta_copy(src, dst, other):
        return remote(src, dst, meta_ss, meta_rs, other, 0)

    def side_copy(dm, arriving):
        into = (1 + dm) // 2 if arriving else (1 - dm) // 2
        return remote(
            wanted, wanted_side.at[into], side_ss.at[(dm + 1) // 2], side_rs.at[into], s, dm
        )

    def mem_copy(sends, receives, step, dm, arriving):
        into = (1 + dm) // 2 if arriving else (1 - dm) // 2
        return remote(
            sends,
            receives.at[into],
            mem_ss.at[step, (dm + 1) // 2],
            mem_rs.at[step, into],
            s,
            dm,
        )

    def up_a_copy(src, dst, other):
        return remote(src, dst, up_a_ss, up_a_rs, other, 0)

    def up_b_copy(src, dst, other, dm):
        return remote(src, dst, up_b_ss, up_b_rs, other, dm)

    def down_copy(src, dst, other, dm):
        return remote(src, dst, down_ss, down_rs, other, dm)

    singles = tuple(range(1, NSEC))
    groups = tuple(sorted({k * e for k in range(1, NSEC - 1) for e in (2, 3)}))

    def wait_group(count, cases, ref, copy, receive):
        for n in cases:

            @pl.when(count == n)
            def _(n=n):
                whole = ref.at[pl.ds(0, n), pl.ds(0, 34)] if len(ref.shape) == 3 else ref.at[pl.ds(0, n)]
                both = copy(whole, whole)
                both.wait_recv() if receive else both.wait_send()

    below = s
    higher = NSEC - 1 - s
    below_direct = jnp.maximum(s - 1, 0)
    above = jnp.where(s == 0, NSEC, s + 1)
    higher_direct = NSEC - above

    for load in loads[:3]:
        load.wait()
    own = level[s]
    rate = jnp.where(
        own == 0, F32(1.0 / 0.55), jnp.where(own == 1, F32(1.0 / 0.6), F32(1.0 / 0.7))
    )
    blocks(lambda b: read_wanted(link, m, wanted_own, table, b))
    for load in loads[3:]:
        load.wait()

    def first_part(b):
        collide(pop, mask_ref, star, b, rate, own >= 1, True)
        export(star, faces_a, out_a, b)

    blocks(first_part)
    pl.semaphore_wait(barrier, NSEC * around - 1)

    def start_members(sends, receives, step):
        for dm in (-1, 1):
            if_member(dm, lambda dm=dm: mem_copy(sends, receives, step, dm, False).start())

    def receive_members(faces, receives, step):
        for dm in (-1, 1):

            def take(dm=dm):
                mem_copy(out_a, receives, step, dm, True).wait_recv()
                open_message(receives.at[(1 + dm) // 2], faces, 2 + 2 * dm)

            if_member(dm, take)

    each(0, s, lambda other: meta_copy(wanted_own, wanted.at[s], other).start())
    start_members(out_a, in_a, 0)
    restrict(faces_a, down_send)

    def start_down(other):
        for dm in (-1, 0, 1):
            if_member(
                dm,
                lambda dm=dm: down_copy(
                    down_send.at[pl.ds(0, 34)], message(down, s * 3 + 1 - dm), other, dm
                ).start(),
            )

    each(1, s, start_down)
    blocks(lambda b: read_links(nbr, link, level, own, m, table, b))
    receive_members(faces_a, in_a, 0)
    wait_group(higher, singles, wanted, lambda x, y: meta_copy(x, y, s), True)

    def send_up(other):
        select_quadrants(faces_a, lambda i: wanted[other, i], up_send_a, other, False)
        up_a_copy(message(up_send_a, other), message(up_a, s), other).start()

    each(s + 1, NSEC, send_up)
    for dm in (-1, 1):
        if_member(dm, lambda dm=dm: side_copy(dm, False).start())
    def prepare_first(b):
        drift(star, middle, b, own >= 1)
        build_near(faces_a, halo, b, table)

    blocks(prepare_first)
    wait_group(below, singles, up_a, lambda x, y: up_a_copy(x, y, s), True)
    wait_group(
        jnp.where(s == 0, 0, higher) * around,
        groups,
        down,
        lambda x, y: down_copy(x, y, s, 0),
        True,
    )

    def second_part(b):
        build_links(up_a, down, halo, b, table, False)
        finish(middle, halo, middle, b, own >= 1, False)

    blocks(second_part)

    def third_part(b):
        collide(middle, mask_ref, star, b, rate, own == 2, False)
        export(star, faces_b, out_b, b)

    blocks(third_part)
    start_members(out_b, in_b, 1)
    for dm in (-1, 1):
        if_member(dm, lambda dm=dm: side_copy(dm, True).wait_recv())

    def send_direct(other):
        for dm in (-1, 0, 1):

            def send(dm=dm):
                def ask(i):
                    return wanted[other, i] if dm == 0 else wanted_side[(1 + dm) // 2, other, i]

                place = other * 3 + dm + 1
                select_quadrants(faces_b, ask, up_send_b, place, True)
                up_b_copy(
                    message(up_send_b, place), message(up_b, s * 3 + 1 - dm), other, dm
                ).start()

            if_member(dm, send)

    each(above, NSEC, send_direct)
    blocks(lambda b: drift(star, middle, b, own == 2))
    wait_group(below, singles, wanted, lambda x, y: meta_copy(x, y, s), False)
    for dm in (-1, 1):
        if_member(dm, lambda dm=dm: mem_copy(out_a, in_a, 0, dm, False).wait_send())
        if_member(dm, lambda dm=dm: side_copy(dm, False).wait_send())
    wait_group(
        below_direct * around, groups, down, lambda x, y: down_copy(x, y, s, 0), False
    )
    wait_group(higher, singles, up_send_a, lambda x, y: up_a_copy(x, y, s), False)
    receive_members(faces_b, in_b, 1)
    blocks(lambda b: build_near(faces_b, halo, b, table))
    for dm in (-1, 1):
        if_member(dm, lambda dm=dm: mem_copy(out_b, in_b, 1, dm, False).wait_send())
    wait_group(
        higher_direct * around, groups, up_send_b, lambda x, y: up_b_copy(x, y, s, 0), False
    )
    wait_group(
        below_direct * around, groups, up_b, lambda x, y: up_b_copy(x, y, s, 0), True
    )

    def fourth_part(b):
        build_links(up_b, None, halo, b, table, True)
        finish(middle, halo, out, b, own == 2, True)

    blocks(fourth_part)


def body(populations, fluid_mask, section_level, neighbours, interface):
    state = pltpu.VMEM((2, 19, 16, 256), F32)
    faces = pltpu.VMEM((72, 8, 128), F32)
    by_section = pltpu.VMEM((NSEC, 40, 128), F32)
    by_device = pltpu.VMEM((NSEC * 3, 40, 128), F32)
    members = pltpu.VMEM((2, 60, 128), F32)
    arrived = pltpu.VMEM((2, 2, 60, 128), F32)
    vmem = pl.BlockSpec(memory_space=pltpu.VMEM)
    hbm = pl.BlockSpec(memory_space=pltpu.HBM)
    dma = pltpu.SemaphoreType.DMA
    out = pl.pallas_call(
        kernel,
        out_shape=pltpu.VMEM((19, 64, 128), F32),
        in_specs=[hbm] * 5,
        out_specs=vmem,
        scratch_shapes=[
            pltpu.VMEM((19, 64, 128), F32),
            pltpu.VMEM((64, 128), jnp.int32),
            pltpu.SMEM((NSEC,), jnp.int32),
            pltpu.SMEM((2, 18), jnp.int32),
            pltpu.SMEM((2, 4, 6), jnp.int32),
            dma((5,)),
            state,
            state,
            faces,
            faces,
            members,
            members,
            arrived,
            arrived,
            by_section,
            by_device,
            by_section,
            by_device,
            pltpu.VMEM((40, 128), F32),
            by_device,
            pltpu.VMEM((2, 3, 16, 256), F32),
            pltpu.SMEM((2 * TABLE,), jnp.int32),
            pltpu.SMEM((128,), jnp.int32),
            pltpu.SMEM((NSEC, 128), jnp.int32),
            pltpu.SMEM((2, NSEC, 128), jnp.int32),
            dma((2, 2)),
            dma((2, 2)),
            dma((2,)),
            dma((2,)),
        ]
        + [dma] * 8,
        compiler_params=pltpu.CompilerParams(
            collective_id=0, has_side_effects=True, vmem_limit_bytes=54656 * 1024
        ),
        name="lattice_step",
    )(
        populations.reshape(2, 19, 32, 128).transpose(1, 2, 0, 3).reshape(19, 64, 128),
        fluid_mask.reshape(2, 32, 128).transpose(1, 0, 2).reshape(64, 128),
        section_level,
        neighbours,
        interface.transpose(0, 2, 1),
    )
    return out.reshape(19, 32, 2, 128).transpose(2, 0, 1, 3).reshape(2, 19, 4096)


def solution(mesh):
    return jax.shard_map(
        body,
        mesh=mesh,
        in_specs=(
            P(("section", "member"), None, None),
            P(("section", "member"), None),
            P(),
            P(("section", "member"), None),
            P(("section", "member"), None, None),
        ),
        out_specs=P(("section", "member"), None, None),
        check_vma=False,
    )
```

```python
import jax
import jax.numpy as jnp
from jax import lax
from jax.experimental import pallas as pl
from jax.experimental.pallas import tpu as pltpu
from jax.sharding import PartitionSpec as P

MESH = pl.DeviceIdType.MESH
F32 = jnp.float32
NSEC = 8
NMEM = 32

VELOCITIES = (
    (0, 0, 0),
    (1, 0, 0),
    (-1, 0, 0),
    (0, 1, 0),
    (0, -1, 0),
    (0, 0, 1),
    (0, 0, -1),
    (1, 1, 0),
    (-1, -1, 0),
    (1, -1, 0),
    (-1, 1, 0),
    (1, 0, 1),
    (-1, 0, -1),
    (1, 0, -1),
    (-1, 0, 1),
    (0, 1, 1),
    (0, -1, -1),
    (0, 1, -1),
    (0, -1, 1),
)
OPPOSITE = (0, 2, 1, 4, 3, 6, 5, 8, 7, 10, 9, 12, 11, 14, 13, 16, 15, 18, 17)
SIDE_LISTS = tuple(
    tuple(tuple(q for q in range(19) if VELOCITIES[q][axis] == sign) for sign in (1, -1))
    for axis in range(3)
)


def side_of(q, axis):
    side = 0 if VELOCITIES[q][axis] > 0 else 1
    return side, SIDE_LISTS[axis][side].index(q)


def iotas(shape=(8, 128)):
    return lax.broadcasted_iota(jnp.int32, shape, 0), lax.broadcasted_iota(jnp.int32, shape, 1)


def lanes_from(x, index):
    return jnp.take_along_axis(x, index, axis=1)


def rows_from(x, index):
    return jnp.take_along_axis(x, index, axis=0)


def pick(cond, a, b):
    return lax.select(cond, a, b)


def tile_slices(axis, tile):
    first, second = 8 * (tile // 2), 128 * (tile % 2)
    return slice(first, first + 8), slice(second, second + 128)


def packing(count):
    packed = -(-count * 5 // 8)
    spare = [(d, g) for d in range(packed) for g in (5, 6, 7)]
    runs = []
    for source in range(packed, count):
        for group in range(5):
            d, g = spare.pop(0)
            last = runs[-1] if runs else None
            if last and last[0] == source and last[2] == d and last[3] + last[4] == g:
                runs[-1] = last[:4] + (last[4] + 1,)
            else:
                runs.append((source, group, d, g, 1))
    return packed, runs


def lane_roll(x, shift):
    shift %= 128
    return pltpu.roll(x, shift, 1) if shift else x


def pack(tiles):
    lane = iotas()[1]
    packed, runs = packing(len(tiles))
    result = list(tiles[:packed])
    for source, group, d, g, length in runs:
        moved = lane_roll(tiles[source], 16 * (g - group))
        inside = (lane >= 16 * g) & (lane < 16 * (g + length))
        result[d] = jnp.where(inside, moved, result[d])
    return result


def unpack(load, source, count):
    lane = iotas()[1]
    packed, runs = packing(count)
    if source < packed:
        return load(source)
    result = None
    for which, group, d, g, length in runs:
        if which == source:
            moved = lane_roll(load(d), 16 * (group - g))
            result = moved if result is None else jnp.where(lane >= 16 * group, moved, result)
    return result


def store_message(tiles, put):
    for d, t in enumerate(pack([tiles[1], tiles[2], tiles[4], tiles[5]])):
        put(8 * d, t)
    for b in range(2):
        put(24 + 5 * b, tiles[3 * b][0:5])


def message_tile(load, axis, block):
    def tile(b):
        return load(24 + 5 * b) if axis == 0 else unpack(lambda d: load(8 * d), 2 * b + axis - 1, 4)

    return tile(block) if isinstance(block, int) else pick(block == 0, tile(0), tile(1))


def face_order(lane):
    return (lane % 8) * 16 + lane // 8 % 2 * 8 + lane // 16


def woven(b, tile):
    return pl.ds(32 * (tile // 2) + 2 * (tile % 2) + b, 8, stride=4)


def collide(cur, mask_ref, star, b, rate, advances, first):
    for tile in range(4):
        rows, lanes = tile_slices(0, tile)
        if first:
            f = [cur[q, woven(b, tile), :] for q in range(19)]
        else:
            f = [cur[b, q, rows, lanes] for q in range(19)]
        density = f[0]
        for q in range(1, 19):
            density = density + f[q]
        velocity = []
        for axis in range(3):
            plus, minus = SIDE_LISTS[axis]
            momentum = f[plus[0]] - f[minus[0]]
            for i in range(1, 5):
                momentum = momentum + f[plus[i]]
            for i in range(1, 5):
                momentum = momentum - f[minus[i]]
            velocity.append(momentum / density)
        base = 1.0 - 1.5 * (
            velocity[0] * velocity[0] + velocity[1] * velocity[1] + velocity[2] * velocity[2]
        )
        fluid = mask_ref[woven(b, tile), :] == 1
        keep = 1.0 - rate
        scaled = rate * density

        def put(q, relaxed):
            star[b, q, rows, lanes] = pick(
                advances, jnp.where(fluid, relaxed, f[OPPOSITE[q]]), f[q]
            )

        put(0, keep * f[0] + scaled * (1.0 / 3.0) * base)
        axis_weight = scaled * (1.0 / 18.0)
        edge_weight = scaled * (1.0 / 36.0)
        for q in range(1, 19, 2):
            c = VELOCITIES[q]
            along = None
            for axis in range(3):
                if c[axis]:
                    term = velocity[axis] if c[axis] > 0 else -velocity[axis]
                    along = term if along is None else along + term
            weight = axis_weight if q < 7 else edge_weight
            even = weight * (base + 4.5 * along * along)
            odd = weight * (3.0 * along)
            put(q, keep * f[q] + (even + odd))
            put(q + 1, keep * f[q + 1] + (even - odd))


def export(star, faces, message, b):
    row, lane = iotas()
    group, within = lane // 16, lane % 16
    for side in range(2):
        for p, q in enumerate(SIDE_LISTS[0][side]):
            layer = 15 if side == 0 else 0
            for half in range(2):
                line = star[b, q, layer : layer + 1, 128 * half : 128 * half + 128]
                place = side * 2 + half
                faces[(2 + b) * 12 + place, p : p + 1, :] = line
                message[b, 40 + 5 * place + p : 41 + 5 * place + p, :] = line
    zero = jnp.zeros((8, 128), F32)
    tiles = [None] * 8
    order = face_order(lane)
    for a in range(2):
        for side in range(2):
            total = zero
            for p, q in enumerate(SIDE_LISTS[1][side]):
                half = 1 - side
                x = star[b, q, 8 * a : 8 * a + 8, 128 * half : 128 * half + 128]
                shift = (16 * p + 16 if side == 0 else 16 * p) % 128
                x = pltpu.roll(x, shift, 1) if shift else x
                total = jnp.where(group == p, x, total)
            tiles[a * 2 + side] = total
        for half in range(2):
            total = zero
            for side in range(2):
                for p, q in enumerate(SIDE_LISTS[2][side]):
                    x = star[b, q, 8 * a : 8 * a + 8, 128 * half : 128 * half + 128]
                    shift = 113 + p if side == 0 else 8 + p
                    x = pltpu.roll(x, shift, 1)
                    total = jnp.where(within == side * 8 + p, x, total)
            tiles[4 + a * 2 + half] = lanes_from(total, order)
    for i, t in enumerate(tiles):
        faces[(2 + b) * 12 + 4 + i] = t
    for d, t in enumerate(pack(tiles)):
        message[b, 8 * d : 8 * d + 8, :] = t


def open_message(message, faces, place):
    for b in range(2):
        for i in range(8):
            faces[(place + b) * 12 + 4 + i] = unpack(
                lambda d: message[b, 8 * d : 8 * d + 8, :], i, 8
            )
        for tile in range(4):
            faces[(place + b) * 12 + tile, 0:5, :] = message[b, 40 + 5 * tile : 45 + 5 * tile, :]


def restrict(faces, down):
    tiles = [t for b in range(2) for t in restrict_block(faces, b)]

    def put(row, t):
        down[row : row + t.shape[0], :] = t

    store_message(tiles, put)


def restrict_block(faces, b):
    row, lane = iotas()
    group, within, low = lane // 16, lane % 16, lane % 8
    second = (lane // 8) % 2
    fine = group * 16 + 2 * low
    coarse = (2 * (group % 4)) * 16
    pair_rows = 2 * (row % 4)
    parts = []
    for side in range(2):
        halves = []
        for half in range(2):
            t = faces[(2 + b) * 12 + side * 2 + half]
            t = t + pltpu.roll(t, 127, 1)
            t = t + pltpu.roll(t, 112, 1)
            halves.append(lanes_from(t, coarse + 2 * low))
        parts.append(jnp.where(group < 4, halves[0], halves[1]))
    tiles = [0.25 * jnp.where(second == 0, parts[0], parts[1])]
    parts = []
    for side in range(2):
        rows = []
        for a in range(2):
            t = faces[(2 + b) * 12 + 4 + a * 2 + side]
            t = t + pltpu.roll(t, 127, 1)
            t = t + pltpu.roll(t, 7, 0)
            rows.append(rows_from(lanes_from(t, fine), pair_rows))
        parts.append(jnp.where(row < 4, rows[0], rows[1]))
    tiles.append(0.25 * jnp.where(second == 0, parts[0], parts[1]))
    rows = []
    for a in range(2):
        halves = []
        for half in range(2):
            t = faces[(2 + b) * 12 + 8 + a * 2 + half]
            t = t + pltpu.roll(t, 127, 1)
            halves.append(lanes_from(t, group * 16 + second * 8 + 2 * (low % 4)))
        t = jnp.where(low < 4, halves[0], halves[1])
        t = t + pltpu.roll(t, 7, 0)
        rows.append(rows_from(t, pair_rows))
    tiles.append(0.25 * jnp.where(row < 4, rows[0], rows[1]))
    return tiles


def member_offset(block, member):
    return jnp.clip(((block >> 1) & (NMEM - 1)) - member + 1, 0, 2)


def slot_of(block, member):
    return member_offset(block, member) * 2 + (block & 1)


NEAR, STATE, UP_SAME, UP_DIRECT, DOWN, DOWN_BLOCK, EDGE, EDGE_THERE, TABLE = (
    0,
    6,
    12,
    18,
    24,
    48,
    72,
    84,
    96,
)


SECTION_SHIFT = NMEM.bit_length()


def read_wanted(link, member, wanted, table, b):
    for axis in range(3):
        for side in range(2):
            i, j = axis * 2 + side, axis * 2 + 1 - side
            code = jnp.int32(-1)
            for k in range(4):
                block = link[b, k, j]
                code = jnp.maximum(code, jnp.where(block >= 0, block * 4 + k, -1))
            table[b * TABLE + STATE + i] = code
            safe = jnp.maximum(code, 0)
            k, block = safe & 3, safe >> 2
            first, last = k >> 1, k & 1
            if axis == 0:
                tile = side * 2 + first
            elif axis == 1:
                tile = 4 + first * 2 + side
            else:
                tile = 8 + k
            wanted[b * 6 + i] = slot_of(block, member) * 12 + tile
            wanted[12 + b * 6 + i] = (2 + (block & 1)) * 12 + tile
            wanted[24 + b * 6 + i] = last


def read_links(nbr, link, level, own, member, table, b):
    for axis in range(3):
        for side in range(2):
            i, j = axis * 2 + side, axis * 2 + 1 - side
            for k in range(4):
                block = link[b, k, j]
                safe = jnp.maximum(block, 0)
                place = (safe >> SECTION_SHIFT) * 3 + member_offset(safe, member)
                table[b * TABLE + DOWN + i * 4 + k] = place
                table[b * TABLE + DOWN_BLOCK + i * 4 + k] = jnp.where(block >= 0, safe & 1, -1)
            code = table[b * TABLE + STATE + i]
            block = jnp.maximum(code, 0) >> 2
            section = block >> SECTION_SHIFT
            near = nbr[b, j]
            table[b * TABLE + NEAR + i] = slot_of(jnp.maximum(near, 0), member) * 12
            linked = jnp.where(code < 0, 3, jnp.where(level[section] < own, 1, 2))
            table[b * TABLE + STATE + i] = jnp.where(near >= 0, 0, linked)
            table[b * TABLE + UP_SAME + i] = section
            table[b * TABLE + UP_DIRECT + i] = section * 3 + member_offset(block, member)
    for q in range(7, 19):
        block = nbr[b, OPPOSITE[q] - 1]
        table[b * TABLE + EDGE + q - 7] = slot_of(jnp.maximum(block, 0), member) * 12
        table[b * TABLE + EDGE_THERE + q - 7] = block


def select_quadrants(faces, ask, out, place, direct):
    lane = iotas()[1]
    second = (lane // 8) % 2
    tiles = []
    for b in range(2):
        for axis in range(3):
            parts = []
            for side in range(2):
                i = b * 6 + axis * 2 + side
                t = faces[ask((12 if direct else 0) + i)]
                if axis < 2:
                    t = pick(ask(24 + i) == side, t, pltpu.roll(t, 8 if side else 120, 1))
                parts.append(t)
            tiles.append(jnp.where(second == 0, parts[0], parts[1]))

    def put(row, t):
        out[place, row : row + t.shape[0], :] = t

    store_message(tiles, put)


def edge_place(q):
    row, lane = iotas()
    group, second = lane // 16, (lane // 8) % 2
    c = VELOCITIES[q]
    one, two = [axis for axis in range(3) if c[axis]]
    side, p = side_of(q, two)
    end, line = (1, 7) if c[one] > 0 else (0, 0)
    if two == 1:
        return two, [(end * 2 + side, (row == line) & (group == p))]
    if one == 0:
        cells = (row == line) & (group == p) & (second == side)
        return two, [(end * 2 + half, cells) for half in range(2)]
    return two, [(a * 2 + end, lane == p * 16 + side * 8 + line) for a in range(2)]


def build_near(faces, halo, b, table):
    row, lane = iotas()
    group, second = lane // 16, (lane // 8) % 2

    def entry(place):
        return table[b * TABLE + place]

    for axis in range(3):
        rest = jnp.where((row if axis == 0 else group) == 0, F32(1.0 / 18.0), F32(1.0 / 36.0))
        for tile in range(4):
            sides = [tile // 2] if axis == 0 else [tile % 2] if axis == 1 else [0, 1]
            parts = []
            for side in sides:
                i = axis * 2 + side
                t = faces[entry(NEAR + i) + axis * 4 + tile]
                parts.append(pick(entry(STATE + i) == 0, t, rest))
            t = parts[0] if axis < 2 else jnp.where(second == 0, parts[0], parts[1])
            rows, lanes = tile_slices(axis, tile)
            halo[b, axis, rows, lanes] = t
    for q in range(7, 19):
        two, places = edge_place(q)
        near, there = entry(EDGE + q - 7) + two * 4, entry(EDGE_THERE + q - 7) >= 0
        for tile, cells in places:
            rows, lanes = tile_slices(two, tile)
            line = faces[near + tile]
            line = pick(there, line, jnp.full_like(line, 1.0 / 36.0))
            halo[b, two, rows, lanes] = jnp.where(cells, line, halo[b, two, rows, lanes])


def build_links(up, down, halo, b, table, direct):
    row, lane = iotas()
    group, within, low = lane // 16, lane % 16, lane % 8
    second = (lane // 8) % 2
    spread_rows = [4 * a + row // 2 for a in range(2)]
    edges = {}
    for q in range(7, 19):
        two, places = edge_place(q)
        for tile, cells in places:
            edges[two, tile] = edges[two, tile] | cells if (two, tile) in edges else cells

    def entry(place):
        return table[b * TABLE + place]

    def means(axis, i, k):
        place, block = entry(DOWN + i * 4 + k), entry(DOWN_BLOCK + i * 4 + k)
        t = message_tile(lambda row: down[place, row : row + 8, :], axis, block)
        return pick(block >= 0, t, jnp.zeros_like(t))

    for axis in range(3):
        states, quads, ups = [], [], []
        for side in range(2):
            i = axis * 2 + side
            states.append(entry(STATE + i))
            place = entry((UP_DIRECT if direct else UP_SAME) + i)
            ups.append(
                message_tile(lambda row, place=place: up[place, row : row + 8, :], axis, b)
            )
            if down is not None:
                quads.append([means(axis, i, k) for k in range(4)])

        def choose(side, old, from_up, from_down):
            state = states[side]
            t = old if from_down is None else pick(state == 2, from_down, old)
            return pick(state == 1, from_up, t)

        def put(tile, old, t):
            if (axis, tile) in edges:
                t = jnp.where(edges[axis, tile], old, t)
            if axis == 2:
                t = lanes_from(t, face_order(lane))
            rows, lanes = tile_slices(axis, tile)
            halo[b, axis, rows, lanes] = t

        def present(tile):
            rows, lanes = tile_slices(axis, tile)
            return halo[b, axis, rows, lanes]

        if axis < 2:
            for side in range(2):
                if axis == 1:
                    wide = lanes_from(ups[side], group * 16 + side * 8 + within // 2)
                for a in range(2):
                    if axis == 0:
                        tile = side * 2 + a
                        from_up = lanes_from(
                            ups[side], (4 * a + group // 2) * 16 + side * 8 + within // 2
                        )
                    else:
                        tile = a * 2 + side
                        from_up = rows_from(wide, spread_rows[a])
                    from_down = None
                    if down is not None:
                        low_part, high_part = quads[side][2 * a], quads[side][2 * a + 1]
                        if side:
                            low_part = pltpu.roll(low_part, 120, 1)
                        else:
                            high_part = pltpu.roll(high_part, 8, 1)
                        from_down = jnp.where(second == 0, low_part, high_part)
                    old = present(tile)
                    put(tile, old, choose(side, old, from_up, from_down))
        else:
            both = jnp.where(second == 0, ups[0], ups[1])
            for half in range(2):
                wide = lanes_from(both, group * 16 + second * 8 + 4 * half + low // 2)
                for a in range(2):
                    tile = a * 2 + half
                    from_up = rows_from(wide, spread_rows[a])
                    old = present(tile)
                    parts = [
                        choose(side, old, from_up, quads[side][tile] if down is not None else None)
                        for side in range(2)
                    ]
                    put(tile, old, jnp.where(second == 0, parts[0], parts[1]))


def roll(x, shift, axis):
    shift %= x.shape[axis]
    return pltpu.roll(x, shift, axis) if shift else x


def ring(left, right, sign):
    lane = iotas(left.shape)[1]
    a, c = roll(left, 16 * sign, 1), roll(right, 16 * sign, 1)
    if sign > 0:
        return [jnp.where(lane < 16, c, a), jnp.where(lane < 16, a, c)]
    return [jnp.where(lane >= 112, c, a), jnp.where(lane >= 112, a, c)]


def drift(star, moved, b, advances):
    for q in range(1, 19):
        c = VELOCITIES[q]
        old = [star[b, q, :, 128 * half : 128 * half + 128] for half in range(2)]
        new = [roll(t, c[0], 0) for t in old]
        if c[1]:
            new = ring(new[0], new[1], c[1])
        for half in range(2):
            t = roll(new[half], c[2], 1)
            moved[b, q, :, 128 * half : 128 * half + 128] = pick(advances, t, old[half])
    moved[b, 0] = star[b, 0]


def finish(moved, halo, out, b, advances, final):
    row, lane = iotas((16, 128))
    row = pick(advances, row, jnp.full_like(row, -1))
    within = pick(advances, lane % 16, jnp.full_like(lane, 8))
    lane = pick(advances, lane, jnp.full_like(lane, 64))
    first, last = lane < 16, lane >= 112

    for q in range(19):
        c = VELOCITIES[q]
        new = [moved[b, q, :, 128 * half : 128 * half + 128] for half in range(2)]
        if c[0]:
            side, p = side_of(q, 0)
            place = side * 8 + p
            plane = [
                halo[b, 0, place : place + 1, 128 * half : 128 * half + 128] for half in range(2)
            ]
            if c[1]:
                plane = ring(plane[0], plane[1], c[1])
            for half in range(2):
                line = roll(plane[half], c[2], 1)
                new[half] = jnp.where(row == (0 if c[0] > 0 else 15), line, new[half])
        if c[1]:
            side, p = side_of(q, 1)
            border = halo[b, 1, :, 128 * side : 128 * side + 128]
            border = roll(border, (-16 * p if side == 0 else 112 - 16 * p) + c[2], 1)
            border = roll(border, c[0], 0)
            new[side] = jnp.where(last if side else first, border, new[side])
        if c[2]:
            side, p = side_of(q, 2)
            borders = []
            for half in range(2):
                border = halo[b, 2, :, 128 * half : 128 * half + 128]
                border = roll(border, -p if side == 0 else 7 - p, 1)
                borders.append(roll(border, c[0], 0))
            if c[1]:
                borders = ring(borders[0], borders[1], c[1])
            for half in range(2):
                new[half] = jnp.where(
                    within == (0 if c[2] > 0 else 15), borders[half], new[half]
                )
        for half in range(2):
            if final:
                for a in range(2):
                    out[q, woven(b, 2 * a + half), :] = new[half][8 * a : 8 * a + 8]
            elif q:
                out[b, q, :, 128 * half : 128 * half + 128] = new[half]


def kernel(
    pop_hbm,
    mask_hbm,
    level_hbm,
    nbr_hbm,
    link_hbm,
    out,
    pop,
    mask_ref,
    level,
    nbr,
    link,
    in_sems,
    star,
    middle,
    faces_a,
    faces_b,
    out_a,
    out_b,
    in_a,
    in_b,
    up_send_a,
    up_send_b,
    up_a,
    up_b,
    down_send,
    down,
    halo,
    table,
    wanted_own,
    wanted,
    wanted_side,
    mem_ss,
    mem_rs,
    side_ss,
    side_rs,
    meta_ss,
    meta_rs,
    up_a_ss,
    up_a_rs,
    up_b_ss,
    up_b_rs,
    down_ss,
    down_rs,
):
    s = lax.axis_index("section")
    m = lax.axis_index("member")
    loads = [
        pltpu.make_async_copy(src, dst, in_sems.at[i])
        for i, (src, dst) in enumerate(
            [
                (link_hbm, link),
                (level_hbm, level),
                (nbr_hbm, nbr),
                (pop_hbm, pop),
                (mask_hbm, mask_ref),
            ]
        )
    ]
    for load in loads:
        load.start()
    has = {-1: m > 0, 0: None, 1: m < NMEM - 1}
    one = jnp.int32(1)
    around = 1 + jnp.where(has[-1], one, 0) + jnp.where(has[1], one, 0)

    def if_member(dm, do):
        if has[dm] is None:
            do()
        else:
            pl.when(has[dm])(do)

    def each(low, high, do):
        def step(i, carry):
            do(i)
            return carry

        lax.fori_loop(low, high, step, 0)

    def blocks(do):
        for b in range(2):
            do(b)

    barrier = pltpu.get_barrier_semaphore()

    def greet(other):
        def signal(dm):
            pl.semaphore_signal(barrier, inc=1, device_id=(other, m + dm), device_id_type=MESH)

        pl.when(other != s)(lambda: signal(0))
        for dm in (-1, 1):
            if_member(dm, lambda dm=dm: signal(dm))

    each(0, NSEC, greet)

    def remote(src, dst, send_sem, recv_sem, other, dm):
        return pltpu.make_async_remote_copy(
            src_ref=src,
            dst_ref=dst,
            send_sem=send_sem,
            recv_sem=recv_sem,
            device_id=(other, m + dm),
            device_id_type=MESH,
        )

    def message(ref, place):
        return ref.at[place, pl.ds(0, 34)]

    def meta_copy(src, dst, other):
        return remote(src, dst, meta_ss, meta_rs, other, 0)

    def side_copy(dm, arriving):
        into = (1 + dm) // 2 if arriving else (1 - dm) // 2
        return remote(
            wanted, wanted_side.at[into], side_ss.at[(dm + 1) // 2], side_rs.at[into], s, dm
        )

    def mem_copy(sends, receives, step, dm, arriving):
        into = (1 + dm) // 2 if arriving else (1 - dm) // 2
        return remote(
            sends,
            receives.at[into],
            mem_ss.at[step, (dm + 1) // 2],
            mem_rs.at[step, into],
            s,
            dm,
        )

    def up_a_copy(src, dst, other):
        return remote(src, dst, up_a_ss, up_a_rs, other, 0)

    def up_b_copy(src, dst, other, dm):
        return remote(src, dst, up_b_ss, up_b_rs, other, dm)

    def down_copy(src, dst, other, dm):
        return remote(src, dst, down_ss, down_rs, other, dm)

    singles = tuple(range(1, NSEC))
    groups = tuple(sorted({k * e for k in range(1, NSEC - 1) for e in (2, 3)}))

    def wait_group(count, cases, ref, copy, receive):
        for n in cases:

            @pl.when(count == n)
            def _(n=n):
                whole = ref.at[pl.ds(0, n), pl.ds(0, 34)] if len(ref.shape) == 3 else ref.at[pl.ds(0, n)]
                both = copy(whole, whole)
                both.wait_recv() if receive else both.wait_send()

    below = s
    higher = NSEC - 1 - s
    below_direct = jnp.maximum(s - 1, 0)
    above = jnp.where(s == 0, NSEC, s + 1)
    higher_direct = NSEC - above

    for load in loads[:3]:
        load.wait()
    own = level[s]
    rate = jnp.where(
        own == 0, F32(1.0 / 0.55), jnp.where(own == 1, F32(1.0 / 0.6), F32(1.0 / 0.7))
    )
    blocks(lambda b: read_wanted(link, m, wanted_own, table, b))
    for load in loads[3:]:
        load.wait()

    def first_part(b):
        collide(pop, mask_ref, star, b, rate, own >= 1, True)
        export(star, faces_a, out_a, b)

    blocks(first_part)
    pl.semaphore_wait(barrier, NSEC * around - 1)

    def start_members(sends, receives, step):
        for dm in (-1, 1):
            if_member(dm, lambda dm=dm: mem_copy(sends, receives, step, dm, False).start())

    def receive_members(faces, receives, step):
        for dm in (-1, 1):

            def take(dm=dm):
                mem_copy(out_a, receives, step, dm, True).wait_recv()
                open_message(receives.at[(1 + dm) // 2], faces, 2 + 2 * dm)

            if_member(dm, take)

    each(0, s, lambda other: meta_copy(wanted_own, wanted.at[s], other).start())
    start_members(out_a, in_a, 0)
    restrict(faces_a, down_send)

    def start_down(other):
        for dm in (-1, 0, 1):
            if_member(
                dm,
                lambda dm=dm: down_copy(
                    down_send.at[pl.ds(0, 34)], message(down, s * 3 + 1 - dm), other, dm
                ).start(),
            )

    each(1, s, start_down)
    blocks(lambda b: read_links(nbr, link, level, own, m, table, b))
    receive_members(faces_a, in_a, 0)
    wait_group(higher, singles, wanted, lambda x, y: meta_copy(x, y, s), True)

    def send_up(other):
        select_quadrants(faces_a, lambda i: wanted[other, i], up_send_a, other, False)
        up_a_copy(message(up_send_a, other), message(up_a, s), other).start()

    each(s + 1, NSEC, send_up)
    for dm in (-1, 1):
        if_member(dm, lambda dm=dm: side_copy(dm, False).start())
    def prepare_first(b):
        drift(star, middle, b, own >= 1)
        build_near(faces_a, halo, b, table)

    blocks(prepare_first)
    wait_group(below, singles, up_a, lambda x, y: up_a_copy(x, y, s), True)
    wait_group(
        jnp.where(s == 0, 0, higher) * around,
        groups,
        down,
        lambda x, y: down_copy(x, y, s, 0),
        True,
    )

    def second_part(b):
        build_links(up_a, down, halo, b, table, False)
        finish(middle, halo, middle, b, own >= 1, False)

    blocks(second_part)

    def third_part(b):
        collide(middle, mask_ref, star, b, rate, own == 2, False)
        export(star, faces_b, out_b, b)

    blocks(third_part)
    start_members(out_b, in_b, 1)
    for dm in (-1, 1):
        if_member(dm, lambda dm=dm: side_copy(dm, True).wait_recv())

    def send_direct(other):
        for dm in (-1, 0, 1):

            def send(dm=dm):
                def ask(i):
                    return wanted[other, i] if dm == 0 else wanted_side[(1 + dm) // 2, other, i]

                place = other * 3 + dm + 1
                select_quadrants(faces_b, ask, up_send_b, place, True)
                up_b_copy(
                    message(up_send_b, place), message(up_b, s * 3 + 1 - dm), other, dm
                ).start()

            if_member(dm, send)

    each(above, NSEC, send_direct)
    blocks(lambda b: drift(star, middle, b, own == 2))
    wait_group(below, singles, wanted, lambda x, y: meta_copy(x, y, s), False)
    for dm in (-1, 1):
        if_member(dm, lambda dm=dm: mem_copy(out_a, in_a, 0, dm, False).wait_send())
        if_member(dm, lambda dm=dm: side_copy(dm, False).wait_send())
    wait_group(
        below_direct * around, groups, down, lambda x, y: down_copy(x, y, s, 0), False
    )
    wait_group(higher, singles, up_send_a, lambda x, y: up_a_copy(x, y, s), False)
    receive_members(faces_b, in_b, 1)
    blocks(lambda b: build_near(faces_b, halo, b, table))
    for dm in (-1, 1):
        if_member(dm, lambda dm=dm: mem_copy(out_b, in_b, 1, dm, False).wait_send())
    wait_group(
        higher_direct * around, groups, up_send_b, lambda x, y: up_b_copy(x, y, s, 0), False
    )
    wait_group(
        below_direct * around, groups, up_b, lambda x, y: up_b_copy(x, y, s, 0), True
    )

    def fourth_part(b):
        build_links(up_b, None, halo, b, table, True)
        finish(middle, halo, out, b, own == 2, True)

    blocks(fourth_part)


def body(populations, fluid_mask, section_level, neighbours, interface):
    state = pltpu.VMEM((2, 19, 16, 256), F32)
    faces = pltpu.VMEM((72, 8, 128), F32)
    by_section = pltpu.VMEM((NSEC, 40, 128), F32)
    by_device = pltpu.VMEM((NSEC * 3, 40, 128), F32)
    members = pltpu.VMEM((2, 60, 128), F32)
    arrived = pltpu.VMEM((2, 2, 60, 128), F32)
    vmem = pl.BlockSpec(memory_space=pltpu.VMEM)
    hbm = pl.BlockSpec(memory_space=pltpu.HBM)
    dma = pltpu.SemaphoreType.DMA
    out = pl.pallas_call(
        kernel,
        out_shape=pltpu.VMEM((19, 64, 128), F32),
        in_specs=[hbm] * 5,
        out_specs=vmem,
        scratch_shapes=[
            pltpu.VMEM((19, 64, 128), F32),
            pltpu.VMEM((64, 128), jnp.int32),
            pltpu.SMEM((NSEC,), jnp.int32),
            pltpu.SMEM((2, 18), jnp.int32),
            pltpu.SMEM((2, 4, 6), jnp.int32),
            dma((5,)),
            state,
            state,
            faces,
            faces,
            members,
            members,
            arrived,
            arrived,
            by_section,
            by_device,
            by_section,
            by_device,
            pltpu.VMEM((40, 128), F32),
            by_device,
            pltpu.VMEM((2, 3, 16, 256), F32),
            pltpu.SMEM((2 * TABLE,), jnp.int32),
            pltpu.SMEM((128,), jnp.int32),
            pltpu.SMEM((NSEC, 128), jnp.int32),
            pltpu.SMEM((2, NSEC, 128), jnp.int32),
            dma((2, 2)),
            dma((2, 2)),
            dma((2,)),
            dma((2,)),
        ]
        + [dma] * 8,
        compiler_params=pltpu.CompilerParams(
            collective_id=0, has_side_effects=True, vmem_limit_bytes=54656 * 1024
        ),
        name="lattice_step",
    )(
        populations.reshape(2, 19, 32, 128).transpose(1, 2, 0, 3).reshape(19, 64, 128),
        fluid_mask.reshape(2, 32, 128).transpose(1, 0, 2).reshape(64, 128),
        section_level,
        neighbours,
        interface.transpose(0, 2, 1),
    )
    return out.reshape(19, 32, 2, 128).transpose(2, 0, 1, 3).reshape(2, 19, 4096)


def solution(mesh):
    return jax.shard_map(
        body,
        mesh=mesh,
        in_specs=(
            P(("section", "member"), None, None),
            P(("section", "member"), None),
            P(),
            P(("section", "member"), None),
            P(("section", "member"), None, None),
        ),
        out_specs=P(("section", "member"), None, None),
        check_vma=False,
    )
```

```python
import jax
import jax.numpy as jnp
from jax import lax
from jax.experimental import pallas as pl
from jax.experimental.pallas import tpu as pltpu
from jax.sharding import PartitionSpec as P

MESH = pl.DeviceIdType.MESH
F32 = jnp.float32
NSEC = 8
NMEM = 32

VELOCITIES = (
    (0, 0, 0),
    (1, 0, 0),
    (-1, 0, 0),
    (0, 1, 0),
    (0, -1, 0),
    (0, 0, 1),
    (0, 0, -1),
    (1, 1, 0),
    (-1, -1, 0),
    (1, -1, 0),
    (-1, 1, 0),
    (1, 0, 1),
    (-1, 0, -1),
    (1, 0, -1),
    (-1, 0, 1),
    (0, 1, 1),
    (0, -1, -1),
    (0, 1, -1),
    (0, -1, 1),
)
OPPOSITE = (0, 2, 1, 4, 3, 6, 5, 8, 7, 10, 9, 12, 11, 14, 13, 16, 15, 18, 17)
SIDE_LISTS = tuple(
    tuple(tuple(q for q in range(19) if VELOCITIES[q][axis] == sign) for sign in (1, -1))
    for axis in range(3)
)


def side_of(q, axis):
    side = 0 if VELOCITIES[q][axis] > 0 else 1
    return side, SIDE_LISTS[axis][side].index(q)


def iotas(shape=(8, 128)):
    return lax.broadcasted_iota(jnp.int32, shape, 0), lax.broadcasted_iota(jnp.int32, shape, 1)


def lanes_from(x, index):
    return jnp.take_along_axis(x, index, axis=1)


def rows_from(x, index):
    return jnp.take_along_axis(x, index, axis=0)


def pick(cond, a, b):
    return lax.select(cond, a, b)


def tile_slices(axis, tile):
    first, second = 8 * (tile // 2), 128 * (tile % 2)
    return slice(first, first + 8), slice(second, second + 128)


def packing(count):
    packed = -(-count * 5 // 8)
    spare = [(d, g) for d in range(packed) for g in (5, 6, 7)]
    runs = []
    for source in range(packed, count):
        for group in range(5):
            d, g = spare.pop(0)
            last = runs[-1] if runs else None
            if last and last[0] == source and last[2] == d and last[3] + last[4] == g:
                runs[-1] = last[:4] + (last[4] + 1,)
            else:
                runs.append((source, group, d, g, 1))
    return packed, runs


def lane_roll(x, shift):
    shift %= 128
    return pltpu.roll(x, shift, 1) if shift else x


def pack(tiles):
    lane = iotas()[1]
    packed, runs = packing(len(tiles))
    result = list(tiles[:packed])
    for source, group, d, g, length in runs:
        moved = lane_roll(tiles[source], 16 * (g - group))
        inside = (lane >= 16 * g) & (lane < 16 * (g + length))
        result[d] = jnp.where(inside, moved, result[d])
    return result


def unpack(load, source, count):
    lane = iotas()[1]
    packed, runs = packing(count)
    if source < packed:
        return load(source)
    result = None
    for which, group, d, g, length in runs:
        if which == source:
            moved = lane_roll(load(d), 16 * (group - g))
            result = moved if result is None else jnp.where(lane >= 16 * group, moved, result)
    return result


def store_message(tiles, put):
    for d, t in enumerate(pack([tiles[1], tiles[2], tiles[4], tiles[5]])):
        put(8 * d, t)
    for b in range(2):
        put(24 + 5 * b, tiles[3 * b][0:5])


def message_tile(load, axis, block):
    def tile(b):
        return load(24 + 5 * b) if axis == 0 else unpack(lambda d: load(8 * d), 2 * b + axis - 1, 4)

    return tile(block) if isinstance(block, int) else pick(block == 0, tile(0), tile(1))


def face_order(lane):
    return (lane % 8) * 16 + lane // 8 % 2 * 8 + lane // 16


def woven(b, tile):
    return pl.ds(32 * (tile // 2) + 2 * (tile % 2) + b, 8, stride=4)


def collide(cur, mask_ref, star, b, rate, advances, first):
    for tile in range(4):
        rows, lanes = tile_slices(0, tile)
        if first:
            f = [cur[q, woven(b, tile), :] for q in range(19)]
        else:
            f = [cur[b, q, rows, lanes] for q in range(19)]
        density = f[0]
        for q in range(1, 19):
            density = density + f[q]
        velocity = []
        for axis in range(3):
            plus, minus = SIDE_LISTS[axis]
            momentum = f[plus[0]] - f[minus[0]]
            for i in range(1, 5):
                momentum = momentum + f[plus[i]]
            for i in range(1, 5):
                momentum = momentum - f[minus[i]]
            velocity.append(momentum / density)
        base = 1.0 - 1.5 * (
            velocity[0] * velocity[0] + velocity[1] * velocity[1] + velocity[2] * velocity[2]
        )
        fluid = mask_ref[woven(b, tile), :] == 1
        keep = 1.0 - rate
        scaled = rate * density

        def put(q, relaxed):
            star[b, q, rows, lanes] = pick(
                advances, jnp.where(fluid, relaxed, f[OPPOSITE[q]]), f[q]
            )

        put(0, keep * f[0] + scaled * (1.0 / 3.0) * base)
        axis_weight = scaled * (1.0 / 18.0)
        edge_weight = scaled * (1.0 / 36.0)
        for q in range(1, 19, 2):
            c = VELOCITIES[q]
            along = None
            for axis in range(3):
                if c[axis]:
                    term = velocity[axis] if c[axis] > 0 else -velocity[axis]
                    along = term if along is None else along + term
            weight = axis_weight if q < 7 else edge_weight
            even = weight * (base + 4.5 * along * along)
            odd = weight * (3.0 * along)
            put(q, keep * f[q] + (even + odd))
            put(q + 1, keep * f[q + 1] + (even - odd))


def export(star, faces, message, b):
    row, lane = iotas()
    group, within = lane // 16, lane % 16
    for side in range(2):
        for p, q in enumerate(SIDE_LISTS[0][side]):
            layer = 15 if side == 0 else 0
            for half in range(2):
                line = star[b, q, layer : layer + 1, 128 * half : 128 * half + 128]
                place = side * 2 + half
                faces[(2 + b) * 12 + place, p : p + 1, :] = line
                message[b, 40 + 5 * place + p : 41 + 5 * place + p, :] = line
    zero = jnp.zeros((8, 128), F32)
    tiles = [None] * 8
    order = face_order(lane)
    for a in range(2):
        for side in range(2):
            total = zero
            for p, q in enumerate(SIDE_LISTS[1][side]):
                half = 1 - side
                x = star[b, q, 8 * a : 8 * a + 8, 128 * half : 128 * half + 128]
                shift = (16 * p + 16 if side == 0 else 16 * p) % 128
                x = pltpu.roll(x, shift, 1) if shift else x
                total = jnp.where(group == p, x, total)
            tiles[a * 2 + side] = total
        for half in range(2):
            total = zero
            for side in range(2):
                for p, q in enumerate(SIDE_LISTS[2][side]):
                    x = star[b, q, 8 * a : 8 * a + 8, 128 * half : 128 * half + 128]
                    shift = 113 + p if side == 0 else 8 + p
                    x = pltpu.roll(x, shift, 1)
                    total = jnp.where(within == side * 8 + p, x, total)
            tiles[4 + a * 2 + half] = lanes_from(total, order)
    for i, t in enumerate(tiles):
        faces[(2 + b) * 12 + 4 + i] = t
    for d, t in enumerate(pack(tiles)):
        message[b, 8 * d : 8 * d + 8, :] = t


def open_message(message, faces, place):
    for b in range(2):
        for i in range(8):
            faces[(place + b) * 12 + 4 + i] = unpack(
                lambda d: message[b, 8 * d : 8 * d + 8, :], i, 8
            )
        for tile in range(4):
            faces[(place + b) * 12 + tile, 0:5, :] = message[b, 40 + 5 * tile : 45 + 5 * tile, :]


def restrict(faces, down):
    tiles = [t for b in range(2) for t in restrict_block(faces, b)]

    def put(row, t):
        down[row : row + t.shape[0], :] = t

    store_message(tiles, put)


def restrict_block(faces, b):
    row, lane = iotas()
    group, within, low = lane // 16, lane % 16, lane % 8
    second = (lane // 8) % 2
    fine = group * 16 + 2 * low
    coarse = (2 * (group % 4)) * 16
    pair_rows = 2 * (row % 4)
    parts = []
    for side in range(2):
        halves = []
        for half in range(2):
            t = faces[(2 + b) * 12 + side * 2 + half]
            t = t + pltpu.roll(t, 127, 1)
            t = t + pltpu.roll(t, 112, 1)
            halves.append(lanes_from(t, coarse + 2 * low))
        parts.append(jnp.where(group < 4, halves[0], halves[1]))
    tiles = [0.25 * jnp.where(second == 0, parts[0], parts[1])]
    parts = []
    for side in range(2):
        rows = []
        for a in range(2):
            t = faces[(2 + b) * 12 + 4 + a * 2 + side]
            t = t + pltpu.roll(t, 127, 1)
            t = t + pltpu.roll(t, 7, 0)
            rows.append(rows_from(lanes_from(t, fine), pair_rows))
        parts.append(jnp.where(row < 4, rows[0], rows[1]))
    tiles.append(0.25 * jnp.where(second == 0, parts[0], parts[1]))
    rows = []
    for a in range(2):
        halves = []
        for half in range(2):
            t = faces[(2 + b) * 12 + 8 + a * 2 + half]
            t = t + pltpu.roll(t, 127, 1)
            halves.append(lanes_from(t, group * 16 + second * 8 + 2 * (low % 4)))
        t = jnp.where(low < 4, halves[0], halves[1])
        t = t + pltpu.roll(t, 7, 0)
        rows.append(rows_from(t, pair_rows))
    tiles.append(0.25 * jnp.where(row < 4, rows[0], rows[1]))
    return tiles


def member_offset(block, member):
    return jnp.clip(((block >> 1) & (NMEM - 1)) - member + 1, 0, 2)


def slot_of(block, member):
    return member_offset(block, member) * 2 + (block & 1)


NEAR, STATE, UP_SAME, UP_DIRECT, DOWN, DOWN_BLOCK, EDGE, EDGE_THERE, TABLE = (
    0,
    6,
    12,
    18,
    24,
    48,
    72,
    84,
    96,
)


SECTION_SHIFT = NMEM.bit_length()


def read_wanted(link, member, wanted, table, b):
    for axis in range(3):
        for side in range(2):
            i, j = axis * 2 + side, axis * 2 + 1 - side
            code = jnp.int32(-1)
            for k in range(4):
                block = link[b, k, j]
                code = jnp.maximum(code, jnp.where(block >= 0, block * 4 + k, -1))
            table[b * TABLE + STATE + i] = code
            safe = jnp.maximum(code, 0)
            k, block = safe & 3, safe >> 2
            first, last = k >> 1, k & 1
            if axis == 0:
                tile = side * 2 + first
            elif axis == 1:
                tile = 4 + first * 2 + side
            else:
                tile = 8 + k
            wanted[b * 6 + i] = slot_of(block, member) * 12 + tile
            wanted[12 + b * 6 + i] = (2 + (block & 1)) * 12 + tile
            wanted[24 + b * 6 + i] = last


def read_links(nbr, link, level, own, member, table, b):
    for axis in range(3):
        for side in range(2):
            i, j = axis * 2 + side, axis * 2 + 1 - side
            for k in range(4):
                block = link[b, k, j]
                safe = jnp.maximum(block, 0)
                place = (safe >> SECTION_SHIFT) * 3 + member_offset(safe, member)
                table[b * TABLE + DOWN + i * 4 + k] = place
                table[b * TABLE + DOWN_BLOCK + i * 4 + k] = jnp.where(block >= 0, safe & 1, -1)
            code = table[b * TABLE + STATE + i]
            block = jnp.maximum(code, 0) >> 2
            section = block >> SECTION_SHIFT
            near = nbr[b, j]
            table[b * TABLE + NEAR + i] = slot_of(jnp.maximum(near, 0), member) * 12
            linked = jnp.where(code < 0, 3, jnp.where(level[section] < own, 1, 2))
            table[b * TABLE + STATE + i] = jnp.where(near >= 0, 0, linked)
            table[b * TABLE + UP_SAME + i] = section
            table[b * TABLE + UP_DIRECT + i] = section * 3 + member_offset(block, member)
    for q in range(7, 19):
        block = nbr[b, OPPOSITE[q] - 1]
        table[b * TABLE + EDGE + q - 7] = slot_of(jnp.maximum(block, 0), member) * 12
        table[b * TABLE + EDGE_THERE + q - 7] = block


def select_quadrants(faces, ask, out, place, direct):
    lane = iotas()[1]
    second = (lane // 8) % 2
    tiles = []
    for b in range(2):
        for axis in range(3):
            parts = []
            for side in range(2):
                i = b * 6 + axis * 2 + side
                t = faces[ask((12 if direct else 0) + i)]
                if axis < 2:
                    t = pick(ask(24 + i) == side, t, pltpu.roll(t, 8 if side else 120, 1))
                parts.append(t)
            tiles.append(jnp.where(second == 0, parts[0], parts[1]))

    def put(row, t):
        out[place, row : row + t.shape[0], :] = t

    store_message(tiles, put)


def edge_place(q):
    row, lane = iotas()
    group, second = lane // 16, (lane // 8) % 2
    c = VELOCITIES[q]
    one, two = [axis for axis in range(3) if c[axis]]
    side, p = side_of(q, two)
    end, line = (1, 7) if c[one] > 0 else (0, 0)
    if two == 1:
        return two, [(end * 2 + side, (row == line) & (group == p))]
    if one == 0:
        cells = (row == line) & (group == p) & (second == side)
        return two, [(end * 2 + half, cells) for half in range(2)]
    return two, [(a * 2 + end, lane == p * 16 + side * 8 + line) for a in range(2)]


def build_near(faces, halo, b, table):
    row, lane = iotas()
    group, second = lane // 16, (lane // 8) % 2

    def entry(place):
        return table[b * TABLE + place]

    for axis in range(3):
        rest = jnp.where((row if axis == 0 else group) == 0, F32(1.0 / 18.0), F32(1.0 / 36.0))
        for tile in range(4):
            sides = [tile // 2] if axis == 0 else [tile % 2] if axis == 1 else [0, 1]
            parts = []
            for side in sides:
                i = axis * 2 + side
                t = faces[entry(NEAR + i) + axis * 4 + tile]
                parts.append(pick(entry(STATE + i) == 0, t, rest))
            t = parts[0] if axis < 2 else jnp.where(second == 0, parts[0], parts[1])
            rows, lanes = tile_slices(axis, tile)
            halo[b, axis, rows, lanes] = t
    for q in range(7, 19):
        two, places = edge_place(q)
        near, there = entry(EDGE + q - 7) + two * 4, entry(EDGE_THERE + q - 7) >= 0
        for tile, cells in places:
            rows, lanes = tile_slices(two, tile)
            line = faces[near + tile]
            line = pick(there, line, jnp.full_like(line, 1.0 / 36.0))
            halo[b, two, rows, lanes] = jnp.where(cells, line, halo[b, two, rows, lanes])


def build_links(up, down, halo, b, table, direct):
    row, lane = iotas()
    group, within, low = lane // 16, lane % 16, lane % 8
    second = (lane // 8) % 2
    spread_rows = [4 * a + row // 2 for a in range(2)]
    edges = {}
    for q in range(7, 19):
        two, places = edge_place(q)
        for tile, cells in places:
            edges[two, tile] = edges[two, tile] | cells if (two, tile) in edges else cells

    def entry(place):
        return table[b * TABLE + place]

    def means(axis, i, k):
        place, block = entry(DOWN + i * 4 + k), entry(DOWN_BLOCK + i * 4 + k)
        t = message_tile(lambda row: down[place, row : row + 8, :], axis, block)
        return pick(block >= 0, t, jnp.zeros_like(t))

    for axis in range(3):
        states, quads, ups = [], [], []
        for side in range(2):
            i = axis * 2 + side
            states.append(entry(STATE + i))
            place = entry((UP_DIRECT if direct else UP_SAME) + i)
            ups.append(
                message_tile(lambda row, place=place: up[place, row : row + 8, :], axis, b)
            )
            if down is not None:
                quads.append([means(axis, i, k) for k in range(4)])

        def choose(side, old, from_up, from_down):
            state = states[side]
            t = old if from_down is None else pick(state == 2, from_down, old)
            return pick(state == 1, from_up, t)

        def put(tile, old, t):
            if (axis, tile) in edges:
                t = jnp.where(edges[axis, tile], old, t)
            if axis == 2:
                t = lanes_from(t, face_order(lane))
            rows, lanes = tile_slices(axis, tile)
            halo[b, axis, rows, lanes] = t

        def present(tile):
            rows, lanes = tile_slices(axis, tile)
            return halo[b, axis, rows, lanes]

        if axis < 2:
            for side in range(2):
                if axis == 1:
                    wide = lanes_from(ups[side], group * 16 + side * 8 + within // 2)
                for a in range(2):
                    if axis == 0:
                        tile = side * 2 + a
                        from_up = lanes_from(
                            ups[side], (4 * a + group // 2) * 16 + side * 8 + within // 2
                        )
                    else:
                        tile = a * 2 + side
                        from_up = rows_from(wide, spread_rows[a])
                    from_down = None
                    if down is not None:
                        low_part, high_part = quads[side][2 * a], quads[side][2 * a + 1]
                        if side:
                            low_part = pltpu.roll(low_part, 120, 1)
                        else:
                            high_part = pltpu.roll(high_part, 8, 1)
                        from_down = jnp.where(second == 0, low_part, high_part)
                    old = present(tile)
                    put(tile, old, choose(side, old, from_up, from_down))
        else:
            both = jnp.where(second == 0, ups[0], ups[1])
            for half in range(2):
                wide = lanes_from(both, group * 16 + second * 8 + 4 * half + low // 2)
                for a in range(2):
                    tile = a * 2 + half
                    from_up = rows_from(wide, spread_rows[a])
                    old = present(tile)
                    parts = [
                        choose(side, old, from_up, quads[side][tile] if down is not None else None)
                        for side in range(2)
                    ]
                    put(tile, old, jnp.where(second == 0, parts[0], parts[1]))


def roll(x, shift, axis):
    shift %= x.shape[axis]
    return pltpu.roll(x, shift, axis) if shift else x


def ring(left, right, sign):
    lane = iotas(left.shape)[1]
    a, c = roll(left, 16 * sign, 1), roll(right, 16 * sign, 1)
    if sign > 0:
        return [jnp.where(lane < 16, c, a), jnp.where(lane < 16, a, c)]
    return [jnp.where(lane >= 112, c, a), jnp.where(lane >= 112, a, c)]


def drift(star, moved, b, advances):
    for q in range(1, 19):
        c = VELOCITIES[q]
        old = [star[b, q, :, 128 * half : 128 * half + 128] for half in range(2)]
        new = [roll(t, c[0], 0) for t in old]
        if c[1]:
            new = ring(new[0], new[1], c[1])
        for half in range(2):
            t = roll(new[half], c[2], 1)
            moved[b, q, :, 128 * half : 128 * half + 128] = pick(advances, t, old[half])
    moved[b, 0] = star[b, 0]


def finish(moved, halo, out, b, advances, final):
    row, lane = iotas((16, 128))
    row = pick(advances, row, jnp.full_like(row, -1))
    within = pick(advances, lane % 16, jnp.full_like(lane, 8))
    lane = pick(advances, lane, jnp.full_like(lane, 64))
    first, last = lane < 16, lane >= 112

    for q in range(19):
        c = VELOCITIES[q]
        new = [moved[b, q, :, 128 * half : 128 * half + 128] for half in range(2)]
        if c[0]:
            side, p = side_of(q, 0)
            place = side * 8 + p
            plane = [
                halo[b, 0, place : place + 1, 128 * half : 128 * half + 128] for half in range(2)
            ]
            if c[1]:
                plane = ring(plane[0], plane[1], c[1])
            for half in range(2):
                line = roll(plane[half], c[2], 1)
                new[half] = jnp.where(row == (0 if c[0] > 0 else 15), line, new[half])
        if c[1]:
            side, p = side_of(q, 1)
            border = halo[b, 1, :, 128 * side : 128 * side + 128]
            border = roll(border, (-16 * p if side == 0 else 112 - 16 * p) + c[2], 1)
            border = roll(border, c[0], 0)
            new[side] = jnp.where(last if side else first, border, new[side])
        if c[2]:
            side, p = side_of(q, 2)
            borders = []
            for half in range(2):
                border = halo[b, 2, :, 128 * half : 128 * half + 128]
                border = roll(border, -p if side == 0 else 7 - p, 1)
                borders.append(roll(border, c[0], 0))
            if c[1]:
                borders = ring(borders[0], borders[1], c[1])
            for half in range(2):
                new[half] = jnp.where(
                    within == (0 if c[2] > 0 else 15), borders[half], new[half]
                )
        for half in range(2):
            if final:
                for a in range(2):
                    out[q, woven(b, 2 * a + half), :] = new[half][8 * a : 8 * a + 8]
            elif q:
                out[b, q, :, 128 * half : 128 * half + 128] = new[half]


def kernel(
    pop_hbm,
    mask_hbm,
    level_hbm,
    nbr_hbm,
    link_hbm,
    out,
    pop,
    mask_ref,
    level,
    nbr,
    link,
    in_sems,
    star,
    middle,
    faces_a,
    faces_b,
    out_a,
    out_b,
    in_a,
    in_b,
    up_send_a,
    up_send_b,
    up_a,
    up_b,
    down_send,
    down,
    halo,
    table,
    wanted_own,
    wanted,
    wanted_side,
    mem_ss,
    mem_rs,
    side_ss,
    side_rs,
    meta_ss,
    meta_rs,
    up_a_ss,
    up_a_rs,
    up_b_ss,
    up_b_rs,
    down_ss,
    down_rs,
):
    s = lax.axis_index("section")
    m = lax.axis_index("member")
    loads = [
        pltpu.make_async_copy(src, dst, in_sems.at[i])
        for i, (src, dst) in enumerate(
            [
                (link_hbm, link),
                (level_hbm, level),
                (nbr_hbm, nbr),
                (pop_hbm, pop),
                (mask_hbm, mask_ref),
            ]
        )
    ]
    for load in loads:
        load.start()
    has = {-1: m > 0, 0: None, 1: m < NMEM - 1}
    one = jnp.int32(1)
    around = 1 + jnp.where(has[-1], one, 0) + jnp.where(has[1], one, 0)

    def if_member(dm, do):
        if has[dm] is None:
            do()
        else:
            pl.when(has[dm])(do)

    def each(low, high, do):
        def step(i, carry):
            do(i)
            return carry

        lax.fori_loop(low, high, step, 0)

    def blocks(do):
        for b in range(2):
            do(b)

    barrier = pltpu.get_barrier_semaphore()

    def greet(other):
        def signal(dm):
            pl.semaphore_signal(barrier, inc=1, device_id=(other, m + dm), device_id_type=MESH)

        pl.when(other != s)(lambda: signal(0))
        for dm in (-1, 1):
            if_member(dm, lambda dm=dm: signal(dm))

    each(0, NSEC, greet)

    def remote(src, dst, send_sem, recv_sem, other, dm):
        return pltpu.make_async_remote_copy(
            src_ref=src,
            dst_ref=dst,
            send_sem=send_sem,
            recv_sem=recv_sem,
            device_id=(other, m + dm),
            device_id_type=MESH,
        )

    def message(ref, place):
        return ref.at[place, pl.ds(0, 34)]

    def meta_copy(src, dst, other):
        return remote(src, dst, meta_ss, meta_rs, other, 0)

    def side_copy(dm, arriving):
        into = (1 + dm) // 2 if arriving else (1 - dm) // 2
        return remote(
            wanted, wanted_side.at[into], side_ss.at[(dm + 1) // 2], side_rs.at[into], s, dm
        )

    def mem_copy(sends, receives, step, dm, arriving):
        into = (1 + dm) // 2 if arriving else (1 - dm) // 2
        return remote(
            sends,
            receives.at[into],
            mem_ss.at[step, (dm + 1) // 2],
            mem_rs.at[step, into],
            s,
            dm,
        )

    def up_a_copy(src, dst, other):
        return remote(src, dst, up_a_ss, up_a_rs, other, 0)

    def up_b_copy(src, dst, other, dm):
        return remote(src, dst, up_b_ss, up_b_rs, other, dm)

    def down_copy(src, dst, other, dm):
        return remote(src, dst, down_ss, down_rs, other, dm)

    singles = tuple(range(1, NSEC))
    groups = tuple(sorted({k * e for k in range(1, NSEC - 1) for e in (2, 3)}))

    def wait_group(count, cases, ref, copy, receive):
        for n in cases:

            @pl.when(count == n)
            def _(n=n):
                whole = ref.at[pl.ds(0, n), pl.ds(0, 34)] if len(ref.shape) == 3 else ref.at[pl.ds(0, n)]
                both = copy(whole, whole)
                both.wait_recv() if receive else both.wait_send()

    below = s
    higher = NSEC - 1 - s
    below_direct = jnp.maximum(s - 1, 0)
    above = jnp.where(s == 0, NSEC, s + 1)
    higher_direct = NSEC - above

    for load in loads[:3]:
        load.wait()
    own = level[s]
    rate = jnp.where(
        own == 0, F32(1.0 / 0.55), jnp.where(own == 1, F32(1.0 / 0.6), F32(1.0 / 0.7))
    )
    blocks(lambda b: read_wanted(link, m, wanted_own, table, b))
    for load in loads[3:]:
        load.wait()

    def first_part(b):
        collide(pop, mask_ref, star, b, rate, own >= 1, True)
        export(star, faces_a, out_a, b)

    blocks(first_part)
    pl.semaphore_wait(barrier, NSEC * around - 1)

    def start_members(sends, receives, step):
        for dm in (-1, 1):
            if_member(dm, lambda dm=dm: mem_copy(sends, receives, step, dm, False).start())

    def receive_members(faces, receives, step):
        for dm in (-1, 1):
            if_member(dm, lambda dm=dm: mem_copy(out_a, receives, step, dm, True).wait_recv())
        for dm in (-1, 1):
            open_message(receives.at[(1 + dm) // 2], faces, 2 + 2 * dm)

    each(0, s, lambda other: meta_copy(wanted_own, wanted.at[s], other).start())
    start_members(out_a, in_a, 0)
    restrict(faces_a, down_send)

    def start_down(other):
        for dm in (-1, 0, 1):
            if_member(
                dm,
                lambda dm=dm: down_copy(
                    down_send.at[pl.ds(0, 34)], message(down, s * 3 + 1 - dm), other, dm
                ).start(),
            )

    each(1, s, start_down)
    blocks(lambda b: read_links(nbr, link, level, own, m, table, b))
    receive_members(faces_a, in_a, 0)
    wait_group(higher, singles, wanted, lambda x, y: meta_copy(x, y, s), True)

    def send_up(other):
        select_quadrants(faces_a, lambda i: wanted[other, i], up_send_a, other, False)
        up_a_copy(message(up_send_a, other), message(up_a, s), other).start()

    each(s + 1, NSEC, send_up)
    for dm in (-1, 1):
        if_member(dm, lambda dm=dm: side_copy(dm, False).start())
    def prepare_first(b):
        drift(star, middle, b, own >= 1)
        build_near(faces_a, halo, b, table)

    blocks(prepare_first)
    wait_group(below, singles, up_a, lambda x, y: up_a_copy(x, y, s), True)
    wait_group(
        jnp.where(s == 0, 0, higher) * around,
        groups,
        down,
        lambda x, y: down_copy(x, y, s, 0),
        True,
    )

    blocks(lambda b: build_links(up_a, down, halo, b, table, False))
    blocks(lambda b: finish(middle, halo, middle, b, own >= 1, False))
    blocks(lambda b: collide(middle, mask_ref, star, b, rate, own == 2, False))
    blocks(lambda b: export(star, faces_b, out_b, b))
    start_members(out_b, in_b, 1)
    for dm in (-1, 1):
        if_member(dm, lambda dm=dm: side_copy(dm, True).wait_recv())

    def send_direct(other):
        for dm in (-1, 0, 1):

            def send(dm=dm):
                def ask(i):
                    return wanted[other, i] if dm == 0 else wanted_side[(1 + dm) // 2, other, i]

                place = other * 3 + dm + 1
                select_quadrants(faces_b, ask, up_send_b, place, True)
                up_b_copy(
                    message(up_send_b, place), message(up_b, s * 3 + 1 - dm), other, dm
                ).start()

            if_member(dm, send)

    each(above, NSEC, send_direct)
    blocks(lambda b: drift(star, middle, b, own == 2))
    wait_group(below, singles, wanted, lambda x, y: meta_copy(x, y, s), False)
    for dm in (-1, 1):
        if_member(dm, lambda dm=dm: mem_copy(out_a, in_a, 0, dm, False).wait_send())
        if_member(dm, lambda dm=dm: side_copy(dm, False).wait_send())
    wait_group(
        below_direct * around, groups, down, lambda x, y: down_copy(x, y, s, 0), False
    )
    wait_group(higher, singles, up_send_a, lambda x, y: up_a_copy(x, y, s), False)
    receive_members(faces_b, in_b, 1)
    blocks(lambda b: build_near(faces_b, halo, b, table))
    for dm in (-1, 1):
        if_member(dm, lambda dm=dm: mem_copy(out_b, in_b, 1, dm, False).wait_send())
    wait_group(
        higher_direct * around, groups, up_send_b, lambda x, y: up_b_copy(x, y, s, 0), False
    )
    wait_group(
        below_direct * around, groups, up_b, lambda x, y: up_b_copy(x, y, s, 0), True
    )

    blocks(lambda b: build_links(up_b, None, halo, b, table, True))
    blocks(lambda b: finish(middle, halo, out, b, own == 2, True))


def body(populations, fluid_mask, section_level, neighbours, interface):
    state = pltpu.VMEM((2, 19, 16, 256), F32)
    faces = pltpu.VMEM((72, 8, 128), F32)
    by_section = pltpu.VMEM((NSEC, 40, 128), F32)
    by_device = pltpu.VMEM((NSEC * 3, 40, 128), F32)
    members = pltpu.VMEM((2, 60, 128), F32)
    arrived = pltpu.VMEM((2, 2, 60, 128), F32)
    vmem = pl.BlockSpec(memory_space=pltpu.VMEM)
    hbm = pl.BlockSpec(memory_space=pltpu.HBM)
    dma = pltpu.SemaphoreType.DMA
    out = pl.pallas_call(
        kernel,
        out_shape=pltpu.VMEM((19, 64, 128), F32),
        in_specs=[hbm] * 5,
        out_specs=vmem,
        scratch_shapes=[
            pltpu.VMEM((19, 64, 128), F32),
            pltpu.VMEM((64, 128), jnp.int32),
            pltpu.SMEM((NSEC,), jnp.int32),
            pltpu.SMEM((2, 18), jnp.int32),
            pltpu.SMEM((2, 4, 6), jnp.int32),
            dma((5,)),
            state,
            state,
            faces,
            faces,
            members,
            members,
            arrived,
            arrived,
            by_section,
            by_device,
            by_section,
            by_device,
            pltpu.VMEM((40, 128), F32),
            by_device,
            pltpu.VMEM((2, 3, 16, 256), F32),
            pltpu.SMEM((2 * TABLE,), jnp.int32),
            pltpu.SMEM((128,), jnp.int32),
            pltpu.SMEM((NSEC, 128), jnp.int32),
            pltpu.SMEM((2, NSEC, 128), jnp.int32),
            dma((2, 2)),
            dma((2, 2)),
            dma((2,)),
            dma((2,)),
        ]
        + [dma] * 8,
        compiler_params=pltpu.CompilerParams(
            collective_id=0, has_side_effects=True, vmem_limit_bytes=54656 * 1024
        ),
        name="lattice_step",
    )(
        populations.reshape(2, 19, 32, 128).transpose(1, 2, 0, 3).reshape(19, 64, 128),
        fluid_mask.reshape(2, 32, 128).transpose(1, 0, 2).reshape(64, 128),
        section_level,
        neighbours,
        interface.transpose(0, 2, 1),
    )
    return out.reshape(19, 32, 2, 128).transpose(2, 0, 1, 3).reshape(2, 19, 4096)


def solution(mesh):
    return jax.shard_map(
        body,
        mesh=mesh,
        in_specs=(
            P(("section", "member"), None, None),
            P(("section", "member"), None),
            P(),
            P(("section", "member"), None),
            P(("section", "member"), None, None),
        ),
        out_specs=P(("section", "member"), None, None),
        check_vma=False,
    )
```

```python
import jax
import jax.numpy as jnp
from jax import lax
from jax.experimental import pallas as pl
from jax.experimental.pallas import tpu as pltpu
from jax.sharding import PartitionSpec as P

MESH = pl.DeviceIdType.MESH
F32 = jnp.float32
NSEC = 8
NMEM = 32

VELOCITIES = (
    (0, 0, 0),
    (1, 0, 0),
    (-1, 0, 0),
    (0, 1, 0),
    (0, -1, 0),
    (0, 0, 1),
    (0, 0, -1),
    (1, 1, 0),
    (-1, -1, 0),
    (1, -1, 0),
    (-1, 1, 0),
    (1, 0, 1),
    (-1, 0, -1),
    (1, 0, -1),
    (-1, 0, 1),
    (0, 1, 1),
    (0, -1, -1),
    (0, 1, -1),
    (0, -1, 1),
)
OPPOSITE = (0, 2, 1, 4, 3, 6, 5, 8, 7, 10, 9, 12, 11, 14, 13, 16, 15, 18, 17)
SIDE_LISTS = tuple(
    tuple(tuple(q for q in range(19) if VELOCITIES[q][axis] == sign) for sign in (1, -1))
    for axis in range(3)
)


def side_of(q, axis):
    side = 0 if VELOCITIES[q][axis] > 0 else 1
    return side, SIDE_LISTS[axis][side].index(q)


def iotas(shape=(8, 128)):
    return lax.broadcasted_iota(jnp.int32, shape, 0), lax.broadcasted_iota(jnp.int32, shape, 1)


def lanes_from(x, index):
    return jnp.take_along_axis(x, index, axis=1)


def rows_from(x, index):
    return jnp.take_along_axis(x, index, axis=0)


def pick(cond, a, b):
    return lax.select(cond, a, b)


def tile_slices(axis, tile):
    first, second = 8 * (tile // 2), 128 * (tile % 2)
    return slice(first, first + 8), slice(second, second + 128)


def packing(count):
    packed = -(-count * 5 // 8)
    spare = [(d, g) for d in range(packed) for g in (5, 6, 7)]
    runs = []
    for source in range(packed, count):
        for group in range(5):
            d, g = spare.pop(0)
            last = runs[-1] if runs else None
            if last and last[0] == source and last[2] == d and last[3] + last[4] == g:
                runs[-1] = last[:4] + (last[4] + 1,)
            else:
                runs.append((source, group, d, g, 1))
    return packed, runs


def lane_roll(x, shift):
    shift %= 128
    return pltpu.roll(x, shift, 1) if shift else x


def pack(tiles):
    lane = iotas()[1]
    packed, runs = packing(len(tiles))
    result = list(tiles[:packed])
    for source, group, d, g, length in runs:
        moved = lane_roll(tiles[source], 16 * (g - group))
        inside = (lane >= 16 * g) & (lane < 16 * (g + length))
        result[d] = jnp.where(inside, moved, result[d])
    return result


def unpack(load, source, count):
    lane = iotas()[1]
    packed, runs = packing(count)
    if source < packed:
        return load(source)
    result = None
    for which, group, d, g, length in runs:
        if which == source:
            moved = lane_roll(load(d), 16 * (group - g))
            result = moved if result is None else jnp.where(lane >= 16 * group, moved, result)
    return result


def store_message(tiles, put):
    for d, t in enumerate(pack([tiles[1], tiles[2], tiles[4], tiles[5]])):
        put(8 * d, t)
    for b in range(2):
        put(24 + 5 * b, tiles[3 * b][0:5])


def message_tile(load, axis, block):
    def tile(b):
        return load(24 + 5 * b) if axis == 0 else unpack(lambda d: load(8 * d), 2 * b + axis - 1, 4)

    return tile(block) if isinstance(block, int) else pick(block == 0, tile(0), tile(1))


def face_order(lane):
    return (lane % 8) * 16 + lane // 8 % 2 * 8 + lane // 16


def woven(b, tile):
    return pl.ds(32 * (tile // 2) + 2 * (tile % 2) + b, 8, stride=4)


def collide(cur, mask_ref, star, b, rate, advances, first):
    for tile in range(4):
        rows, lanes = tile_slices(0, tile)
        if first:
            f = [cur[q, woven(b, tile), :] for q in range(19)]
        else:
            f = [cur[b, q, rows, lanes] for q in range(19)]
        density = f[0]
        for q in range(1, 19):
            density = density + f[q]
        velocity = []
        for axis in range(3):
            plus, minus = SIDE_LISTS[axis]
            momentum = f[plus[0]] - f[minus[0]]
            for i in range(1, 5):
                momentum = momentum + f[plus[i]]
            for i in range(1, 5):
                momentum = momentum - f[minus[i]]
            velocity.append(momentum / density)
        base = 1.0 - 1.5 * (
            velocity[0] * velocity[0] + velocity[1] * velocity[1] + velocity[2] * velocity[2]
        )
        fluid = mask_ref[woven(b, tile), :] == 1
        keep = 1.0 - rate
        scaled = rate * density

        def put(q, relaxed):
            star[b, q, rows, lanes] = pick(
                advances, jnp.where(fluid, relaxed, f[OPPOSITE[q]]), f[q]
            )

        put(0, keep * f[0] + scaled * (1.0 / 3.0) * base)
        axis_weight = scaled * (1.0 / 18.0)
        edge_weight = scaled * (1.0 / 36.0)
        for q in range(1, 19, 2):
            c = VELOCITIES[q]
            along = None
            for axis in range(3):
                if c[axis]:
                    term = velocity[axis] if c[axis] > 0 else -velocity[axis]
                    along = term if along is None else along + term
            weight = axis_weight if q < 7 else edge_weight
            even = weight * (base + 4.5 * along * along)
            odd = weight * (3.0 * along)
            put(q, keep * f[q] + (even + odd))
            put(q + 1, keep * f[q + 1] + (even - odd))


def export(star, faces, message, b):
    row, lane = iotas()
    group, within = lane // 16, lane % 16
    for side in range(2):
        for p, q in enumerate(SIDE_LISTS[0][side]):
            layer = 15 if side == 0 else 0
            for half in range(2):
                line = star[b, q, layer : layer + 1, 128 * half : 128 * half + 128]
                place = side * 2 + half
                faces[(2 + b) * 12 + place, p : p + 1, :] = line
                message[b, 40 + 5 * place + p : 41 + 5 * place + p, :] = line
    zero = jnp.zeros((8, 128), F32)
    tiles = [None] * 8
    order = face_order(lane)
    for a in range(2):
        for side in range(2):
            total = zero
            for p, q in enumerate(SIDE_LISTS[1][side]):
                half = 1 - side
                x = star[b, q, 8 * a : 8 * a + 8, 128 * half : 128 * half + 128]
                shift = (16 * p + 16 if side == 0 else 16 * p) % 128
                x = pltpu.roll(x, shift, 1) if shift else x
                total = jnp.where(group == p, x, total)
            tiles[a * 2 + side] = total
        for half in range(2):
            total = zero
            for side in range(2):
                for p, q in enumerate(SIDE_LISTS[2][side]):
                    x = star[b, q, 8 * a : 8 * a + 8, 128 * half : 128 * half + 128]
                    shift = 113 + p if side == 0 else 8 + p
                    x = pltpu.roll(x, shift, 1)
                    total = jnp.where(within == side * 8 + p, x, total)
            tiles[4 + a * 2 + half] = lanes_from(total, order)
    for i, t in enumerate(tiles):
        faces[(2 + b) * 12 + 4 + i] = t
    for d, t in enumerate(pack(tiles)):
        message[b, 8 * d : 8 * d + 8, :] = t


def open_message(message, faces, place):
    for b in range(2):
        for i in range(8):
            faces[(place + b) * 12 + 4 + i] = unpack(
                lambda d: message[b, 8 * d : 8 * d + 8, :], i, 8
            )
        for tile in range(4):
            faces[(place + b) * 12 + tile, 0:5, :] = message[b, 40 + 5 * tile : 45 + 5 * tile, :]


def restrict(faces, down):
    tiles = [t for b in range(2) for t in restrict_block(faces, b)]

    def put(row, t):
        down[row : row + t.shape[0], :] = t

    store_message(tiles, put)


def restrict_block(faces, b):
    row, lane = iotas()
    group, within, low = lane // 16, lane % 16, lane % 8
    second = (lane // 8) % 2
    fine = group * 16 + 2 * low
    coarse = (2 * (group % 4)) * 16
    pair_rows = 2 * (row % 4)
    parts = []
    for side in range(2):
        halves = []
        for half in range(2):
            t = faces[(2 + b) * 12 + side * 2 + half]
            t = t + pltpu.roll(t, 127, 1)
            t = t + pltpu.roll(t, 112, 1)
            halves.append(lanes_from(t, coarse + 2 * low))
        parts.append(jnp.where(group < 4, halves[0], halves[1]))
    tiles = [0.25 * jnp.where(second == 0, parts[0], parts[1])]
    parts = []
    for side in range(2):
        rows = []
        for a in range(2):
            t = faces[(2 + b) * 12 + 4 + a * 2 + side]
            t = t + pltpu.roll(t, 127, 1)
            t = t + pltpu.roll(t, 7, 0)
            rows.append(rows_from(lanes_from(t, fine), pair_rows))
        parts.append(jnp.where(row < 4, rows[0], rows[1]))
    tiles.append(0.25 * jnp.where(second == 0, parts[0], parts[1]))
    rows = []
    for a in range(2):
        halves = []
        for half in range(2):
            t = faces[(2 + b) * 12 + 8 + a * 2 + half]
            t = t + pltpu.roll(t, 127, 1)
            halves.append(lanes_from(t, group * 16 + second * 8 + 2 * (low % 4)))
        t = jnp.where(low < 4, halves[0], halves[1])
        t = t + pltpu.roll(t, 7, 0)
        rows.append(rows_from(t, pair_rows))
    tiles.append(0.25 * jnp.where(row < 4, rows[0], rows[1]))
    return tiles


def member_offset(block, member):
    return jnp.clip(((block >> 1) & (NMEM - 1)) - member + 1, 0, 2)


def slot_of(block, member):
    return member_offset(block, member) * 2 + (block & 1)


NEAR, STATE, UP_SAME, UP_DIRECT, DOWN, DOWN_BLOCK, EDGE, EDGE_THERE, TABLE = (
    0,
    6,
    12,
    18,
    24,
    48,
    72,
    84,
    96,
)


SECTION_SHIFT = NMEM.bit_length()


def read_wanted(link, member, wanted, table, b):
    for axis in range(3):
        for side in range(2):
            i, j = axis * 2 + side, axis * 2 + 1 - side
            code = jnp.int32(-1)
            for k in range(4):
                block = link[b, k, j]
                code = jnp.maximum(code, jnp.where(block >= 0, block * 4 + k, -1))
            table[b * TABLE + STATE + i] = code
            safe = jnp.maximum(code, 0)
            k, block = safe & 3, safe >> 2
            first, last = k >> 1, k & 1
            if axis == 0:
                tile = side * 2 + first
            elif axis == 1:
                tile = 4 + first * 2 + side
            else:
                tile = 8 + k
            wanted[b * 6 + i] = slot_of(block, member) * 12 + tile
            wanted[12 + b * 6 + i] = (2 + (block & 1)) * 12 + tile
            wanted[24 + b * 6 + i] = last


def read_links(nbr, link, level, own, member, table, b):
    for axis in range(3):
        for side in range(2):
            i, j = axis * 2 + side, axis * 2 + 1 - side
            for k in range(4):
                block = link[b, k, j]
                safe = jnp.maximum(block, 0)
                place = (safe >> SECTION_SHIFT) * 3 + member_offset(safe, member)
                table[b * TABLE + DOWN + i * 4 + k] = place
                table[b * TABLE + DOWN_BLOCK + i * 4 + k] = jnp.where(block >= 0, safe & 1, -1)
            code = table[b * TABLE + STATE + i]
            block = jnp.maximum(code, 0) >> 2
            section = block >> SECTION_SHIFT
            near = nbr[b, j]
            table[b * TABLE + NEAR + i] = slot_of(jnp.maximum(near, 0), member) * 12
            linked = jnp.where(code < 0, 3, jnp.where(level[section] < own, 1, 2))
            table[b * TABLE + STATE + i] = jnp.where(near >= 0, 0, linked)
            table[b * TABLE + UP_SAME + i] = section
            table[b * TABLE + UP_DIRECT + i] = section * 3 + member_offset(block, member)
    for q in range(7, 19):
        block = nbr[b, OPPOSITE[q] - 1]
        table[b * TABLE + EDGE + q - 7] = slot_of(jnp.maximum(block, 0), member) * 12
        table[b * TABLE + EDGE_THERE + q - 7] = block


def select_quadrants(faces, ask, out, place, direct):
    lane = iotas()[1]
    second = (lane // 8) % 2
    tiles = []
    for b in range(2):
        for axis in range(3):
            parts = []
            for side in range(2):
                i = b * 6 + axis * 2 + side
                t = faces[ask((12 if direct else 0) + i)]
                if axis < 2:
                    t = pick(ask(24 + i) == side, t, pltpu.roll(t, 8 if side else 120, 1))
                parts.append(t)
            tiles.append(jnp.where(second == 0, parts[0], parts[1]))

    def put(row, t):
        out[place, row : row + t.shape[0], :] = t

    store_message(tiles, put)


def edge_place(q):
    row, lane = iotas()
    group, second = lane // 16, (lane // 8) % 2
    c = VELOCITIES[q]
    one, two = [axis for axis in range(3) if c[axis]]
    side, p = side_of(q, two)
    end, line = (1, 7) if c[one] > 0 else (0, 0)
    if two == 1:
        return two, [(end * 2 + side, (row == line) & (group == p))]
    if one == 0:
        cells = (row == line) & (group == p) & (second == side)
        return two, [(end * 2 + half, cells) for half in range(2)]
    return two, [(a * 2 + end, lane == p * 16 + side * 8 + line) for a in range(2)]


def build_near(faces, halo, b, table):
    row, lane = iotas()
    group, second = lane // 16, (lane // 8) % 2

    def entry(place):
        return table[b * TABLE + place]

    for axis in range(3):
        rest = jnp.where((row if axis == 0 else group) == 0, F32(1.0 / 18.0), F32(1.0 / 36.0))
        for tile in range(4):
            sides = [tile // 2] if axis == 0 else [tile % 2] if axis == 1 else [0, 1]
            parts = []
            for side in sides:
                i = axis * 2 + side
                t = faces[entry(NEAR + i) + axis * 4 + tile]
                parts.append(pick(entry(STATE + i) == 0, t, rest))
            t = parts[0] if axis < 2 else jnp.where(second == 0, parts[0], parts[1])
            rows, lanes = tile_slices(axis, tile)
            halo[b, axis, rows, lanes] = t
    for q in range(7, 19):
        two, places = edge_place(q)
        near, there = entry(EDGE + q - 7) + two * 4, entry(EDGE_THERE + q - 7) >= 0
        for tile, cells in places:
            rows, lanes = tile_slices(two, tile)
            line = faces[near + tile]
            line = pick(there, line, jnp.full_like(line, 1.0 / 36.0))
            halo[b, two, rows, lanes] = jnp.where(cells, line, halo[b, two, rows, lanes])


def build_links(up, down, halo, b, table, direct):
    row, lane = iotas()
    group, within, low = lane // 16, lane % 16, lane % 8
    second = (lane // 8) % 2
    spread_rows = [4 * a + row // 2 for a in range(2)]
    edges = {}
    for q in range(7, 19):
        two, places = edge_place(q)
        for tile, cells in places:
            edges[two, tile] = edges[two, tile] | cells if (two, tile) in edges else cells

    def entry(place):
        return table[b * TABLE + place]

    def means(axis, i, k):
        place, block = entry(DOWN + i * 4 + k), entry(DOWN_BLOCK + i * 4 + k)
        t = message_tile(lambda row: down[place, row : row + 8, :], axis, block)
        return pick(block >= 0, t, jnp.zeros_like(t))

    for axis in range(3):
        states, quads, ups = [], [], []
        for side in range(2):
            i = axis * 2 + side
            states.append(entry(STATE + i))
            place = entry((UP_DIRECT if direct else UP_SAME) + i)
            ups.append(
                message_tile(lambda row, place=place: up[place, row : row + 8, :], axis, b)
            )
            if down is not None:
                quads.append([means(axis, i, k) for k in range(4)])

        def choose(side, old, from_up, from_down):
            state = states[side]
            t = old if from_down is None else pick(state == 2, from_down, old)
            return pick(state == 1, from_up, t)

        def put(tile, old, t):
            if (axis, tile) in edges:
                t = jnp.where(edges[axis, tile], old, t)
            if axis == 2:
                t = lanes_from(t, face_order(lane))
            rows, lanes = tile_slices(axis, tile)
            halo[b, axis, rows, lanes] = t

        def present(tile):
            rows, lanes = tile_slices(axis, tile)
            return halo[b, axis, rows, lanes]

        if axis < 2:
            for side in range(2):
                if axis == 1:
                    wide = lanes_from(ups[side], group * 16 + side * 8 + within // 2)
                for a in range(2):
                    if axis == 0:
                        tile = side * 2 + a
                        from_up = lanes_from(
                            ups[side], (4 * a + group // 2) * 16 + side * 8 + within // 2
                        )
                    else:
                        tile = a * 2 + side
                        from_up = rows_from(wide, spread_rows[a])
                    from_down = None
                    if down is not None:
                        low_part, high_part = quads[side][2 * a], quads[side][2 * a + 1]
                        if side:
                            low_part = pltpu.roll(low_part, 120, 1)
                        else:
                            high_part = pltpu.roll(high_part, 8, 1)
                        from_down = jnp.where(second == 0, low_part, high_part)
                    old = present(tile)
                    put(tile, old, choose(side, old, from_up, from_down))
        else:
            both = jnp.where(second == 0, ups[0], ups[1])
            for half in range(2):
                wide = lanes_from(both, group * 16 + second * 8 + 4 * half + low // 2)
                for a in range(2):
                    tile = a * 2 + half
                    from_up = rows_from(wide, spread_rows[a])
                    old = present(tile)
                    parts = [
                        choose(side, old, from_up, quads[side][tile] if down is not None else None)
                        for side in range(2)
                    ]
                    put(tile, old, jnp.where(second == 0, parts[0], parts[1]))


def roll(x, shift, axis):
    shift %= x.shape[axis]
    return pltpu.roll(x, shift, axis) if shift else x


def ring(left, right, sign):
    lane = iotas(left.shape)[1]
    a, c = roll(left, 16 * sign, 1), roll(right, 16 * sign, 1)
    if sign > 0:
        return [jnp.where(lane < 16, c, a), jnp.where(lane < 16, a, c)]
    return [jnp.where(lane >= 112, c, a), jnp.where(lane >= 112, a, c)]


def drift(star, moved, b, advances):
    for q in range(1, 19):
        c = VELOCITIES[q]
        old = [star[b, q, :, 128 * half : 128 * half + 128] for half in range(2)]
        new = [roll(t, c[0], 0) for t in old]
        if c[1]:
            new = ring(new[0], new[1], c[1])
        for half in range(2):
            t = roll(new[half], c[2], 1)
            moved[b, q, :, 128 * half : 128 * half + 128] = pick(advances, t, old[half])
    moved[b, 0] = star[b, 0]


def finish(moved, halo, out, b, advances, final):
    row, lane = iotas((16, 128))
    row = pick(advances, row, jnp.full_like(row, -1))
    within = pick(advances, lane % 16, jnp.full_like(lane, 8))
    lane = pick(advances, lane, jnp.full_like(lane, 64))
    first, last = lane < 16, lane >= 112

    for q in range(19):
        c = VELOCITIES[q]
        new = [moved[b, q, :, 128 * half : 128 * half + 128] for half in range(2)]
        if c[0]:
            side, p = side_of(q, 0)
            place = side * 8 + p
            plane = [
                halo[b, 0, place : place + 1, 128 * half : 128 * half + 128] for half in range(2)
            ]
            if c[1]:
                plane = ring(plane[0], plane[1], c[1])
            for half in range(2):
                line = roll(plane[half], c[2], 1)
                new[half] = jnp.where(row == (0 if c[0] > 0 else 15), line, new[half])
        if c[1]:
            side, p = side_of(q, 1)
            border = halo[b, 1, :, 128 * side : 128 * side + 128]
            border = roll(border, (-16 * p if side == 0 else 112 - 16 * p) + c[2], 1)
            border = roll(border, c[0], 0)
            new[side] = jnp.where(last if side else first, border, new[side])
        if c[2]:
            side, p = side_of(q, 2)
            borders = []
            for half in range(2):
                border = halo[b, 2, :, 128 * half : 128 * half + 128]
                border = roll(border, -p if side == 0 else 7 - p, 1)
                borders.append(roll(border, c[0], 0))
            if c[1]:
                borders = ring(borders[0], borders[1], c[1])
            for half in range(2):
                new[half] = jnp.where(
                    within == (0 if c[2] > 0 else 15), borders[half], new[half]
                )
        for half in range(2):
            if final:
                for a in range(2):
                    out[q, woven(b, 2 * a + half), :] = new[half][8 * a : 8 * a + 8]
            elif q:
                out[b, q, :, 128 * half : 128 * half + 128] = new[half]


def kernel(
    pop_hbm,
    mask_hbm,
    level_hbm,
    nbr_hbm,
    link_hbm,
    out,
    pop,
    mask_ref,
    level,
    nbr,
    link,
    in_sems,
    star,
    middle,
    faces_a,
    faces_b,
    out_a,
    out_b,
    in_a,
    in_b,
    up_send_a,
    up_send_b,
    up_a,
    up_b,
    down_send,
    down,
    halo,
    table,
    wanted_own,
    wanted,
    wanted_side,
    mem_ss,
    mem_rs,
    side_ss,
    side_rs,
    meta_ss,
    meta_rs,
    up_a_ss,
    up_a_rs,
    up_b_ss,
    up_b_rs,
    down_ss,
    down_rs,
):
    s = lax.axis_index("section")
    m = lax.axis_index("member")
    loads = [
        pltpu.make_async_copy(src, dst, in_sems.at[i])
        for i, (src, dst) in enumerate(
            [
                (link_hbm, link),
                (level_hbm, level),
                (nbr_hbm, nbr),
                (pop_hbm, pop),
                (mask_hbm, mask_ref),
            ]
        )
    ]
    for load in loads:
        load.start()
    has = {-1: m > 0, 0: None, 1: m < NMEM - 1}
    one = jnp.int32(1)
    around = 1 + jnp.where(has[-1], one, 0) + jnp.where(has[1], one, 0)

    def if_member(dm, do):
        if has[dm] is None:
            do()
        else:
            pl.when(has[dm])(do)

    def each(low, high, do):
        def step(i, carry):
            do(i)
            return carry

        lax.fori_loop(low, high, step, 0)

    def blocks(do):
        for b in range(2):
            do(b)

    barrier = pltpu.get_barrier_semaphore()

    def greet(other):
        def signal(dm):
            pl.semaphore_signal(barrier, inc=1, device_id=(other, m + dm), device_id_type=MESH)

        pl.when(other != s)(lambda: signal(0))
        for dm in (-1, 1):
            if_member(dm, lambda dm=dm: signal(dm))

    each(0, NSEC, greet)

    def remote(src, dst, send_sem, recv_sem, other, dm):
        return pltpu.make_async_remote_copy(
            src_ref=src,
            dst_ref=dst,
            send_sem=send_sem,
            recv_sem=recv_sem,
            device_id=(other, m + dm),
            device_id_type=MESH,
        )

    def message(ref, place):
        return ref.at[place, pl.ds(0, 34)]

    def meta_copy(src, dst, other):
        return remote(src, dst, meta_ss, meta_rs, other, 0)

    def side_copy(dm, arriving):
        into = (1 + dm) // 2 if arriving else (1 - dm) // 2
        return remote(
            wanted, wanted_side.at[into], side_ss.at[(dm + 1) // 2], side_rs.at[into], s, dm
        )

    def mem_copy(sends, receives, step, dm, arriving):
        into = (1 + dm) // 2 if arriving else (1 - dm) // 2
        return remote(
            sends,
            receives.at[into],
            mem_ss.at[step, (dm + 1) // 2],
            mem_rs.at[step, into],
            s,
            dm,
        )

    def up_a_copy(src, dst, other):
        return remote(src, dst, up_a_ss, up_a_rs, other, 0)

    def up_b_copy(src, dst, other, dm):
        return remote(src, dst, up_b_ss, up_b_rs, other, dm)

    def down_copy(src, dst, other, dm):
        return remote(src, dst, down_ss, down_rs, other, dm)

    singles = tuple(range(1, NSEC))
    groups = tuple(sorted({k * e for k in range(1, NSEC - 1) for e in (2, 3)}))

    def wait_group(count, cases, ref, copy, receive):
        for n in cases:

            @pl.when(count == n)
            def _(n=n):
                whole = ref.at[pl.ds(0, n), pl.ds(0, 34)] if len(ref.shape) == 3 else ref.at[pl.ds(0, n)]
                both = copy(whole, whole)
                both.wait_recv() if receive else both.wait_send()

    below = s
    higher = NSEC - 1 - s
    below_direct = jnp.maximum(s - 1, 0)
    above = jnp.where(s == 0, NSEC, s + 1)
    higher_direct = NSEC - above

    for load in loads[:3]:
        load.wait()
    own = level[s]
    rate = jnp.where(
        own == 0, F32(1.0 / 0.55), jnp.where(own == 1, F32(1.0 / 0.6), F32(1.0 / 0.7))
    )
    blocks(lambda b: read_wanted(link, m, wanted_own, table, b))
    for load in loads[3:]:
        load.wait()

    def first_part(b):
        collide(pop, mask_ref, star, b, rate, own >= 1, True)
        export(star, faces_a, out_a, b)

    blocks(first_part)
    pl.semaphore_wait(barrier, NSEC * around - 1)

    def start_members(sends, receives, step):
        for dm in (-1, 1):
            if_member(dm, lambda dm=dm: mem_copy(sends, receives, step, dm, False).start())

    def receive_members(faces, receives, step):
        for dm in (-1, 1):
            if_member(dm, lambda dm=dm: mem_copy(out_a, receives, step, dm, True).wait_recv())
        for dm in (-1, 1):
            open_message(receives.at[(1 + dm) // 2], faces, 2 + 2 * dm)

    each(0, s, lambda other: meta_copy(wanted_own, wanted.at[s], other).start())
    start_members(out_a, in_a, 0)
    restrict(faces_a, down_send)

    def start_down(other):
        for dm in (-1, 0, 1):
            if_member(
                dm,
                lambda dm=dm: down_copy(
                    down_send.at[pl.ds(0, 34)], message(down, s * 3 + 1 - dm), other, dm
                ).start(),
            )

    each(1, s, start_down)
    blocks(lambda b: read_links(nbr, link, level, own, m, table, b))
    receive_members(faces_a, in_a, 0)
    wait_group(higher, singles, wanted, lambda x, y: meta_copy(x, y, s), True)

    def send_up(other):
        select_quadrants(faces_a, lambda i: wanted[other, i], up_send_a, other, False)
        up_a_copy(message(up_send_a, other), message(up_a, s), other).start()

    each(s + 1, NSEC, send_up)
    for dm in (-1, 1):
        if_member(dm, lambda dm=dm: side_copy(dm, False).start())
    def prepare_first(b):
        drift(star, middle, b, own >= 1)
        build_near(faces_a, halo, b, table)

    blocks(prepare_first)
    wait_group(below, singles, up_a, lambda x, y: up_a_copy(x, y, s), True)
    wait_group(
        jnp.where(s == 0, 0, higher) * around,
        groups,
        down,
        lambda x, y: down_copy(x, y, s, 0),
        True,
    )

    blocks(lambda b: build_links(up_a, down, halo, b, table, False))
    blocks(lambda b: finish(middle, halo, middle, b, own >= 1, False))
    blocks(lambda b: collide(middle, mask_ref, star, b, rate, own == 2, False))
    blocks(lambda b: export(star, faces_b, out_b, b))
    start_members(out_b, in_b, 1)
    for dm in (-1, 1):
        if_member(dm, lambda dm=dm: side_copy(dm, True).wait_recv())

    def send_direct(other):
        for dm in (-1, 0, 1):

            def ask(i, dm=dm):
                if dm == 0:
                    return wanted[other, i]
                return jnp.where(has[dm], wanted_side[(1 + dm) // 2, other, i], 0)

            select_quadrants(faces_b, ask, up_send_b, other * 3 + dm + 1, True)
        for dm in (-1, 0, 1):

            def send(dm=dm):
                up_b_copy(
                    message(up_send_b, other * 3 + dm + 1),
                    message(up_b, s * 3 + 1 - dm),
                    other,
                    dm,
                ).start()

            if_member(dm, send)

    each(above, NSEC, send_direct)
    blocks(lambda b: drift(star, middle, b, own == 2))
    wait_group(below, singles, wanted, lambda x, y: meta_copy(x, y, s), False)
    for dm in (-1, 1):
        if_member(dm, lambda dm=dm: mem_copy(out_a, in_a, 0, dm, False).wait_send())
        if_member(dm, lambda dm=dm: side_copy(dm, False).wait_send())
    wait_group(
        below_direct * around, groups, down, lambda x, y: down_copy(x, y, s, 0), False
    )
    wait_group(higher, singles, up_send_a, lambda x, y: up_a_copy(x, y, s), False)
    receive_members(faces_b, in_b, 1)
    blocks(lambda b: build_near(faces_b, halo, b, table))
    for dm in (-1, 1):
        if_member(dm, lambda dm=dm: mem_copy(out_b, in_b, 1, dm, False).wait_send())
    wait_group(
        higher_direct * around, groups, up_send_b, lambda x, y: up_b_copy(x, y, s, 0), False
    )
    wait_group(
        below_direct * around, groups, up_b, lambda x, y: up_b_copy(x, y, s, 0), True
    )

    blocks(lambda b: build_links(up_b, None, halo, b, table, True))
    blocks(lambda b: finish(middle, halo, out, b, own == 2, True))


def body(populations, fluid_mask, section_level, neighbours, interface):
    state = pltpu.VMEM((2, 19, 16, 256), F32)
    faces = pltpu.VMEM((72, 8, 128), F32)
    by_section = pltpu.VMEM((NSEC, 40, 128), F32)
    by_device = pltpu.VMEM((NSEC * 3, 40, 128), F32)
    members = pltpu.VMEM((2, 60, 128), F32)
    arrived = pltpu.VMEM((2, 2, 60, 128), F32)
    vmem = pl.BlockSpec(memory_space=pltpu.VMEM)
    hbm = pl.BlockSpec(memory_space=pltpu.HBM)
    dma = pltpu.SemaphoreType.DMA
    out = pl.pallas_call(
        kernel,
        out_shape=pltpu.VMEM((19, 64, 128), F32),
        in_specs=[hbm] * 5,
        out_specs=vmem,
        scratch_shapes=[
            pltpu.VMEM((19, 64, 128), F32),
            pltpu.VMEM((64, 128), jnp.int32),
            pltpu.SMEM((NSEC,), jnp.int32),
            pltpu.SMEM((2, 18), jnp.int32),
            pltpu.SMEM((2, 4, 6), jnp.int32),
            dma((5,)),
            state,
            state,
            faces,
            faces,
            members,
            members,
            arrived,
            arrived,
            by_section,
            by_device,
            by_section,
            by_device,
            pltpu.VMEM((40, 128), F32),
            by_device,
            pltpu.VMEM((2, 3, 16, 256), F32),
            pltpu.SMEM((2 * TABLE,), jnp.int32),
            pltpu.SMEM((128,), jnp.int32),
            pltpu.SMEM((NSEC, 128), jnp.int32),
            pltpu.SMEM((2, NSEC, 128), jnp.int32),
            dma((2, 2)),
            dma((2, 2)),
            dma((2,)),
            dma((2,)),
        ]
        + [dma] * 8,
        compiler_params=pltpu.CompilerParams(
            collective_id=0, has_side_effects=True, vmem_limit_bytes=54656 * 1024
        ),
        name="lattice_step",
    )(
        populations.reshape(2, 19, 32, 128).transpose(1, 2, 0, 3).reshape(19, 64, 128),
        fluid_mask.reshape(2, 32, 128).transpose(1, 0, 2).reshape(64, 128),
        section_level,
        neighbours,
        interface.transpose(0, 2, 1),
    )
    return out.reshape(19, 32, 2, 128).transpose(2, 0, 1, 3).reshape(2, 19, 4096)


def solution(mesh):
    return jax.shard_map(
        body,
        mesh=mesh,
        in_specs=(
            P(("section", "member"), None, None),
            P(("section", "member"), None),
            P(),
            P(("section", "member"), None),
            P(("section", "member"), None, None),
        ),
        out_specs=P(("section", "member"), None, None),
        check_vma=False,
    )
```

```python
import jax
import jax.numpy as jnp
from jax import lax
from jax.experimental import pallas as pl
from jax.experimental.pallas import tpu as pltpu
from jax.sharding import PartitionSpec as P

MESH = pl.DeviceIdType.MESH
F32 = jnp.float32
NSEC = 8
NMEM = 32

VELOCITIES = (
    (0, 0, 0),
    (1, 0, 0),
    (-1, 0, 0),
    (0, 1, 0),
    (0, -1, 0),
    (0, 0, 1),
    (0, 0, -1),
    (1, 1, 0),
    (-1, -1, 0),
    (1, -1, 0),
    (-1, 1, 0),
    (1, 0, 1),
    (-1, 0, -1),
    (1, 0, -1),
    (-1, 0, 1),
    (0, 1, 1),
    (0, -1, -1),
    (0, 1, -1),
    (0, -1, 1),
)
OPPOSITE = (0, 2, 1, 4, 3, 6, 5, 8, 7, 10, 9, 12, 11, 14, 13, 16, 15, 18, 17)
SIDE_LISTS = tuple(
    tuple(tuple(q for q in range(19) if VELOCITIES[q][axis] == sign) for sign in (1, -1))
    for axis in range(3)
)


def side_of(q, axis):
    side = 0 if VELOCITIES[q][axis] > 0 else 1
    return side, SIDE_LISTS[axis][side].index(q)


def iotas(shape=(8, 128)):
    return lax.broadcasted_iota(jnp.int32, shape, 0), lax.broadcasted_iota(jnp.int32, shape, 1)


def lanes_from(x, index):
    return jnp.take_along_axis(x, index, axis=1)


def rows_from(x, index):
    return jnp.take_along_axis(x, index, axis=0)


def pick(cond, a, b):
    return lax.select(cond, a, b)


def tile_slices(axis, tile):
    first, second = 8 * (tile // 2), 128 * (tile % 2)
    return slice(first, first + 8), slice(second, second + 128)


def packing(count):
    packed = -(-count * 5 // 8)
    spare = [(d, g) for d in range(packed) for g in (5, 6, 7)]
    runs = []
    for source in range(packed, count):
        for group in range(5):
            d, g = spare.pop(0)
            last = runs[-1] if runs else None
            if last and last[0] == source and last[2] == d and last[3] + last[4] == g:
                runs[-1] = last[:4] + (last[4] + 1,)
            else:
                runs.append((source, group, d, g, 1))
    return packed, runs


def lane_roll(x, shift):
    shift %= 128
    return pltpu.roll(x, shift, 1) if shift else x


def pack(tiles):
    lane = iotas()[1]
    packed, runs = packing(len(tiles))
    result = list(tiles[:packed])
    for source, group, d, g, length in runs:
        moved = lane_roll(tiles[source], 16 * (g - group))
        inside = (lane >= 16 * g) & (lane < 16 * (g + length))
        result[d] = jnp.where(inside, moved, result[d])
    return result


def unpack(load, source, count):
    lane = iotas()[1]
    packed, runs = packing(count)
    if source < packed:
        return load(source)
    result = None
    for which, group, d, g, length in runs:
        if which == source:
            moved = lane_roll(load(d), 16 * (group - g))
            result = moved if result is None else jnp.where(lane >= 16 * group, moved, result)
    return result


def store_message(tiles, put):
    for d, t in enumerate(pack([tiles[1], tiles[2], tiles[4], tiles[5]])):
        put(8 * d, t)
    for b in range(2):
        put(24 + 5 * b, tiles[3 * b][0:5])


def message_tile(load, axis, block):
    def tile(b):
        return load(24 + 5 * b) if axis == 0 else unpack(lambda d: load(8 * d), 2 * b + axis - 1, 4)

    return tile(block) if isinstance(block, int) else pick(block == 0, tile(0), tile(1))


def face_order(lane):
    return (lane % 8) * 16 + lane // 8 % 2 * 8 + lane // 16


def woven(b, tile):
    return pl.ds(32 * (tile // 2) + 2 * (tile % 2) + b, 8, stride=4)


def collide(cur, mask_ref, star, b, rate, advances, first):
    for tile in range(4):
        rows, lanes = tile_slices(0, tile)
        if first:
            f = [cur[q, woven(b, tile), :] for q in range(19)]
        else:
            f = [cur[b, q, rows, lanes] for q in range(19)]
        density = f[0]
        for q in range(1, 19):
            density = density + f[q]
        velocity = []
        for axis in range(3):
            plus, minus = SIDE_LISTS[axis]
            momentum = f[plus[0]] - f[minus[0]]
            for i in range(1, 5):
                momentum = momentum + f[plus[i]]
            for i in range(1, 5):
                momentum = momentum - f[minus[i]]
            velocity.append(momentum / density)
        base = 1.0 - 1.5 * (
            velocity[0] * velocity[0] + velocity[1] * velocity[1] + velocity[2] * velocity[2]
        )
        fluid = mask_ref[woven(b, tile), :] == 1
        keep = 1.0 - rate
        scaled = rate * density

        def put(q, relaxed):
            star[b, q, rows, lanes] = pick(
                advances, jnp.where(fluid, relaxed, f[OPPOSITE[q]]), f[q]
            )

        put(0, keep * f[0] + scaled * (1.0 / 3.0) * base)
        axis_weight = scaled * (1.0 / 18.0)
        edge_weight = scaled * (1.0 / 36.0)
        for q in range(1, 19, 2):
            c = VELOCITIES[q]
            along = None
            for axis in range(3):
                if c[axis]:
                    term = velocity[axis] if c[axis] > 0 else -velocity[axis]
                    along = term if along is None else along + term
            weight = axis_weight if q < 7 else edge_weight
            even = weight * (base + 4.5 * along * along)
            odd = weight * (3.0 * along)
            put(q, keep * f[q] + (even + odd))
            put(q + 1, keep * f[q + 1] + (even - odd))


def export(star, faces, message, b):
    row, lane = iotas()
    group, within = lane // 16, lane % 16
    for side in range(2):
        for p, q in enumerate(SIDE_LISTS[0][side]):
            layer = 15 if side == 0 else 0
            for half in range(2):
                line = star[b, q, layer : layer + 1, 128 * half : 128 * half + 128]
                place = side * 2 + half
                faces[(2 + b) * 12 + place, p : p + 1, :] = line
                message[b, 40 + 5 * place + p : 41 + 5 * place + p, :] = line
    zero = jnp.zeros((8, 128), F32)
    tiles = [None] * 8
    order = face_order(lane)
    for a in range(2):
        for side in range(2):
            total = zero
            for p, q in enumerate(SIDE_LISTS[1][side]):
                half = 1 - side
                x = star[b, q, 8 * a : 8 * a + 8, 128 * half : 128 * half + 128]
                shift = (16 * p + 16 if side == 0 else 16 * p) % 128
                x = pltpu.roll(x, shift, 1) if shift else x
                total = jnp.where(group == p, x, total)
            tiles[a * 2 + side] = total
        for half in range(2):
            total = zero
            for side in range(2):
                for p, q in enumerate(SIDE_LISTS[2][side]):
                    x = star[b, q, 8 * a : 8 * a + 8, 128 * half : 128 * half + 128]
                    shift = 113 + p if side == 0 else 8 + p
                    x = pltpu.roll(x, shift, 1)
                    total = jnp.where(within == side * 8 + p, x, total)
            tiles[4 + a * 2 + half] = lanes_from(total, order)
    for i, t in enumerate(tiles):
        faces[(2 + b) * 12 + 4 + i] = t
    for d, t in enumerate(pack(tiles)):
        message[b, 8 * d : 8 * d + 8, :] = t


def open_message(message, faces, place):
    for b in range(2):
        for i in range(8):
            faces[(place + b) * 12 + 4 + i] = unpack(
                lambda d: message[b, 8 * d : 8 * d + 8, :], i, 8
            )
        for tile in range(4):
            faces[(place + b) * 12 + tile, 0:5, :] = message[b, 40 + 5 * tile : 45 + 5 * tile, :]


def restrict(faces, down):
    tiles = [t for b in range(2) for t in restrict_block(faces, b)]

    def put(row, t):
        down[row : row + t.shape[0], :] = t

    store_message(tiles, put)


def restrict_block(faces, b):
    row, lane = iotas()
    group, within, low = lane // 16, lane % 16, lane % 8
    second = (lane // 8) % 2
    fine = group * 16 + 2 * low
    coarse = (2 * (group % 4)) * 16
    pair_rows = 2 * (row % 4)
    parts = []
    for side in range(2):
        halves = []
        for half in range(2):
            t = faces[(2 + b) * 12 + side * 2 + half]
            t = t + pltpu.roll(t, 127, 1)
            t = t + pltpu.roll(t, 112, 1)
            halves.append(lanes_from(t, coarse + 2 * low))
        parts.append(jnp.where(group < 4, halves[0], halves[1]))
    tiles = [0.25 * jnp.where(second == 0, parts[0], parts[1])]
    parts = []
    for side in range(2):
        rows = []
        for a in range(2):
            t = faces[(2 + b) * 12 + 4 + a * 2 + side]
            t = t + pltpu.roll(t, 127, 1)
            t = t + pltpu.roll(t, 7, 0)
            rows.append(rows_from(lanes_from(t, fine), pair_rows))
        parts.append(jnp.where(row < 4, rows[0], rows[1]))
    tiles.append(0.25 * jnp.where(second == 0, parts[0], parts[1]))
    rows = []
    for a in range(2):
        halves = []
        for half in range(2):
            t = faces[(2 + b) * 12 + 8 + a * 2 + half]
            t = t + pltpu.roll(t, 127, 1)
            halves.append(lanes_from(t, group * 16 + second * 8 + 2 * (low % 4)))
        t = jnp.where(low < 4, halves[0], halves[1])
        t = t + pltpu.roll(t, 7, 0)
        rows.append(rows_from(t, pair_rows))
    tiles.append(0.25 * jnp.where(row < 4, rows[0], rows[1]))
    return tiles


def member_offset(block, member):
    return jnp.clip(((block >> 1) & (NMEM - 1)) - member + 1, 0, 2)


def slot_of(block, member):
    return member_offset(block, member) * 2 + (block & 1)


NEAR, STATE, UP_SAME, UP_DIRECT, DOWN, DOWN_BLOCK, EDGE, EDGE_THERE, TABLE = (
    0,
    6,
    12,
    18,
    24,
    48,
    72,
    84,
    96,
)


SECTION_SHIFT = NMEM.bit_length()


def read_wanted(link, member, wanted, table, b):
    for axis in range(3):
        for side in range(2):
            i, j = axis * 2 + side, axis * 2 + 1 - side
            code = jnp.int32(-1)
            for k in range(4):
                block = link[b, k, j]
                code = jnp.maximum(code, jnp.where(block >= 0, block * 4 + k, -1))
            table[b * TABLE + STATE + i] = code
            safe = jnp.maximum(code, 0)
            k, block = safe & 3, safe >> 2
            first, last = k >> 1, k & 1
            if axis == 0:
                tile = side * 2 + first
            elif axis == 1:
                tile = 4 + first * 2 + side
            else:
                tile = 8 + k
            wanted[b * 6 + i] = slot_of(block, member) * 12 + tile
            wanted[12 + b * 6 + i] = (2 + (block & 1)) * 12 + tile
            wanted[24 + b * 6 + i] = last


def read_links(nbr, link, level, own, member, table, b):
    for axis in range(3):
        for side in range(2):
            i, j = axis * 2 + side, axis * 2 + 1 - side
            for k in range(4):
                block = link[b, k, j]
                safe = jnp.maximum(block, 0)
                place = (safe >> SECTION_SHIFT) * 3 + member_offset(safe, member)
                table[b * TABLE + DOWN + i * 4 + k] = place
                table[b * TABLE + DOWN_BLOCK + i * 4 + k] = jnp.where(block >= 0, safe & 1, -1)
            code = table[b * TABLE + STATE + i]
            block = jnp.maximum(code, 0) >> 2
            section = block >> SECTION_SHIFT
            near = nbr[b, j]
            table[b * TABLE + NEAR + i] = slot_of(jnp.maximum(near, 0), member) * 12
            linked = jnp.where(code < 0, 3, jnp.where(level[section] < own, 1, 2))
            table[b * TABLE + STATE + i] = jnp.where(near >= 0, 0, linked)
            table[b * TABLE + UP_SAME + i] = section
            table[b * TABLE + UP_DIRECT + i] = section * 3 + member_offset(block, member)
    for q in range(7, 19):
        block = nbr[b, OPPOSITE[q] - 1]
        table[b * TABLE + EDGE + q - 7] = slot_of(jnp.maximum(block, 0), member) * 12
        table[b * TABLE + EDGE_THERE + q - 7] = block


def select_quadrants(faces, ask, out, place, direct):
    lane = iotas()[1]
    second = (lane // 8) % 2
    tiles = []
    for b in range(2):
        for axis in range(3):
            parts = []
            for side in range(2):
                i = b * 6 + axis * 2 + side
                t = faces[ask((12 if direct else 0) + i)]
                if axis < 2:
                    t = pick(ask(24 + i) == side, t, pltpu.roll(t, 8 if side else 120, 1))
                parts.append(t)
            tiles.append(jnp.where(second == 0, parts[0], parts[1]))

    def put(row, t):
        out[place, row : row + t.shape[0], :] = t

    store_message(tiles, put)


def edge_place(q):
    row, lane = iotas()
    group, second = lane // 16, (lane // 8) % 2
    c = VELOCITIES[q]
    one, two = [axis for axis in range(3) if c[axis]]
    side, p = side_of(q, two)
    end, line = (1, 7) if c[one] > 0 else (0, 0)
    if two == 1:
        return two, [(end * 2 + side, (row == line) & (group == p))]
    if one == 0:
        cells = (row == line) & (group == p) & (second == side)
        return two, [(end * 2 + half, cells) for half in range(2)]
    return two, [(a * 2 + end, lane == p * 16 + side * 8 + line) for a in range(2)]


def build_near(faces, halo, b, table):
    row, lane = iotas()
    group, second = lane // 16, (lane // 8) % 2

    def entry(place):
        return table[b * TABLE + place]

    for axis in range(3):
        rest = jnp.where((row if axis == 0 else group) == 0, F32(1.0 / 18.0), F32(1.0 / 36.0))
        for tile in range(4):
            sides = [tile // 2] if axis == 0 else [tile % 2] if axis == 1 else [0, 1]
            parts = []
            for side in sides:
                i = axis * 2 + side
                t = faces[entry(NEAR + i) + axis * 4 + tile]
                parts.append(pick(entry(STATE + i) == 0, t, rest))
            t = parts[0] if axis < 2 else jnp.where(second == 0, parts[0], parts[1])
            rows, lanes = tile_slices(axis, tile)
            halo[b, axis, rows, lanes] = t
    for q in range(7, 19):
        two, places = edge_place(q)
        near, there = entry(EDGE + q - 7) + two * 4, entry(EDGE_THERE + q - 7) >= 0
        for tile, cells in places:
            rows, lanes = tile_slices(two, tile)
            line = faces[near + tile]
            line = pick(there, line, jnp.full_like(line, 1.0 / 36.0))
            halo[b, two, rows, lanes] = jnp.where(cells, line, halo[b, two, rows, lanes])


def build_links(up, down, halo, b, table, direct):
    row, lane = iotas()
    group, within, low = lane // 16, lane % 16, lane % 8
    second = (lane // 8) % 2
    spread_rows = [4 * a + row // 2 for a in range(2)]
    edges = {}
    for q in range(7, 19):
        two, places = edge_place(q)
        for tile, cells in places:
            edges[two, tile] = edges[two, tile] | cells if (two, tile) in edges else cells

    def entry(place):
        return table[b * TABLE + place]

    def means(axis, i, k):
        place, block = entry(DOWN + i * 4 + k), entry(DOWN_BLOCK + i * 4 + k)
        t = message_tile(lambda row: down[place, row : row + 8, :], axis, block)
        return pick(block >= 0, t, jnp.zeros_like(t))

    for axis in range(3):
        states, quads, ups = [], [], []
        for side in range(2):
            i = axis * 2 + side
            states.append(entry(STATE + i))
            place = entry((UP_DIRECT if direct else UP_SAME) + i)
            ups.append(
                message_tile(lambda row, place=place: up[place, row : row + 8, :], axis, b)
            )
            if down is not None:
                quads.append([means(axis, i, k) for k in range(4)])

        def choose(side, old, from_up, from_down):
            state = states[side]
            t = old if from_down is None else pick(state == 2, from_down, old)
            return pick(state == 1, from_up, t)

        def put(tile, old, t):
            if (axis, tile) in edges:
                t = jnp.where(edges[axis, tile], old, t)
            if axis == 2:
                t = lanes_from(t, face_order(lane))
            rows, lanes = tile_slices(axis, tile)
            halo[b, axis, rows, lanes] = t

        def present(tile):
            rows, lanes = tile_slices(axis, tile)
            return halo[b, axis, rows, lanes]

        if axis < 2:
            for side in range(2):
                if axis == 1:
                    wide = lanes_from(ups[side], group * 16 + side * 8 + within // 2)
                for a in range(2):
                    if axis == 0:
                        tile = side * 2 + a
                        from_up = lanes_from(
                            ups[side], (4 * a + group // 2) * 16 + side * 8 + within // 2
                        )
                    else:
                        tile = a * 2 + side
                        from_up = rows_from(wide, spread_rows[a])
                    from_down = None
                    if down is not None:
                        low_part, high_part = quads[side][2 * a], quads[side][2 * a + 1]
                        if side:
                            low_part = pltpu.roll(low_part, 120, 1)
                        else:
                            high_part = pltpu.roll(high_part, 8, 1)
                        from_down = jnp.where(second == 0, low_part, high_part)
                    old = present(tile)
                    put(tile, old, choose(side, old, from_up, from_down))
        else:
            both = jnp.where(second == 0, ups[0], ups[1])
            for half in range(2):
                wide = lanes_from(both, group * 16 + second * 8 + 4 * half + low // 2)
                for a in range(2):
                    tile = a * 2 + half
                    from_up = rows_from(wide, spread_rows[a])
                    old = present(tile)
                    parts = [
                        choose(side, old, from_up, quads[side][tile] if down is not None else None)
                        for side in range(2)
                    ]
                    put(tile, old, jnp.where(second == 0, parts[0], parts[1]))


def roll(x, shift, axis):
    shift %= x.shape[axis]
    return pltpu.roll(x, shift, axis) if shift else x


def ring(left, right, sign):
    lane = iotas(left.shape)[1]
    a, c = roll(left, 16 * sign, 1), roll(right, 16 * sign, 1)
    if sign > 0:
        return [jnp.where(lane < 16, c, a), jnp.where(lane < 16, a, c)]
    return [jnp.where(lane >= 112, c, a), jnp.where(lane >= 112, a, c)]


def drift(star, moved, b, advances):
    for q in range(1, 19):
        c = VELOCITIES[q]
        old = [star[b, q, :, 128 * half : 128 * half + 128] for half in range(2)]
        new = [roll(t, c[0], 0) for t in old]
        if c[1]:
            new = ring(new[0], new[1], c[1])
        for half in range(2):
            t = roll(new[half], c[2], 1)
            moved[b, q, :, 128 * half : 128 * half + 128] = pick(advances, t, old[half])
    moved[b, 0] = star[b, 0]


def finish(moved, halo, out, b, advances, final):
    row, lane = iotas((16, 128))
    row = pick(advances, row, jnp.full_like(row, -1))
    within = pick(advances, lane % 16, jnp.full_like(lane, 8))
    lane = pick(advances, lane, jnp.full_like(lane, 64))
    first, last = lane < 16, lane >= 112

    for q in range(19):
        c = VELOCITIES[q]
        new = [moved[b, q, :, 128 * half : 128 * half + 128] for half in range(2)]
        if c[0]:
            side, p = side_of(q, 0)
            place = side * 8 + p
            plane = [
                halo[b, 0, place : place + 1, 128 * half : 128 * half + 128] for half in range(2)
            ]
            if c[1]:
                plane = ring(plane[0], plane[1], c[1])
            for half in range(2):
                line = roll(plane[half], c[2], 1)
                new[half] = jnp.where(row == (0 if c[0] > 0 else 15), line, new[half])
        if c[1]:
            side, p = side_of(q, 1)
            border = halo[b, 1, :, 128 * side : 128 * side + 128]
            border = roll(border, (-16 * p if side == 0 else 112 - 16 * p) + c[2], 1)
            border = roll(border, c[0], 0)
            new[side] = jnp.where(last if side else first, border, new[side])
        if c[2]:
            side, p = side_of(q, 2)
            borders = []
            for half in range(2):
                border = halo[b, 2, :, 128 * half : 128 * half + 128]
                border = roll(border, -p if side == 0 else 7 - p, 1)
                borders.append(roll(border, c[0], 0))
            if c[1]:
                borders = ring(borders[0], borders[1], c[1])
            for half in range(2):
                new[half] = jnp.where(
                    within == (0 if c[2] > 0 else 15), borders[half], new[half]
                )
        for half in range(2):
            if final:
                for a in range(2):
                    out[q, woven(b, 2 * a + half), :] = new[half][8 * a : 8 * a + 8]
            elif q:
                out[b, q, :, 128 * half : 128 * half + 128] = new[half]


def kernel(
    pop_hbm,
    mask_hbm,
    level_hbm,
    nbr_hbm,
    link_hbm,
    out,
    pop,
    mask_ref,
    level,
    nbr,
    link,
    in_sems,
    star,
    middle,
    faces_a,
    faces_b,
    out_a,
    out_b,
    in_a,
    in_b,
    up_send_a,
    up_send_b,
    up_a,
    up_b,
    down_send,
    down,
    halo,
    table,
    wanted_own,
    wanted,
    wanted_side,
    mem_ss,
    mem_rs,
    side_ss,
    side_rs,
    meta_ss,
    meta_rs,
    up_a_ss,
    up_a_rs,
    up_b_ss,
    up_b_rs,
    down_ss,
    down_rs,
):
    s = lax.axis_index("section")
    m = lax.axis_index("member")
    loads = [
        pltpu.make_async_copy(src, dst, in_sems.at[i])
        for i, (src, dst) in enumerate(
            [
                (link_hbm, link),
                (level_hbm, level),
                (nbr_hbm, nbr),
                (pop_hbm, pop),
                (mask_hbm, mask_ref),
            ]
        )
    ]
    for load in loads:
        load.start()
    has = {-1: m > 0, 0: None, 1: m < NMEM - 1}
    one = jnp.int32(1)
    around = 1 + jnp.where(has[-1], one, 0) + jnp.where(has[1], one, 0)

    def if_member(dm, do):
        if has[dm] is None:
            do()
        else:
            pl.when(has[dm])(do)

    def each(low, high, do):
        def step(i, carry):
            do(i)
            return carry

        lax.fori_loop(low, high, step, 0)

    def blocks(do):
        for b in range(2):
            do(b)

    barrier = pltpu.get_barrier_semaphore()

    def greet(other):
        def signal(dm):
            pl.semaphore_signal(barrier, inc=1, device_id=(other, m + dm), device_id_type=MESH)

        pl.when(other != s)(lambda: signal(0))
        for dm in (-1, 1):
            if_member(dm, lambda dm=dm: signal(dm))

    each(0, NSEC, greet)

    def remote(src, dst, send_sem, recv_sem, other, dm):
        return pltpu.make_async_remote_copy(
            src_ref=src,
            dst_ref=dst,
            send_sem=send_sem,
            recv_sem=recv_sem,
            device_id=(other, m + dm),
            device_id_type=MESH,
        )

    def message(ref, place):
        return ref.at[place, pl.ds(0, 34)]

    def meta_copy(src, dst, other):
        return remote(src, dst, meta_ss, meta_rs, other, 0)

    def side_copy(dm, arriving):
        into = (1 + dm) // 2 if arriving else (1 - dm) // 2
        return remote(
            wanted, wanted_side.at[into], side_ss.at[(dm + 1) // 2], side_rs.at[into], s, dm
        )

    def mem_copy(sends, receives, step, dm, arriving):
        into = (1 + dm) // 2 if arriving else (1 - dm) // 2
        return remote(
            sends,
            receives.at[into],
            mem_ss.at[step, (dm + 1) // 2],
            mem_rs.at[step, into],
            s,
            dm,
        )

    def up_a_copy(src, dst, other):
        return remote(src, dst, up_a_ss, up_a_rs, other, 0)

    def up_b_copy(src, dst, other, dm):
        return remote(src, dst, up_b_ss, up_b_rs, other, dm)

    def down_copy(src, dst, other, dm):
        return remote(src, dst, down_ss, down_rs, other, dm)

    singles = tuple(range(1, NSEC))
    groups = tuple(sorted({k * e for k in range(1, NSEC - 1) for e in (2, 3)}))

    def wait_group(count, cases, ref, copy, receive):
        for n in cases:

            @pl.when(count == n)
            def _(n=n):
                whole = ref.at[pl.ds(0, n), pl.ds(0, 34)] if len(ref.shape) == 3 else ref.at[pl.ds(0, n)]
                both = copy(whole, whole)
                both.wait_recv() if receive else both.wait_send()

    below = s
    higher = NSEC - 1 - s
    below_direct = jnp.maximum(s - 1, 0)
    above = jnp.where(s == 0, NSEC, s + 1)
    higher_direct = NSEC - above

    for load in loads[:3]:
        load.wait()
    own = level[s]
    rate = jnp.where(
        own == 0, F32(1.0 / 0.55), jnp.where(own == 1, F32(1.0 / 0.6), F32(1.0 / 0.7))
    )
    blocks(lambda b: read_wanted(link, m, wanted_own, table, b))
    for load in loads[3:]:
        load.wait()

    def first_part(b):
        collide(pop, mask_ref, star, b, rate, own >= 1, True)
        export(star, faces_a, out_a, b)

    blocks(first_part)
    pl.semaphore_wait(barrier, NSEC * around - 1)

    def start_members(sends, receives, step):
        for dm in (-1, 1):
            if_member(dm, lambda dm=dm: mem_copy(sends, receives, step, dm, False).start())

    def receive_members(faces, receives, step):
        for dm in (-1, 1):
            if_member(dm, lambda dm=dm: mem_copy(out_a, receives, step, dm, True).wait_recv())
        for dm in (-1, 1):
            open_message(receives.at[(1 + dm) // 2], faces, 2 + 2 * dm)

    each(0, s, lambda other: meta_copy(wanted_own, wanted.at[s], other).start())
    start_members(out_a, in_a, 0)
    restrict(faces_a, down_send)

    def start_down(other):
        for dm in (-1, 0, 1):
            if_member(
                dm,
                lambda dm=dm: down_copy(
                    down_send.at[pl.ds(0, 34)], message(down, s * 3 + 1 - dm), other, dm
                ).start(),
            )

    each(1, s, start_down)
    blocks(lambda b: read_links(nbr, link, level, own, m, table, b))
    receive_members(faces_a, in_a, 0)
    wait_group(higher, singles, wanted, lambda x, y: meta_copy(x, y, s), True)

    def send_up(pair):
        other = s + 1 + 2 * pair
        later = jnp.minimum(other + 1, NSEC - 1)
        select_quadrants(faces_a, lambda i: wanted[other, i], up_send_a, other, False)
        select_quadrants(faces_a, lambda i: wanted[later, i], up_send_a, other + 1, False)
        up_a_copy(message(up_send_a, other), message(up_a, s), other).start()

        @pl.when(other + 1 < NSEC)
        def _():
            up_a_copy(message(up_send_a, other + 1), message(up_a, s), other + 1).start()

    each(0, (NSEC - s) // 2, send_up)
    for dm in (-1, 1):
        if_member(dm, lambda dm=dm: side_copy(dm, False).start())
    def prepare_first(b):
        drift(star, middle, b, own >= 1)
        build_near(faces_a, halo, b, table)

    blocks(prepare_first)
    wait_group(below, singles, up_a, lambda x, y: up_a_copy(x, y, s), True)
    wait_group(
        jnp.where(s == 0, 0, higher) * around,
        groups,
        down,
        lambda x, y: down_copy(x, y, s, 0),
        True,
    )

    blocks(lambda b: build_links(up_a, down, halo, b, table, False))
    blocks(lambda b: finish(middle, halo, middle, b, own >= 1, False))
    blocks(lambda b: collide(middle, mask_ref, star, b, rate, own == 2, False))
    blocks(lambda b: export(star, faces_b, out_b, b))
    start_members(out_b, in_b, 1)
    for dm in (-1, 1):
        if_member(dm, lambda dm=dm: side_copy(dm, True).wait_recv())

    def send_direct(other):
        for dm in (-1, 0, 1):

            def ask(i, dm=dm):
                if dm == 0:
                    return wanted[other, i]
                return jnp.where(has[dm], wanted_side[(1 + dm) // 2, other, i], 0)

            select_quadrants(faces_b, ask, up_send_b, other * 3 + dm + 1, True)
        for dm in (-1, 0, 1):

            def send(dm=dm):
                up_b_copy(
                    message(up_send_b, other * 3 + dm + 1),
                    message(up_b, s * 3 + 1 - dm),
                    other,
                    dm,
                ).start()

            if_member(dm, send)

    each(above, NSEC, send_direct)
    blocks(lambda b: drift(star, middle, b, own == 2))
    wait_group(below, singles, wanted, lambda x, y: meta_copy(x, y, s), False)
    for dm in (-1, 1):
        if_member(dm, lambda dm=dm: mem_copy(out_a, in_a, 0, dm, False).wait_send())
        if_member(dm, lambda dm=dm: side_copy(dm, False).wait_send())
    wait_group(
        below_direct * around, groups, down, lambda x, y: down_copy(x, y, s, 0), False
    )
    wait_group(higher, singles, up_send_a, lambda x, y: up_a_copy(x, y, s), False)
    receive_members(faces_b, in_b, 1)
    blocks(lambda b: build_near(faces_b, halo, b, table))
    for dm in (-1, 1):
        if_member(dm, lambda dm=dm: mem_copy(out_b, in_b, 1, dm, False).wait_send())
    wait_group(
        higher_direct * around, groups, up_send_b, lambda x, y: up_b_copy(x, y, s, 0), False
    )
    wait_group(
        below_direct * around, groups, up_b, lambda x, y: up_b_copy(x, y, s, 0), True
    )

    blocks(lambda b: build_links(up_b, None, halo, b, table, True))
    blocks(lambda b: finish(middle, halo, out, b, own == 2, True))


def body(populations, fluid_mask, section_level, neighbours, interface):
    state = pltpu.VMEM((2, 19, 16, 256), F32)
    faces = pltpu.VMEM((72, 8, 128), F32)
    by_section = pltpu.VMEM((NSEC, 40, 128), F32)
    by_device = pltpu.VMEM((NSEC * 3, 40, 128), F32)
    members = pltpu.VMEM((2, 60, 128), F32)
    arrived = pltpu.VMEM((2, 2, 60, 128), F32)
    vmem = pl.BlockSpec(memory_space=pltpu.VMEM)
    hbm = pl.BlockSpec(memory_space=pltpu.HBM)
    dma = pltpu.SemaphoreType.DMA
    out = pl.pallas_call(
        kernel,
        out_shape=pltpu.VMEM((19, 64, 128), F32),
        in_specs=[hbm] * 5,
        out_specs=vmem,
        scratch_shapes=[
            pltpu.VMEM((19, 64, 128), F32),
            pltpu.VMEM((64, 128), jnp.int32),
            pltpu.SMEM((NSEC,), jnp.int32),
            pltpu.SMEM((2, 18), jnp.int32),
            pltpu.SMEM((2, 4, 6), jnp.int32),
            dma((5,)),
            state,
            state,
            faces,
            faces,
            members,
            members,
            arrived,
            arrived,
            pltpu.VMEM((NSEC + 1, 40, 128), F32),
            by_device,
            by_section,
            by_device,
            pltpu.VMEM((40, 128), F32),
            by_device,
            pltpu.VMEM((2, 3, 16, 256), F32),
            pltpu.SMEM((2 * TABLE,), jnp.int32),
            pltpu.SMEM((128,), jnp.int32),
            pltpu.SMEM((NSEC, 128), jnp.int32),
            pltpu.SMEM((2, NSEC, 128), jnp.int32),
            dma((2, 2)),
            dma((2, 2)),
            dma((2,)),
            dma((2,)),
        ]
        + [dma] * 8,
        compiler_params=pltpu.CompilerParams(
            collective_id=0, has_side_effects=True, vmem_limit_bytes=54656 * 1024
        ),
        name="lattice_step",
    )(
        populations.reshape(2, 19, 32, 128).transpose(1, 2, 0, 3).reshape(19, 64, 128),
        fluid_mask.reshape(2, 32, 128).transpose(1, 0, 2).reshape(64, 128),
        section_level,
        neighbours,
        interface.transpose(0, 2, 1),
    )
    return out.reshape(19, 32, 2, 128).transpose(2, 0, 1, 3).reshape(2, 19, 4096)


def solution(mesh):
    return jax.shard_map(
        body,
        mesh=mesh,
        in_specs=(
            P(("section", "member"), None, None),
            P(("section", "member"), None),
            P(),
            P(("section", "member"), None),
            P(("section", "member"), None, None),
        ),
        out_specs=P(("section", "member"), None, None),
        check_vma=False,
    )
```
